128 devices in a mesh: sec: 4 (over y_hi, core), tile: 32 (over z, x, y_lo).
Axes of the slice: x: 4, y: 4 (y_hi: 2, y_lo: 2; y = y_hi * 2 + y_lo), z: 4, core: 2. Of those that a mesh axis runs over, the one named last changes fastest.
Arguments:
- fields: float32 [4, 4, 2048, 256], P('sec', None, 'tile'), may hold values from -6 to 6
- coefficients: float32 [4, 2, 2048, 256], P('sec', None, 'tile'), may hold values from 0.04 to 0.24
- owner_tile: int32 [6144, 2], replicated, may hold values from 0 to 31, all different within a row; in each aligned block of 64 rows (0 to 63, 64 to 127, ...) at most 8 rows name the same one
- dest_block: int32 [6144, 2], replicated, may hold values from 0 to 63
- table_index: int32 [6144, 2], replicated, may hold values from 0 to 3
- tables: float32 [4, 256, 256], replicated, may hold values from -0.375 to 0.375
- land_mask: int32 [2048, 256], P('tile'), may hold values 0 or 1
Outputs:
- fields_out: float32 [4, 4, 2048, 256], P('sec', None, 'tile')
- surface: float32 [4, 2048, 256], P('sec', 'tile')
The draws below stay inside these ranges and needn't reach their ends.
Inputs may be any that keep to these rules, and one draw needn't show every extreme that they name: `owner_tile`: each row names 2 different ocean tiles; in each aligned block of 64 rows (the blocks of one atmosphere device) no tile is named more than 8 times.
All inputs are finite; a program needn't handle non-finite values. No bound on the sum of `land_mask` on one device may be relied on, other than what follows from the above.
Results may differ from the reference program's by a relative error of at most 0.0001.
Values sent between devices are 32-bit elements; how exact they have to be, the bound alone decides.
A program may use at most 64 MiB of HBM per device.

```python
import math
import jax
import jax.numpy as jnp
import numpy as np
from jax import lax

LEV = 4
BY = 64
BX = 256
STENCIL_SUBSTEPS = 2
R = 2
NTAB = 4
NY = 2048
ATM_BLOCKS = 6144
CAP = 8
N_SEC = 4
N_TILE = 32


def with_ends(values, key, least, largest):
    dims = values.shape
    place = [jax.random.randint(jax.random.fold_in(key, axis), (), 0, dims[axis]) for axis in range(len(dims))]
    values = values.at[tuple(place)].set(least)
    longest = dims.index(max(dims))
    place[longest] = (place[longest] + 1) % dims[longest]
    return values.at[tuple(place)].set(largest)


def level_of(rng, shape, split, least, top_value):
    def one(position, blocks):
        steps = jax.random.uniform(jax.random.fold_in(jax.random.fold_in(rng, 6), position), (blocks,), jnp.float32, least / len(split), top_value / len(split))
        return jnp.repeat(jnp.exp(steps), shape[position] // blocks).reshape((-1,) + (1,) * (len(shape) - position - 1))

    factor_of = one(*split[0])
    for cut in split[1:]:
        factor_of = factor_of * one(*cut)
    return factor_of


def assign_block(key, own, number, rows, count, top, most, skew):
    ranking = jax.random.permutation(key, count)
    packed, common = shares(count, rows * top, most, skew, True), shares(count, rows * top, most, skew, False)
    places = jnp.arange(count)

    def named(sizes, turn):
        used = int((sizes > 0).sum())
        fixed = max(1, used // 4)
        passed = fixed + (places - fixed + turn * (used - fixed)) % max(1, count - fixed)
        return jnp.zeros((count,), jnp.int32).at[ranking[jnp.where(places < fixed, places, passed)]].set(jnp.asarray(sizes, jnp.int32))

    sizes = jnp.where(number % 4 == 0, named(packed, number // 4), named(common, number - number // 4 - 1))
    mixed = jax.random.permutation(jax.random.fold_in(own, 3), count)
    source_of, taker = mixed[0:count // 2 * 2:2], mixed[1:count // 2 * 2:2]
    slack = jnp.minimum(sizes[source_of] - 1, most - sizes[taker]) // 2
    slack = jnp.where((source_of == ranking[0]) | (taker == ranking[0]) | (sizes[taker] == 0), 0, jnp.maximum(slack, 0))
    passed = jax.random.randint(jax.random.fold_in(own, 4), (count // 2,), 0, 1 << 20) % (slack + 1)
    sizes = sizes.at[source_of].add(-passed).at[taker].add(passed)
    members = jnp.searchsorted(jnp.cumsum(sizes), jnp.arange(rows * top), side="right").astype(jnp.int32)
    table = members.reshape(top, rows).T
    table = table[jax.random.permutation(jax.random.fold_in(own, 1), rows)]
    turn = jax.random.randint(jax.random.fold_in(own, 2), (rows, 1), 0, top)
    return jnp.take_along_axis(table, (jnp.arange(top)[None, :] + turn) % top, axis=1)


def shares(count, total, limit, lean, full):
    weights = [(1 << 20) // math.isqrt(grade ** lean) + 1 for grade in range(1, count + 1)]
    largest = limit if full else min(limit, max(-(-total // count), total * weights[0] // sum(weights)))
    least = 1 if total - largest >= count - 1 else 0
    holding, rest = [largest] + [least] * (count - 1), total - largest - least * (count - 1)
    while rest > 0:
        candidates = [i for i in range(1, count) if holding[i] < largest] or [i for i in range(1, count) if holding[i] < limit]
        mass, budget = sum([weights[i] for i in candidates]), rest
        for i in candidates:
            addition = min(limit - holding[i], max(1, budget * weights[i] // mass), rest)
            holding[i] = holding[i] + addition
            rest = rest - addition
    return np.array(holding)


def scatter_about(rng, dims, width, most, pieces=(), kind=jnp.bfloat16):
    values = jax.random.normal(rng, dims, jnp.float32) * width
    if len(pieces) > 0:
        values = level_of(rng, dims, pieces, -0.22, 0.18) * values
    return jnp.clip(values, min=-most, max=most).astype(kind)


def setup_inputs(seed: int = 0) -> dict:
    key_of = jax.random.split(jax.random.key(seed), 8)
    fields = scatter_about(key_of[0], (N_SEC, LEV, NY, BX), 1.0, 6.0, ((0, 4), (2, 32)), jnp.float32)
    coefficients = jnp.clip(0.04 + 0.19999999552965164 * jax.random.uniform(key_of[1], (N_SEC, 2, NY, BX), jnp.float32) ** level_of(key_of[1], (N_SEC, 2, NY, BX), ((0, 4), (2, 32)), -0.2, 0.2), 0.04, 0.24)
    owner_tile_keys = jax.random.split(jax.random.fold_in(key_of[2], 1), ATM_BLOCKS // BY)
    owner_tile_turns = jax.random.permutation(jax.random.fold_in(key_of[2], 3), ATM_BLOCKS // BY)
    owner_tile = jax.vmap(lambda own, number: assign_block(jax.random.fold_in(key_of[2], 2), own, number, BY, N_TILE, R, CAP, 2))(owner_tile_keys, owner_tile_turns).reshape((ATM_BLOCKS, R))
    dest_block = with_ends(jax.random.randint(key_of[3], (ATM_BLOCKS, R), 0, BY), jax.random.fold_in(key_of[3], 1), 0, BY - 1).astype(jnp.int32)
    table_index = with_ends(jax.random.randint(key_of[4], (ATM_BLOCKS, R), 0, NTAB), jax.random.fold_in(key_of[4], 1), 0, NTAB - 1).astype(jnp.int32)
    tables = scatter_about(key_of[5], (NTAB, BX, BX), BX ** -0.5, 0.375, (), jnp.float32)
    land_mask = with_ends((jax.random.randint(key_of[6], (NY, BX), 0, 4) < 3).astype(jnp.int32), jax.random.fold_in(key_of[6], 1), 0, 1)
    return {"fields": fields, "coefficients": coefficients, "owner_tile": owner_tile, "dest_block": dest_block, "table_index": table_index, "tables": tables, "land_mask": land_mask}


forcing_rate = 0.5


def substep(field, kappa, speed):
    padded = jnp.pad(field, ((0, 0), (0, 0), (1, 1), (0, 0)))
    upper_row = padded[:, :, :-2]
    lower_row = padded[:, :, 2:]
    laplace = upper_row + lower_row + jnp.roll(field, 1, axis=3) + jnp.roll(field, -1, axis=3) - 4.0 * field
    return field + kappa[:, None] * laplace - 0.5 * speed[:, None] * (lower_row - upper_row)


def reference(fields, coefficients, owner_tile, dest_block, table_index, tables, land_mask):
    current = fields
    for _ in range(STENCIL_SUBSTEPS):
        current = substep(current, coefficients[:, 0], coefficients[:, 1])
    atmos = current[:N_SEC - 1]
    message_values = jnp.stack([atmos[:, 0], atmos[:, 0] - atmos[:, 1]], axis=2).reshape(ATM_BLOCKS, 2, BX)
    flux = jnp.zeros((NY, 2, BX), jnp.float32)
    for owner_slot in range(R):
        target_rows = owner_tile[:, owner_slot] * BY + dest_block[:, owner_slot]
        contrib = jnp.zeros((ATM_BLOCKS, 2, BX), jnp.float32)
        for table_ordinal in range(NTAB):
            weighted_values = jnp.einsum("wok,kt->wot", message_values, tables[table_ordinal], precision=lax.Precision.HIGHEST)
            chosen = (table_index[:, owner_slot] == table_ordinal)[:, None, None]
            contrib = contrib + jnp.where(chosen, weighted_values, 0.0)
        flux = flux.at[target_rows].add(contrib)
    ocean = current[N_SEC - 1]
    water = land_mask.astype(jnp.float32)
    top_level = ocean[0] + forcing_rate * water * flux[:, 0]
    second_level = ocean[1] + forcing_rate * water * flux[:, 1]
    forced = jnp.concatenate([top_level[None], second_level[None], ocean[2:]], axis=0)
    sea = water * top_level
    atmosphere_surface_field = jnp.zeros((ATM_BLOCKS, BX), jnp.float32)
    for owner_slot in range(R):
        target_rows = owner_tile[:, owner_slot] * BY + dest_block[:, owner_slot]
        values = sea[target_rows]
        for table_ordinal in range(NTAB):
            mirrored = jnp.dot(values, tables[table_ordinal].T, precision=lax.Precision.HIGHEST)
            chosen = (table_index[:, owner_slot] == table_ordinal)[:, None]
            atmosphere_surface_field = atmosphere_surface_field + jnp.where(chosen, mirrored, 0.0)
    fields_out = jnp.concatenate([current[:N_SEC - 1], forced[None]], axis=0)
    surface = jnp.concatenate([atmosphere_surface_field.reshape(N_SEC - 1, NY, BX), sea[None]], axis=0)
    return fields_out, surface
```

```python
import functools

import jax
import jax.numpy as jnp
from jax import lax
from jax.experimental import pallas as pl
from jax.experimental.pallas import tpu as pltpu
from jax.sharding import PartitionSpec as P

forcing_rate = 0.5

F32 = jnp.float32
BF16 = jnp.bfloat16
PAD = 8


def matmul(a, b):
    return lax.dot_general(a, b, (((1,), (0,)), ((), ())), preferred_element_type=F32)


def split(x):
    hi = x.astype(BF16)
    return hi, (x - hi.astype(F32)).astype(BF16)


def iota(shape, dim):
    return lax.broadcasted_iota(jnp.int32, shape, dim)


def kernel(
    n_sec, n_tile, cap,
    fields, coef, ot_in, db_in, ti_in, tables, mask_in,
    fo, su,
    ext, cext, mid, ot, db, ti, tab, mask, hsend, hrecv,
    thi, tlo, tthi, ttlo, mmat, mtmat, pthi, ptlo, send, recv,
    x0, x1, d0, d1, smat, rmat, ret, arr,
    in_sem, hs_sem, hr_sem, fs_sem, fr_sem, bs_sem, br_sem,
):
    n_atm = n_sec - 1
    ocean_sec = n_sec - 1
    half = n_tile // 2
    levels, rows, width = fo.shape[1:]
    ntab = tables.shape[0]
    top, low = PAD, PAD + rows
    sec = lax.axis_index("sec")
    tile = lax.axis_index("tile")
    upper = lax.rem(tile + n_tile - 1, n_tile)
    lower = lax.rem(tile + 1, n_tile)
    is_ocean = sec == ocean_sec
    parity = lax.rem(tile, 2)

    def load(number, src, dst):
        return pltpu.make_async_copy(src, dst, in_sem.at[number])

    loads = [
        load(0, fields.at[0], ext.at[:, top:low, :]),
        load(1, coef.at[0], cext.at[:, top:low, :]),
        load(2, ot_in, ot),
        load(3, db_in, db),
        load(4, ti_in, ti),
        load(5, tables, tab),
        load(6, mask_in, mask),
    ]
    for copy in loads:
        copy.start()

    barrier = pltpu.get_barrier_semaphore()

    def greet(s, t):
        pl.semaphore_signal(barrier, inc=1, device_id=(s, t), device_id_type=pl.DeviceIdType.MESH)

    greet(sec, upper)
    greet(sec, lower)

    @pl.when(is_ocean)
    def _():
        for a in range(n_atm):
            lax.fori_loop(0, n_tile, lambda k, c: (greet(a, lax.rem(tile + k, n_tile)), c)[1], 0)

    @pl.when(jnp.logical_not(is_ocean))
    def _():
        lax.fori_loop(0, n_tile, lambda k, c: (greet(ocean_sec, lax.rem(tile + k, n_tile)), c)[1], 0)

    zero = jnp.zeros((PAD, width), F32)
    for l in range(levels):
        ext[l, 0:top, :] = zero
        ext[l, low : low + PAD, :] = zero
    for c in range(2):
        cext[c, 0:top, :] = zero
        cext[c, low : low + PAD, :] = zero
        hsend[c, 8:16, :] = zero
    loads[0].wait()
    for l in range(levels):
        hsend[0, 2 * l : 2 * l + 2, :] = ext[l, top : top + 2, :]
        hsend[1, 2 * l : 2 * l + 2, :] = ext[l, low - 2 : low, :]
    loads[1].wait()
    for c in range(2):
        hsend[0, 8 + c : 9 + c, :] = cext[c, top : top + 1, :]
        hsend[1, 8 + c : 9 + c, :] = cext[c, low - 1 : low, :]

    @pl.when(is_ocean)
    def _():
        pl.semaphore_wait(barrier, 2 + n_atm * n_tile)

    @pl.when(jnp.logical_not(is_ocean))
    def _():
        pl.semaphore_wait(barrier, 2 + n_tile)

    def halo(way, to):
        return pltpu.make_async_remote_copy(
            src_ref=hsend.at[way],
            dst_ref=hrecv.at[1 - way],
            send_sem=hs_sem.at[way],
            recv_sem=hr_sem.at[1 - way],
            device_id=(sec, to),
            device_id_type=pl.DeviceIdType.MESH,
        )

    halos = [halo(0, upper), halo(1, lower)]
    for copy in halos:
        copy.start()

    loads[2].wait()
    loads[3].wait()
    loads[4].wait()
    loads[5].wait()
    loads[6].wait()

    lane = iota((8, 128), 1)
    left = lane < 64

    @pl.when(is_ocean)
    def _():
        mine_of = tile.astype(F32)
        pair_rows = x0.shape[0]
        for k in range(pair_rows):
            cols = slice(128 * k, 128 * (k + 1))
            x0[k : k + 1, :] = ot[0:1, cols].astype(F32)
            x1[k : k + 1, :] = ot[1:2, cols].astype(F32)
            d0[k : k + 1, :] = db[0:1, cols].astype(F32) + 1.0
            d1[k : k + 1, :] = db[1:2, cols].astype(F32) + 1.0
        src, dst = iota((128, 128), 0), iota((128, 128), 1)
        same = (src // 64) == (dst // 64)
        both = same.astype(F32).astype(BF16)
        before = (same & (src < dst)).astype(F32).astype(BF16)
        mine0 = x0[...] == mine_of
        mine1 = x1[...] == mine_of
        m0 = mine0.astype(F32).astype(BF16)
        m1 = mine1.astype(F32).astype(BF16)
        x0[...] = jnp.where(mine0, matmul(m0, before), -1.0)
        x1[...] = jnp.where(mine1, matmul(m1, before) + matmul(m0, both), -1.0)
        slot = iota((cap, 128), 0).astype(F32)
        lane_c = iota((half * cap, 128), 1)
        want = (lax.rem(lane_c, 64) + 1).astype(F32)
        left_c = lane_c < 64
        for a in range(n_atm):
            parts = []
            for kk in range(half):
                k = a * half + kk
                parts.append(
                    jnp.where(x0[k : k + 1, :] == slot, d0[k : k + 1, :], 0.0)
                    + jnp.where(x1[k : k + 1, :] == slot, d1[k : k + 1, :], 0.0)
                )
            named = jnp.concatenate(parts, axis=0).astype(BF16)
            hot = (matmul(named, both) == want).astype(F32)
            turned = hot.T
            count = half * cap
            smat[a, :, 0:count] = turned[0:64].astype(BF16)
            smat[a, :, count : 2 * count] = turned[64:128].astype(BF16)
            other = pltpu.roll(hot, 64, 1)
            rmat[a, 0:count, :] = jnp.where(left_c, hot, other).astype(BF16)
            rmat[a, count : 2 * count, :] = jnp.where(left_c, other, hot).astype(BF16)

    @pl.when(jnp.logical_not(is_ocean))
    def _():
        number = sec * n_tile + tile
        cols = pl.ds(pl.multiple_of((number // 2) * 128, 128), 128)

        def pairs(ref):
            r0 = jnp.broadcast_to(ref[0:1, cols].astype(F32), (8, 128))
            r1 = jnp.broadcast_to(ref[1:2, cols].astype(F32), (8, 128))
            even = jnp.where(left, r0, pltpu.roll(r1, 64, 1))
            odd = jnp.where(left, pltpu.roll(r0, 64, 1), r1)
            return jnp.where(parity == 0, even, odd)

        own, entry = pairs(ot), pairs(ti)
        across = jnp.broadcast_to(own[0:1], (128, 128))
        earlier = (across.T == across) & (iota((128, 128), 0) < iota((128, 128), 1))
        rank = jnp.sum(earlier.astype(F32), axis=0, keepdims=True)
        target = own * float(cap) + jnp.broadcast_to(rank, (8, 128))

        def doubled(v):
            turned = pltpu.roll(v, 64, 1)
            return jnp.where(left, v, turned), jnp.where(left, turned, v)

        t0, t1 = doubled(target)
        e0, e1 = doubled(entry)
        slots = iota((n_tile * cap, 128), 0).astype(F32)
        for b in range(ntab // 2):
            here = (lane // 64 + 2 * b).astype(F32)
            v0 = jnp.where(e0 == here, t0, -1.0)
            v1 = jnp.where(e1 == here, t1, -1.0)
            hot = ((slots == v0[0:1]) | (slots == v1[0:1])).astype(F32)
            mmat[:, 128 * b : 128 * (b + 1)] = hot.astype(BF16)
            mtmat[128 * b : 128 * (b + 1), :] = hot.T.astype(BF16)
        for t in range(ntab):
            hi, lo = split(tab[t])
            thi[t] = hi
            tlo[t] = lo

    for copy in halos:
        copy.wait()
    above = jnp.where(tile > 0, hrecv[0], 0.0)
    below = jnp.where(tile < n_tile - 1, hrecv[1], 0.0)
    for l in range(levels):
        ext[l, top - 2 : top, :] = above[2 * l : 2 * l + 2]
        ext[l, low : low + 2, :] = below[2 * l : 2 * l + 2]
    for c in range(2):
        cext[c, top - 1 : top, :] = above[8 + c : 9 + c]
        cext[c, low : low + 1, :] = below[8 + c : 9 + c]

    def substep(u, kappa, speed):
        n = u.shape[0]
        up = pltpu.roll(u, 1, 0)
        down = pltpu.roll(u, n - 1, 0)
        sides = pltpu.roll(u, 1, 1) + pltpu.roll(u, width - 1, 1)
        return u + kappa * (up + down + sides - 4.0 * u) - 0.5 * speed * (down - up)

    def stencil(l):
        kappa, speed = cext[0], cext[1]
        u = substep(ext[l], kappa, speed)
        return substep(u, kappa, speed)[top:low]

    fo[0, 0] = stencil(0)
    fo[0, 1] = stencil(1)

    @pl.when(jnp.logical_not(is_ocean))
    def _():
        f0, f1 = fo[0, 0], fo[0, 1]
        phi, plo = split(jnp.concatenate([f0, f0 - f1], axis=0))
        pall = jnp.concatenate([phi, plo], axis=0)
        for t in range(ntab):
            r = matmul(pall, thi[t])
            r = r[: 2 * rows] + r[2 * rows :] + matmul(phi, tlo[t])
            for c in range(2):
                hi, lo = split(r[c * rows : (c + 1) * rows])
                pthi[t * rows : (t + 1) * rows, c * width : (c + 1) * width] = hi
                ptlo[t * rows : (t + 1) * rows, c * width : (c + 1) * width] = lo
        out = matmul(mmat[...], pthi[...]) + matmul(mmat[...], ptlo[...])
        send[...] = out.reshape(send.shape)

        def ship(k, c):
            o = lax.rem(tile + k, n_tile)
            pltpu.make_async_remote_copy(
                src_ref=send.at[o],
                dst_ref=recv.at[sec, parity, tile // 2],
                send_sem=fs_sem,
                recv_sem=fr_sem.at[sec],
                device_id=(ocean_sec, o),
                device_id_type=pl.DeviceIdType.MESH,
            ).start()
            return c

        lax.fori_loop(0, n_tile, ship, 0)
        for l in range(2, levels):
            fo[0, l] = stencil(l)
        for t in range(ntab):
            hi, lo = split(tab[t].T)
            tthi[t] = hi
            ttlo[t] = lo
        pltpu.make_async_copy(arr, arr, br_sem).wait()
        uhi, ulo = split(arr[...].reshape(n_tile * cap, width))
        v = matmul(mtmat[...], uhi) + matmul(mtmat[...], ulo)
        total = jnp.zeros((rows, width), F32)
        for t in range(ntab):
            vhi, vlo = split(v[t * rows : (t + 1) * rows])
            r = matmul(jnp.concatenate([vhi, vlo], axis=0), tthi[t])
            total = total + r[:rows] + r[rows:] + matmul(vhi, ttlo[t])
        su[0] = total
        pltpu.make_async_copy(send, send, fs_sem).wait()

    @pl.when(is_ocean)
    def _():
        for l in range(2, levels):
            fo[0, l] = stencil(l)
        flux = jnp.zeros((rows, 2 * width), F32)
        for a in range(n_atm):
            pltpu.make_async_copy(recv.at[a], recv.at[a], fr_sem.at[a]).wait()
            hi, lo = split(recv[a].reshape(n_tile * cap, 2 * width))
            flux = flux + matmul(smat[a], hi) + matmul(smat[a], lo)
        water = mask[...].astype(F32)
        first = fo[0, 0] + forcing_rate * water * flux[:, :width]
        second = fo[0, 1] + forcing_rate * water * flux[:, width:]
        sea = water * first
        hi, lo = split(sea)
        both = jnp.concatenate([hi, lo], axis=0)
        for a in range(n_atm):
            ret[a] = matmul(rmat[a], both).reshape(ret.shape[1:])

            def back(k, c):
                t = lax.rem(tile + k, n_tile)
                pltpu.make_async_remote_copy(
                    src_ref=ret.at[a, lax.rem(t, 2), t // 2],
                    dst_ref=arr.at[tile],
                    send_sem=bs_sem,
                    recv_sem=br_sem,
                    device_id=(a, t),
                    device_id_type=pl.DeviceIdType.MESH,
                ).start()
                return c

            lax.fori_loop(0, n_tile, back, 0)
        fo[0, 0] = first
        fo[0, 1] = second
        su[0] = sea
        pltpu.make_async_copy(ret, ret, bs_sem).wait()


def local(fields, coefficients, owner_tile, dest_block, table_index, tables, land_mask):
    n_sec = lax.axis_size("sec")
    n_tile = lax.axis_size("tile")
    _, levels, rows, width = fields.shape
    blocks, fan_out = owner_tile.shape
    ntab = tables.shape[0]
    cap = 2 * fan_out * rows // n_tile
    n_atm = n_sec - 1
    half = n_tile // 2
    padded = rows + 2 * PAD
    slots = n_tile * cap
    scratch = [
        pltpu.VMEM((levels, padded, width), F32),
        pltpu.VMEM((2, padded, width), F32),
        pltpu.VMEM((levels, padded, width), F32),
        pltpu.VMEM((fan_out, blocks), jnp.int32),
        pltpu.VMEM((fan_out, blocks), jnp.int32),
        pltpu.VMEM((fan_out, blocks), jnp.int32),
        pltpu.VMEM((ntab, width, width), F32),
        pltpu.VMEM((rows, width), jnp.int32),
        pltpu.VMEM((2, 16, width), F32),
        pltpu.VMEM((2, 16, width), F32),
        pltpu.VMEM((ntab, width, width), BF16),
        pltpu.VMEM((ntab, width, width), BF16),
        pltpu.VMEM((ntab, width, width), BF16),
        pltpu.VMEM((ntab, width, width), BF16),
        pltpu.VMEM((slots, ntab * rows), BF16),
        pltpu.VMEM((ntab * rows, slots), BF16),
        pltpu.VMEM((ntab * rows, 2 * width), BF16),
        pltpu.VMEM((ntab * rows, 2 * width), BF16),
        pltpu.VMEM((n_tile, cap, 2 * width), F32),
        pltpu.VMEM((n_atm, 2, half, cap, 2 * width), F32),
        pltpu.VMEM((n_atm * half, 2 * rows), F32),
        pltpu.VMEM((n_atm * half, 2 * rows), F32),
        pltpu.VMEM((n_atm * half, 2 * rows), F32),
        pltpu.VMEM((n_atm * half, 2 * rows), F32),
        pltpu.VMEM((n_atm, rows, slots), BF16),
        pltpu.VMEM((n_atm, slots, 2 * rows), BF16),
        pltpu.VMEM((n_atm, 2, half, cap, width), F32),
        pltpu.VMEM((n_tile, cap, width), F32),
        pltpu.SemaphoreType.DMA((7,)),
        pltpu.SemaphoreType.DMA((2,)),
        pltpu.SemaphoreType.DMA((2,)),
        pltpu.SemaphoreType.DMA,
        pltpu.SemaphoreType.DMA((n_atm,)),
        pltpu.SemaphoreType.DMA,
        pltpu.SemaphoreType.DMA,
    ]
    return pl.pallas_call(
        functools.partial(kernel, n_sec, n_tile, cap),
        out_shape=(
            jax.ShapeDtypeStruct(fields.shape, F32),
            jax.ShapeDtypeStruct((1, rows, width), F32),
        ),
        in_specs=[pl.BlockSpec(memory_space=pl.ANY)] * 7,
        out_specs=(
            pl.BlockSpec(memory_space=pltpu.VMEM),
            pl.BlockSpec(memory_space=pltpu.VMEM),
        ),
        scratch_shapes=scratch,
        compiler_params=pltpu.CompilerParams(
            collective_id=0, has_side_effects=True, vmem_limit_bytes=32 * 1024 * 1024
        ),
    )(fields, coefficients, owner_tile.T, dest_block.T, table_index.T, tables, land_mask)


def solution(mesh):
    placed = (
        P("sec", None, "tile", None),
        P("sec", None, "tile", None),
        P(),
        P(),
        P(),
        P(),
        P("tile", None),
    )
    return jax.shard_map(
        local,
        mesh=mesh,
        in_specs=placed,
        out_specs=(P("sec", None, "tile", None), P("sec", "tile", None)),
        check_vma=False,
    )
```

```python
import functools

import jax
import jax.numpy as jnp
from jax import lax
from jax.experimental import pallas as pl
from jax.experimental.pallas import tpu as pltpu
from jax.sharding import PartitionSpec as P

forcing_rate = 0.5

F32 = jnp.float32
BF16 = jnp.bfloat16
PAD = 8


def matmul(a, b):
    return lax.dot_general(a, b, (((1,), (0,)), ((), ())), preferred_element_type=F32)


def split(x):
    hi = x.astype(BF16)
    return hi, (x - hi.astype(F32)).astype(BF16)


def iota(shape, dim):
    return lax.broadcasted_iota(jnp.int32, shape, dim)


def kernel(
    n_sec, n_tile, cap,
    fields, coef, ot_in, db_in, ti_in, tables, mask_in,
    fo, su,
    ext, cext, ot, db, ti, tab, mask, hsend, hrecv,
    thi, tlo, tthi, ttlo, mmat, mtmat, pthi, ptlo, send, recv,
    x0, x1, d0, d1, smat, rmat, ret, arr, mine_sum, far_sum,
    in_sem, hs_sem, hr_sem, fs_sem, fr_sem, bs_sem, br_sem, ps_sem, pr_sem,
):
    n_atm = n_sec - 1
    ocean_sec = n_sec - 1
    near_sec = n_sec - 2
    half = n_tile // 2
    levels, rows, width = fo.shape[1:]
    ntab = tables.shape[0]
    top, low = PAD, PAD + rows
    sec = lax.axis_index("sec")
    tile = lax.axis_index("tile")
    upper = lax.rem(tile + n_tile - 1, n_tile)
    lower = lax.rem(tile + 1, n_tile)
    is_ocean = sec == ocean_sec
    is_near = sec == near_sec
    is_far = sec < near_sec
    parity = lax.rem(tile, 2)

    def flipped(t):
        return t + 1 - 2 * lax.rem(t, 2)


    def load(number, src, dst):
        return pltpu.make_async_copy(src, dst, in_sem.at[number])

    loads = [
        load(0, fields.at[0], ext.at[:, top:low, :]),
        load(1, coef.at[0], cext.at[:, top:low, :]),
        load(2, ot_in, ot),
        load(3, db_in, db),
        load(4, ti_in, ti),
        load(5, tables, tab),
        load(6, mask_in, mask),
    ]
    for copy in loads:
        copy.start()

    barrier = pltpu.get_barrier_semaphore()

    def greet(s, t):
        pl.semaphore_signal(barrier, inc=1, device_id=(s, t), device_id_type=pl.DeviceIdType.MESH)

    def greet_tiles(s, first):
        def one(k, c):
            greet(s, lax.rem(tile + k, n_tile))
            return c

        lax.fori_loop(first, n_tile, one, 0)

    @pl.when(is_ocean)
    def _():
        for a in range(n_atm):
            greet_tiles(a, 0)
        greet(sec, upper)
        greet(sec, lower)

    @pl.when(jnp.logical_not(is_ocean))
    def _():
        greet_tiles(ocean_sec, 0)

    @pl.when(is_far)
    def _():
        greet_tiles(sec, 1)

    @pl.when(is_near)
    def _():
        greet(sec, upper)
        greet(sec, lower)

    zero = jnp.zeros((PAD, width), F32)
    for l in range(levels):
        ext[l, 0:top, :] = zero
        ext[l, low : low + PAD, :] = zero
    for c in range(2):
        cext[c, 0:top, :] = zero
        cext[c, low : low + PAD, :] = zero
        hsend[c, 8:16, :] = zero
    loads[0].wait()
    for l in range(levels):
        hsend[0, 2 * l : 2 * l + 2, :] = ext[l, top : top + 2, :]
        hsend[1, 2 * l : 2 * l + 2, :] = ext[l, low - 2 : low, :]
    loads[1].wait()
    for c in range(2):
        hsend[0, 8 + c : 9 + c, :] = cext[c, top : top + 1, :]
        hsend[1, 8 + c : 9 + c, :] = cext[c, low - 1 : low, :]

    @pl.when(is_ocean)
    def _():
        pl.semaphore_wait(barrier, 2 + n_atm * n_tile)

    @pl.when(is_far)
    def _():
        pl.semaphore_wait(barrier, n_tile - 1 + n_tile)

    @pl.when(is_near)
    def _():
        pl.semaphore_wait(barrier, 2 + n_tile)

    def halo(way, to):
        return pltpu.make_async_remote_copy(
            src_ref=hsend.at[way],
            dst_ref=hrecv.at[1 - way],
            send_sem=hs_sem.at[way],
            recv_sem=hr_sem.at[1 - way],
            device_id=(sec, to),
            device_id_type=pl.DeviceIdType.MESH,
        )

    halos = [halo(0, upper), halo(1, lower)]
    for copy in halos:
        copy.start()

    loads[2].wait()
    loads[3].wait()
    loads[4].wait()
    loads[5].wait()
    loads[6].wait()

    lane = iota((8, 128), 1)
    left = lane < 64

    def place(number, a, owner):
        for kk in range(half):
            cols = pl.ds(pl.multiple_of((a * half + kk) * 128, 128), 128)
            x0[kk : kk + 1, :] = ot[0:1, cols].astype(F32)
            x1[kk : kk + 1, :] = ot[1:2, cols].astype(F32)
            d0[kk : kk + 1, :] = db[0:1, cols].astype(F32) + 1.0
            d1[kk : kk + 1, :] = db[1:2, cols].astype(F32) + 1.0
        src, dst = iota((128, 128), 0), iota((128, 128), 1)
        same = (src // 64) == (dst // 64)
        both = same.astype(F32).astype(BF16)
        before = (same & (src < dst)).astype(F32).astype(BF16)
        mine_of = owner.astype(F32)
        mine0 = x0[...] == mine_of
        mine1 = x1[...] == mine_of
        m0 = mine0.astype(F32).astype(BF16)
        m1 = mine1.astype(F32).astype(BF16)
        x0[...] = jnp.where(mine0, matmul(m0, before), -1.0)
        x1[...] = jnp.where(mine1, matmul(m1, before) + matmul(m0, both), -1.0)
        slot = iota((cap, 128), 0).astype(F32)
        parts = []
        for kk in range(half):
            parts.append(
                jnp.where(x0[kk : kk + 1, :] == slot, d0[kk : kk + 1, :], 0.0)
                + jnp.where(x1[kk : kk + 1, :] == slot, d1[kk : kk + 1, :], 0.0)
            )
        named = jnp.concatenate(parts, axis=0).astype(BF16)
        count = half * cap
        lane_c = iota((count, 128), 1)
        left_c = lane_c < 64
        want = (lax.rem(lane_c, 64) + 1).astype(F32)
        hot = (matmul(named, both) == want).astype(F32)
        turned = hot.T
        smat[number, :, 0:count] = turned[0:64].astype(BF16)
        smat[number, :, count : 2 * count] = turned[64:128].astype(BF16)
        other = pltpu.roll(hot, 64, 1)
        rmat[number, 0:count, :] = jnp.where(left_c, hot, other).astype(BF16)
        rmat[number, count : 2 * count, :] = jnp.where(left_c, other, hot).astype(BF16)

    @pl.when(is_ocean)
    def _():
        for a in range(n_atm):
            place(a, a, tile)

    @pl.when(is_far)
    def _():
        place(0, sec, flipped(tile))

    @pl.when(jnp.logical_not(is_ocean))
    def _():
        number = sec * n_tile + tile
        cols = pl.ds(pl.multiple_of((number // 2) * 128, 128), 128)

        def pairs(ref):
            r0 = jnp.broadcast_to(ref[0:1, cols].astype(F32), (8, 128))
            r1 = jnp.broadcast_to(ref[1:2, cols].astype(F32), (8, 128))
            even = jnp.where(left, r0, pltpu.roll(r1, 64, 1))
            odd = jnp.where(left, pltpu.roll(r0, 64, 1), r1)
            return jnp.where(parity == 0, even, odd)

        own, entry = pairs(ot), pairs(ti)
        across = jnp.broadcast_to(own[0:1], (128, 128))
        earlier = (across.T == across) & (iota((128, 128), 0) < iota((128, 128), 1))
        rank = jnp.sum(earlier.astype(F32), axis=0, keepdims=True)
        target = own * float(cap) + jnp.broadcast_to(rank, (8, 128))

        def doubled(v):
            turned = pltpu.roll(v, 64, 1)
            return jnp.where(left, v, turned), jnp.where(left, turned, v)

        t0, t1 = doubled(target)
        e0, e1 = doubled(entry)
        slots = iota((n_tile * cap, 128), 0).astype(F32)
        for b in range(ntab // 2):
            here = (lane // 64 + 2 * b).astype(F32)
            v0 = jnp.where(e0 == here, t0, -1.0)
            v1 = jnp.where(e1 == here, t1, -1.0)
            hot = ((slots == v0[0:1]) | (slots == v1[0:1])).astype(F32)
            mmat[:, 128 * b : 128 * (b + 1)] = hot.astype(BF16)
            mtmat[128 * b : 128 * (b + 1), :] = hot.T.astype(BF16)
        for t in range(ntab):
            hi, lo = split(tab[t])
            thi[t] = hi
            tlo[t] = lo

    for copy in halos:
        copy.wait()
    above = jnp.where(tile > 0, hrecv[0], 0.0)
    below = jnp.where(tile < n_tile - 1, hrecv[1], 0.0)
    for l in range(levels):
        ext[l, top - 2 : top, :] = above[2 * l : 2 * l + 2]
        ext[l, low : low + 2, :] = below[2 * l : 2 * l + 2]
    for c in range(2):
        cext[c, top - 1 : top, :] = above[8 + c : 9 + c]
        cext[c, low : low + 1, :] = below[8 + c : 9 + c]

    def substep(u, kappa, speed):
        n = u.shape[0]
        up = pltpu.roll(u, 1, 0)
        down = pltpu.roll(u, n - 1, 0)
        sides = pltpu.roll(u, 1, 1) + pltpu.roll(u, width - 1, 1)
        return u + kappa * (up + down + sides - 4.0 * u) - 0.5 * speed * (down - up)

    def stencil(l):
        kappa, speed = cext[0], cext[1]
        u = substep(ext[l], kappa, speed)
        return substep(u, kappa, speed)[top:low]

    fo[0, 0] = stencil(0)

    def pack(part, row):
        hi, lo = split(row)
        stacked = jnp.concatenate([hi, lo], axis=0)
        for t in range(ntab):
            r = matmul(stacked, thi[t])
            r = r[:rows] + r[rows:] + matmul(hi, tlo[t])
            here = slice(t * rows, (t + 1) * rows)
            pthi[here, :], ptlo[here, :] = split(r)
        out = matmul(mmat[...], pthi[...]) + matmul(mmat[...], ptlo[...])
        send[part] = out.reshape(send.shape[1:])

    def ship(part, o, to):
        pltpu.make_async_remote_copy(
            src_ref=send.at[part, o],
            dst_ref=recv.at[part, sec, parity, tile // 2],
            send_sem=fs_sem.at[part],
            recv_sem=fr_sem.at[part, sec],
            device_id=to,
            device_id_type=pl.DeviceIdType.MESH,
        ).start()

    def ship_to_ocean(part):
        def one(k, c):
            o = lax.rem(tile + k, n_tile)
            ship(part, o, (ocean_sec, o))
            return c

        lax.fori_loop(0, n_tile, one, 0)

    def ship_to_helpers(part):
        mine = flipped(tile)
        pltpu.make_async_copy(
            send.at[part, mine],
            recv.at[part, sec, parity, tile // 2],
            fr_sem.at[part, sec],
        ).start()

        def one(k, c):
            t = lax.rem(tile + k, n_tile)
            ship(part, flipped(t), (sec, t))
            return c

        lax.fori_loop(1, n_tile, one, 0)

    def spread(number, part, a):
        pltpu.make_async_copy(recv.at[part, a], recv.at[part, a], fr_sem.at[part, a]).wait()
        hi, lo = split(recv[part, a].reshape(n_tile * cap, width))
        return matmul(smat[number], hi) + matmul(smat[number], lo)

    def partial_copy():
        return pltpu.make_async_remote_copy(
            src_ref=mine_sum,
            dst_ref=far_sum.at[sec],
            send_sem=ps_sem,
            recv_sem=pr_sem.at[sec],
            device_id=(ocean_sec, flipped(tile)),
            device_id_type=pl.DeviceIdType.MESH,
        )

    @pl.when(jnp.logical_not(is_ocean))
    def _():
        pack(0, fo[0, 0])
        ship_to_ocean(0)
        for l in range(1, levels):
            fo[0, l] = stencil(l)
        pack(1, fo[0, 0] - fo[0, 1])

        @pl.when(is_near)
        def _():
            ship_to_ocean(1)

        @pl.when(is_far)
        def _():
            ship_to_helpers(1)

        for t in range(ntab):
            hi, lo = split(tab[t].T)
            tthi[t] = hi
            ttlo[t] = lo

        @pl.when(is_far)
        def _():
            mine_sum[...] = spread(0, 1, sec)
            partial_copy().start()

        pltpu.make_async_copy(arr, arr, br_sem).wait()
        uhi, ulo = split(arr[...].reshape(n_tile * cap, width))
        v = matmul(mtmat[...], uhi) + matmul(mtmat[...], ulo)
        total = jnp.zeros((rows, width), F32)
        for t in range(ntab):
            vhi, vlo = split(v[t * rows : (t + 1) * rows])
            r = matmul(jnp.concatenate([vhi, vlo], axis=0), tthi[t])
            total = total + r[:rows] + r[rows:] + matmul(vhi, ttlo[t])
        su[0] = total
        pltpu.make_async_copy(send.at[0], send.at[0], fs_sem.at[0]).wait()

        @pl.when(is_near)
        def _():
            pltpu.make_async_copy(send.at[1], send.at[1], fs_sem.at[1]).wait()

        @pl.when(is_far)
        def _():
            others = send.at[1, 1:n_tile]
            pltpu.make_async_copy(others, others, fs_sem.at[1]).wait()
            partial_copy().wait_send()


    @pl.when(is_ocean)
    def _():
        for l in range(1, levels):
            fo[0, l] = stencil(l)
        water = mask[...].astype(F32)
        flux = spread(near_sec, 0, near_sec)
        for a in range(near_sec):
            flux = flux + spread(a, 0, a)
        first = fo[0, 0] + forcing_rate * water * flux
        sea = water * first
        hi, lo = split(sea)
        both = jnp.concatenate([hi, lo], axis=0)
        for a in range(n_atm):
            ret[a] = matmul(rmat[a], both).reshape(ret.shape[1:])

        def back(k, c):
            t = lax.rem(tile + k, n_tile)
            for a in range(n_atm):
                pltpu.make_async_remote_copy(
                    src_ref=ret.at[a, lax.rem(t, 2), t // 2],
                    dst_ref=arr.at[tile],
                    send_sem=bs_sem,
                    recv_sem=br_sem,
                    device_id=(a, t),
                    device_id_type=pl.DeviceIdType.MESH,
                ).start()
            return c

        lax.fori_loop(0, n_tile, back, 0)
        fo[0, 0] = first
        su[0] = sea
        flux = spread(near_sec, 1, near_sec)
        for a in range(near_sec):
            pltpu.make_async_copy(far_sum.at[a], far_sum.at[a], pr_sem.at[a]).wait()
            flux = flux + far_sum[a]
        fo[0, 1] = fo[0, 1] + forcing_rate * water * flux
        pltpu.make_async_copy(ret, ret, bs_sem).wait()


def local(fields, coefficients, owner_tile, dest_block, table_index, tables, land_mask):
    n_sec = lax.axis_size("sec")
    n_tile = lax.axis_size("tile")
    _, levels, rows, width = fields.shape
    blocks, fan_out = owner_tile.shape
    ntab = tables.shape[0]
    cap = 2 * fan_out * rows // n_tile
    n_atm = n_sec - 1
    half = n_tile // 2
    padded = rows + 2 * PAD
    slots = n_tile * cap
    scratch = [
        pltpu.VMEM((levels, padded, width), F32),
        pltpu.VMEM((2, padded, width), F32),
        pltpu.VMEM((fan_out, blocks), jnp.int32),
        pltpu.VMEM((fan_out, blocks), jnp.int32),
        pltpu.VMEM((fan_out, blocks), jnp.int32),
        pltpu.VMEM((ntab, width, width), F32),
        pltpu.VMEM((rows, width), jnp.int32),
        pltpu.VMEM((2, 16, width), F32),
        pltpu.VMEM((2, 16, width), F32),
        pltpu.VMEM((ntab, width, width), BF16),
        pltpu.VMEM((ntab, width, width), BF16),
        pltpu.VMEM((ntab, width, width), BF16),
        pltpu.VMEM((ntab, width, width), BF16),
        pltpu.VMEM((slots, ntab * rows), BF16),
        pltpu.VMEM((ntab * rows, slots), BF16),
        pltpu.VMEM((ntab * rows, width), BF16),
        pltpu.VMEM((ntab * rows, width), BF16),
        pltpu.VMEM((2, n_tile, cap, width), F32),
        pltpu.VMEM((2, n_atm, 2, half, cap, width), F32),
        pltpu.VMEM((half, 2 * rows), F32),
        pltpu.VMEM((half, 2 * rows), F32),
        pltpu.VMEM((half, 2 * rows), F32),
        pltpu.VMEM((half, 2 * rows), F32),
        pltpu.VMEM((n_atm, rows, slots), BF16),
        pltpu.VMEM((n_atm, slots, 2 * rows), BF16),
        pltpu.VMEM((n_atm, 2, half, cap, width), F32),
        pltpu.VMEM((n_tile, cap, width), F32),
        pltpu.VMEM((rows, width), F32),
        pltpu.VMEM((n_atm - 1, rows, width), F32),
        pltpu.SemaphoreType.DMA((7,)),
        pltpu.SemaphoreType.DMA((2,)),
        pltpu.SemaphoreType.DMA((2,)),
        pltpu.SemaphoreType.DMA((2,)),
        pltpu.SemaphoreType.DMA((2, n_atm)),
        pltpu.SemaphoreType.DMA,
        pltpu.SemaphoreType.DMA,
        pltpu.SemaphoreType.DMA,
        pltpu.SemaphoreType.DMA((n_atm - 1,)),
    ]
    operands = (fields, coefficients, owner_tile.T, dest_block.T, table_index.T, tables, land_mask)
    return pl.pallas_call(
        functools.partial(kernel, n_sec, n_tile, cap),
        out_shape=(
            jax.ShapeDtypeStruct(fields.shape, F32),
            jax.ShapeDtypeStruct((1, rows, width), F32),
        ),
        in_specs=[pl.BlockSpec(memory_space=pltpu.HBM)] * 7,
        out_specs=(
            pl.BlockSpec(memory_space=pltpu.VMEM),
            pl.BlockSpec(memory_space=pltpu.VMEM),
        ),
        scratch_shapes=scratch,
        compiler_params=pltpu.CompilerParams(
            collective_id=0, has_side_effects=True, vmem_limit_bytes=32 * 1024 * 1024
        ),
    )(*(pltpu.with_memory_space_constraint(x, pltpu.HBM) for x in operands))


def solution(mesh):
    placed = (
        P("sec", None, "tile", None),
        P("sec", None, "tile", None),
        P(),
        P(),
        P(),
        P(),
        P("tile", None),
    )
    return jax.shard_map(
        local,
        mesh=mesh,
        in_specs=placed,
        out_specs=(P("sec", None, "tile", None), P("sec", "tile", None)),
        check_vma=False,
    )
```

```python
import functools

import jax
import jax.numpy as jnp
from jax import lax
from jax.experimental import pallas as pl
from jax.experimental.pallas import tpu as pltpu
from jax.sharding import PartitionSpec as P

forcing_rate = 0.5

F32 = jnp.float32
BF16 = jnp.bfloat16
PAD = 8


def matmul(a, b):
    return lax.dot_general(a, b, (((1,), (0,)), ((), ())), preferred_element_type=F32)


def split(x):
    hi = x.astype(BF16)
    return hi, (x - hi.astype(F32)).astype(BF16)


def iota(shape, dim):
    return lax.broadcasted_iota(jnp.int32, shape, dim)


def kernel(
    n_sec, n_tile, cap,
    fields, coef, ot_in, db_in, ti_in, tables, mask_in,
    fo, su,
    ext, cext, ot, db, ti, tab, mask, hsend, hrecv,
    thi, tlo, tthi, ttlo, mmat, mtmat, pthi, ptlo, send, recv,
    x0, x1, d0, d1, smat, rmat, ret, arr, mine_sum, far_sum,
    in_sem, hs_sem, hr_sem, fs_sem, fr_sem, bs_sem, br_sem, ps_sem, pr_sem, z_sem, x_sem,
):
    n_atm = n_sec - 1
    ocean_sec = n_sec - 1
    near_sec = n_sec - 2
    half = n_tile // 2
    levels, rows, width = fo.shape[1:]
    ntab = tables.shape[0]
    top, low = PAD, PAD + rows
    sec = lax.axis_index("sec")
    tile = lax.axis_index("tile")
    upper = lax.rem(tile + n_tile - 1, n_tile)
    lower = lax.rem(tile + 1, n_tile)
    is_ocean = sec == ocean_sec
    is_near = sec == near_sec
    is_far = sec < near_sec
    parity = lax.rem(tile, 2)

    def flipped(t):
        return t + 1 - 2 * lax.rem(t, 2)


    def load(number, src, dst):
        return pltpu.make_async_copy(src, dst, in_sem.at[number])

    loads = [
        load(0, fields.at[0], ext.at[:, top:low, :]),
        load(1, coef.at[0], cext.at[:, top:low, :]),
        load(2, ot_in, ot),
        load(3, db_in, db),
        load(4, ti_in, ti),
        load(5, tables, tab),
        load(6, mask_in, mask),
    ]
    for copy in loads:
        copy.start()

    barrier = pltpu.get_barrier_semaphore()

    def greet(semaphore, s, t):
        pl.semaphore_signal(semaphore, inc=1, device_id=(s, t), device_id_type=pl.DeviceIdType.MESH)

    def z_ring(semaphore):
        for k in range(1, 4):
            greet(semaphore, sec, lax.rem(tile + 8 * k, n_tile))

    def x_ring(semaphore):
        for k in range(1, 4):
            greet(semaphore, sec, (tile // 8) * 8 + lax.rem(lax.rem(tile, 8) + 2 * k, 8))

    for k in range(1, n_sec):
        s = lax.rem(sec + k, n_sec)
        greet(barrier, s, tile)
        greet(barrier, s, flipped(tile))
    greet(barrier, sec, flipped(tile))
    greet(barrier, sec, jnp.where(parity == 0, upper, lower))
    z_ring(barrier)
    x_ring(barrier)

    zero = jnp.zeros((PAD, width), F32)
    for l in range(levels):
        ext[l, 0:top, :] = zero
        ext[l, low : low + PAD, :] = zero
    for c in range(2):
        cext[c, 0:top, :] = zero
        cext[c, low : low + PAD, :] = zero
        hsend[c, 8:16, :] = zero
    loads[0].wait()
    for l in range(levels):
        hsend[0, 2 * l : 2 * l + 2, :] = ext[l, top : top + 2, :]
        hsend[1, 2 * l : 2 * l + 2, :] = ext[l, low - 2 : low, :]
    loads[1].wait()
    for c in range(2):
        hsend[0, 8 + c : 9 + c, :] = cext[c, top : top + 1, :]
        hsend[1, 8 + c : 9 + c, :] = cext[c, low - 1 : low, :]

    pl.semaphore_wait(barrier, 2 * n_sec + 6)

    def halo(way, to):
        return pltpu.make_async_remote_copy(
            src_ref=hsend.at[way],
            dst_ref=hrecv.at[1 - way],
            send_sem=hs_sem.at[way],
            recv_sem=hr_sem.at[1 - way],
            device_id=(sec, to),
            device_id_type=pl.DeviceIdType.MESH,
        )

    halos = [halo(0, upper), halo(1, lower)]
    for copy in halos:
        copy.start()

    z_ring(z_sem)

    loads[2].wait()
    loads[3].wait()
    loads[4].wait()
    loads[5].wait()
    loads[6].wait()

    lane = iota((8, 128), 1)
    left = lane < 64

    def place(number, a, owner):
        for kk in range(half):
            cols = pl.ds(pl.multiple_of((a * half + kk) * 128, 128), 128)
            x0[kk : kk + 1, :] = ot[0:1, cols].astype(F32)
            x1[kk : kk + 1, :] = ot[1:2, cols].astype(F32)
            d0[kk : kk + 1, :] = db[0:1, cols].astype(F32) + 1.0
            d1[kk : kk + 1, :] = db[1:2, cols].astype(F32) + 1.0
        src, dst = iota((128, 128), 0), iota((128, 128), 1)
        same = (src // 64) == (dst // 64)
        both = same.astype(F32).astype(BF16)
        before = (same & (src < dst)).astype(F32).astype(BF16)
        mine_of = owner.astype(F32)
        mine0 = x0[...] == mine_of
        mine1 = x1[...] == mine_of
        m0 = mine0.astype(F32).astype(BF16)
        m1 = mine1.astype(F32).astype(BF16)
        x0[...] = jnp.where(mine0, matmul(m0, before), -1.0)
        x1[...] = jnp.where(mine1, matmul(m1, before) + matmul(m0, both), -1.0)
        slot = iota((cap, 128), 0).astype(F32)
        parts = []
        for kk in range(half):
            parts.append(
                jnp.where(x0[kk : kk + 1, :] == slot, d0[kk : kk + 1, :], 0.0)
                + jnp.where(x1[kk : kk + 1, :] == slot, d1[kk : kk + 1, :], 0.0)
            )
        named = jnp.concatenate(parts, axis=0).astype(BF16)
        count = half * cap
        lane_c = iota((count, 128), 1)
        left_c = lane_c < 64
        want = (lax.rem(lane_c, 64) + 1).astype(F32)
        hot = (matmul(named, both) == want).astype(F32)
        turned = hot.T
        smat[number, :, 0:count] = turned[0:64].astype(BF16)
        smat[number, :, count : 2 * count] = turned[64:128].astype(BF16)
        other = pltpu.roll(hot, 64, 1)
        rmat[number, 0:count, :] = jnp.where(left_c, hot, other).astype(BF16)
        rmat[number, count : 2 * count, :] = jnp.where(left_c, other, hot).astype(BF16)

    @pl.when(is_ocean)
    def _():
        for a in range(n_atm):
            place(a, a, tile)

    @pl.when(is_far)
    def _():
        place(0, sec, flipped(tile))

    @pl.when(jnp.logical_not(is_ocean))
    def _():
        number = sec * n_tile + tile
        cols = pl.ds(pl.multiple_of((number // 2) * 128, 128), 128)

        def pairs(ref):
            r0 = jnp.broadcast_to(ref[0:1, cols].astype(F32), (8, 128))
            r1 = jnp.broadcast_to(ref[1:2, cols].astype(F32), (8, 128))
            even = jnp.where(left, r0, pltpu.roll(r1, 64, 1))
            odd = jnp.where(left, pltpu.roll(r0, 64, 1), r1)
            return jnp.where(parity == 0, even, odd)

        own, entry = pairs(ot), pairs(ti)
        across = jnp.broadcast_to(own[0:1], (128, 128))
        earlier = (across.T == across) & (iota((128, 128), 0) < iota((128, 128), 1))
        rank = jnp.sum(earlier.astype(F32), axis=0, keepdims=True)
        target = own * float(cap) + jnp.broadcast_to(rank, (8, 128))

        def doubled(v):
            turned = pltpu.roll(v, 64, 1)
            return jnp.where(left, v, turned), jnp.where(left, turned, v)

        t0, t1 = doubled(target)
        e0, e1 = doubled(entry)
        slots = iota((n_tile * cap, 128), 0).astype(F32)
        for b in range(ntab // 2):
            here = (lane // 64 + 2 * b).astype(F32)
            v0 = jnp.where(e0 == here, t0, -1.0)
            v1 = jnp.where(e1 == here, t1, -1.0)
            hot = ((slots == v0[0:1]) | (slots == v1[0:1])).astype(F32)
            mmat[:, 128 * b : 128 * (b + 1)] = hot.astype(BF16)
            mtmat[128 * b : 128 * (b + 1), :] = hot.T.astype(BF16)
        for t in range(ntab):
            hi, lo = split(tab[t])
            thi[t] = hi
            tlo[t] = lo

    pl.semaphore_wait(z_sem, 3)
    x_ring(x_sem)

    for copy in halos:
        copy.wait()
    above = jnp.where(tile > 0, hrecv[0], 0.0)
    below = jnp.where(tile < n_tile - 1, hrecv[1], 0.0)
    for l in range(levels):
        ext[l, top - 2 : top, :] = above[2 * l : 2 * l + 2]
        ext[l, low : low + 2, :] = below[2 * l : 2 * l + 2]
    for c in range(2):
        cext[c, top - 1 : top, :] = above[8 + c : 9 + c]
        cext[c, low : low + 1, :] = below[8 + c : 9 + c]

    def substep(u, kappa, speed):
        n = u.shape[0]
        up = pltpu.roll(u, 1, 0)
        down = pltpu.roll(u, n - 1, 0)
        sides = pltpu.roll(u, 1, 1) + pltpu.roll(u, width - 1, 1)
        return u + kappa * (up + down + sides - 4.0 * u) - 0.5 * speed * (down - up)

    def stencil(l):
        kappa, speed = cext[0], cext[1]
        u = substep(ext[l], kappa, speed)
        return substep(u, kappa, speed)[top:low]

    fo[0, 0] = stencil(0)

    def pack(part, row):
        hi, lo = split(row)
        stacked = jnp.concatenate([hi, lo], axis=0)
        for t in range(ntab):
            r = matmul(stacked, thi[t])
            r = r[:rows] + r[rows:] + matmul(hi, tlo[t])
            here = slice(t * rows, (t + 1) * rows)
            pthi[here, :], ptlo[here, :] = split(r)
        out = matmul(mmat[...], pthi[...]) + matmul(mmat[...], ptlo[...])
        send[part] = out.reshape(send.shape[1:])

    def ship(part, o, to):
        pltpu.make_async_remote_copy(
            src_ref=send.at[part, o],
            dst_ref=recv.at[part, sec, parity, tile // 2],
            send_sem=fs_sem.at[part],
            recv_sem=fr_sem.at[part, sec],
            device_id=to,
            device_id_type=pl.DeviceIdType.MESH,
        ).start()

    def ship_to_ocean(part):
        def one(k, c):
            o = lax.rem(tile + k, n_tile)
            ship(part, o, (ocean_sec, o))
            return c

        lax.fori_loop(0, n_tile, one, 0)

    def ship_to_helpers(part):
        mine = flipped(tile)
        pltpu.make_async_copy(
            send.at[part, mine],
            recv.at[part, sec, parity, tile // 2],
            fr_sem.at[part, sec],
        ).start()

        def one(k, c):
            t = lax.rem(tile + k, n_tile)
            ship(part, flipped(t), (sec, t))
            return c

        lax.fori_loop(1, n_tile, one, 0)

    def spread(number, part, a):
        pltpu.make_async_copy(recv.at[part, a], recv.at[part, a], fr_sem.at[part, a]).wait()
        hi, lo = split(recv[part, a].reshape(n_tile * cap, width))
        return matmul(smat[number], hi) + matmul(smat[number], lo)

    def partial_copy():
        return pltpu.make_async_remote_copy(
            src_ref=mine_sum,
            dst_ref=far_sum.at[sec],
            send_sem=ps_sem,
            recv_sem=pr_sem.at[sec],
            device_id=(ocean_sec, flipped(tile)),
            device_id_type=pl.DeviceIdType.MESH,
        )

    @pl.when(jnp.logical_not(is_ocean))
    def _():
        pack(0, fo[0, 0])
        pl.semaphore_wait(x_sem, 3)
        ship_to_ocean(0)
        for l in range(1, levels):
            fo[0, l] = stencil(l)
        pack(1, fo[0, 0] - fo[0, 1])

        @pl.when(is_near)
        def _():
            ship_to_ocean(1)

        @pl.when(is_far)
        def _():
            ship_to_helpers(1)

        for t in range(ntab):
            hi, lo = split(tab[t].T)
            tthi[t] = hi
            ttlo[t] = lo

        @pl.when(is_far)
        def _():
            mine_sum[...] = spread(0, 1, sec)
            partial_copy().start()

        pltpu.make_async_copy(arr, arr, br_sem).wait()
        uhi, ulo = split(arr[...].reshape(n_tile * cap, width))
        v = matmul(mtmat[...], uhi) + matmul(mtmat[...], ulo)
        total = jnp.zeros((rows, width), F32)
        for t in range(ntab):
            vhi, vlo = split(v[t * rows : (t + 1) * rows])
            r = matmul(jnp.concatenate([vhi, vlo], axis=0), tthi[t])
            total = total + r[:rows] + r[rows:] + matmul(vhi, ttlo[t])
        su[0] = total
        pltpu.make_async_copy(send.at[0], send.at[0], fs_sem.at[0]).wait()

        @pl.when(is_near)
        def _():
            pltpu.make_async_copy(send.at[1], send.at[1], fs_sem.at[1]).wait()

        @pl.when(is_far)
        def _():
            others = send.at[1, 1:n_tile]
            pltpu.make_async_copy(others, others, fs_sem.at[1]).wait()
            partial_copy().wait_send()


    @pl.when(is_ocean)
    def _():
        pl.semaphore_wait(x_sem, 3)
        for l in range(1, levels):
            fo[0, l] = stencil(l)
        water = mask[...].astype(F32)
        flux = spread(near_sec, 0, near_sec)
        for a in range(near_sec):
            flux = flux + spread(a, 0, a)
        first = fo[0, 0] + forcing_rate * water * flux
        sea = water * first
        hi, lo = split(sea)
        both = jnp.concatenate([hi, lo], axis=0)
        for a in range(n_atm):
            ret[a] = matmul(rmat[a], both).reshape(ret.shape[1:])

        def back(sections):
            def one(k, c):
                i = lax.rem(k, 16)
                j = i // 2
                z = 2 * (k // 16) + lax.rem(i + tile // 8, 2)
                t = 8 * z + 2 * lax.rem(j + tile // 2, 4) + j // 4
                for a in sections:
                    pltpu.make_async_remote_copy(
                        src_ref=ret.at[a, lax.rem(t, 2), t // 2],
                        dst_ref=arr.at[tile],
                        send_sem=bs_sem,
                        recv_sem=br_sem,
                        device_id=(a, t),
                        device_id_type=pl.DeviceIdType.MESH,
                    ).start()
                return c

            lax.fori_loop(0, n_tile, one, 0)

        back((1, 0, 2))
        fo[0, 0] = first
        su[0] = sea
        flux = spread(near_sec, 1, near_sec)
        for a in range(near_sec):
            pltpu.make_async_copy(far_sum.at[a], far_sum.at[a], pr_sem.at[a]).wait()
            flux = flux + far_sum[a]
        fo[0, 1] = fo[0, 1] + forcing_rate * water * flux
        pltpu.make_async_copy(ret, ret, bs_sem).wait()


def store(fields, surface, fields_out, surface_out, sems):
    copies = [
        pltpu.make_async_copy(fields, fields_out, sems.at[0]),
        pltpu.make_async_copy(surface, surface_out, sems.at[1]),
    ]
    for copy in copies:
        copy.start()
    for copy in copies:
        copy.wait()


def local(fields, coefficients, owner_tile, dest_block, table_index, tables, land_mask):
    n_sec = lax.axis_size("sec")
    n_tile = lax.axis_size("tile")
    _, levels, rows, width = fields.shape
    blocks, fan_out = owner_tile.shape
    ntab = tables.shape[0]
    cap = 2 * fan_out * rows // n_tile
    n_atm = n_sec - 1
    half = n_tile // 2
    padded = rows + 2 * PAD
    slots = n_tile * cap
    scratch = [
        pltpu.VMEM((levels, padded, width), F32),
        pltpu.VMEM((2, padded, width), F32),
        pltpu.VMEM((fan_out, blocks), jnp.int32),
        pltpu.VMEM((fan_out, blocks), jnp.int32),
        pltpu.VMEM((fan_out, blocks), jnp.int32),
        pltpu.VMEM((ntab, width, width), F32),
        pltpu.VMEM((rows, width), jnp.int32),
        pltpu.VMEM((2, 16, width), F32),
        pltpu.VMEM((2, 16, width), F32),
        pltpu.VMEM((ntab, width, width), BF16),
        pltpu.VMEM((ntab, width, width), BF16),
        pltpu.VMEM((ntab, width, width), BF16),
        pltpu.VMEM((ntab, width, width), BF16),
        pltpu.VMEM((slots, ntab * rows), BF16),
        pltpu.VMEM((ntab * rows, slots), BF16),
        pltpu.VMEM((ntab * rows, width), BF16),
        pltpu.VMEM((ntab * rows, width), BF16),
        pltpu.VMEM((2, n_tile, cap, width), F32),
        pltpu.VMEM((2, n_atm, 2, half, cap, width), F32),
        pltpu.VMEM((half, 2 * rows), F32),
        pltpu.VMEM((half, 2 * rows), F32),
        pltpu.VMEM((half, 2 * rows), F32),
        pltpu.VMEM((half, 2 * rows), F32),
        pltpu.VMEM((n_atm, rows, slots), BF16),
        pltpu.VMEM((n_atm, slots, 2 * rows), BF16),
        pltpu.VMEM((n_atm, 2, half, cap, width), F32),
        pltpu.VMEM((n_tile, cap, width), F32),
        pltpu.VMEM((rows, width), F32),
        pltpu.VMEM((n_atm - 1, rows, width), F32),
        pltpu.SemaphoreType.DMA((7,)),
        pltpu.SemaphoreType.DMA((2,)),
        pltpu.SemaphoreType.DMA((2,)),
        pltpu.SemaphoreType.DMA((2,)),
        pltpu.SemaphoreType.DMA((2, n_atm)),
        pltpu.SemaphoreType.DMA,
        pltpu.SemaphoreType.DMA,
        pltpu.SemaphoreType.DMA,
        pltpu.SemaphoreType.DMA((n_atm - 1,)),
        pltpu.SemaphoreType.REGULAR,
        pltpu.SemaphoreType.REGULAR,
    ]
    operands = (fields, coefficients, owner_tile.T, dest_block.T, table_index.T, tables, land_mask)
    shapes = (
        jax.ShapeDtypeStruct(fields.shape, F32),
        jax.ShapeDtypeStruct((1, rows, width), F32),
    )
    results = pl.pallas_call(
        functools.partial(kernel, n_sec, n_tile, cap),
        out_shape=shapes,
        in_specs=[pl.BlockSpec(memory_space=pltpu.HBM)] * 7,
        out_specs=(
            pl.BlockSpec(memory_space=pltpu.VMEM),
            pl.BlockSpec(memory_space=pltpu.VMEM),
        ),
        scratch_shapes=scratch,
        compiler_params=pltpu.CompilerParams(
            collective_id=0, has_side_effects=True, vmem_limit_bytes=32 * 1024 * 1024
        ),
    )(*(pltpu.with_memory_space_constraint(x, pltpu.HBM) for x in operands))
    return pl.pallas_call(
        store,
        out_shape=shapes,
        in_specs=[pl.BlockSpec(memory_space=pltpu.VMEM)] * 2,
        out_specs=(pl.BlockSpec(memory_space=pl.ANY),) * 2,
        scratch_shapes=[pltpu.SemaphoreType.DMA((2,))],
    )(*(pltpu.with_memory_space_constraint(x, pltpu.VMEM) for x in results))


def solution(mesh):
    placed = (
        P("sec", None, "tile", None),
        P("sec", None, "tile", None),
        P(),
        P(),
        P(),
        P(),
        P("tile", None),
    )
    return jax.shard_map(
        local,
        mesh=mesh,
        in_specs=placed,
        out_specs=(P("sec", None, "tile", None), P("sec", "tile", None)),
        check_vma=False,
    )
```

```python
import functools

import jax
import jax.numpy as jnp
from jax import lax
from jax.experimental import pallas as pl
from jax.experimental.pallas import tpu as pltpu
from jax.sharding import PartitionSpec as P

forcing_rate = 0.5

F32 = jnp.float32
BF16 = jnp.bfloat16
PAD = 8


def matmul(a, b):
    return lax.dot_general(a, b, (((1,), (0,)), ((), ())), preferred_element_type=F32)


def split(x):
    hi = x.astype(BF16)
    return hi, (x - hi.astype(F32)).astype(BF16)


def iota(shape, dim):
    return lax.broadcasted_iota(jnp.int32, shape, dim)


def kernel(
    n_sec, n_tile, cap,
    fields, coef, ot_in, db_in, ti_in, tables, mask_in,
    fo, su,
    ext, cext, ot, db, ti, tab, mask, hsend, hrecv,
    thi, tlo, tthi, ttlo, mmat, mtmat, pthi, ptlo, send, recv,
    x0, x1, d0, d1, smat, rmat, ret, arr, mine_sum, far_sum, base, flux0, far_mask,
    in_sem, hs_sem, hr_sem, fs_sem, fr_sem, bs_sem, br_sem, ps_sem, pr_sem, z_sem, cs_sem, cr_sem,
):
    n_atm = n_sec - 1
    ocean_sec = n_sec - 1
    near_sec = n_sec - 2
    relay_sec = near_sec - 1
    half = n_tile // 2
    levels, rows, width = fo.shape[1:]
    ntab = tables.shape[0]
    top, low = PAD, PAD + rows
    sec = lax.axis_index("sec")
    tile = lax.axis_index("tile")
    upper = lax.rem(tile + n_tile - 1, n_tile)
    lower = lax.rem(tile + 1, n_tile)
    is_ocean = sec == ocean_sec
    is_near = sec == near_sec
    is_far = sec < near_sec
    is_relay = sec == relay_sec
    parity = lax.rem(tile, 2)

    def flipped(t):
        return t + 1 - 2 * lax.rem(t, 2)


    def load(number, src, dst):
        return pltpu.make_async_copy(src, dst, in_sem.at[number])

    loads = [
        load(0, fields.at[0], ext.at[:, top:low, :]),
        load(1, coef.at[0], cext.at[:, top:low, :]),
        load(2, ot_in, ot),
        load(3, db_in, db),
        load(4, ti_in, ti),
        load(5, tables, tab),
        load(6, mask_in, mask),
    ]
    for copy in loads:
        copy.start()

    barrier = pltpu.get_barrier_semaphore()

    def greet(semaphore, s, t):
        pl.semaphore_signal(semaphore, inc=1, device_id=(s, t), device_id_type=pl.DeviceIdType.MESH)

    def plane(semaphore):
        def one(k, c):
            z = lax.rem(tile // 8 + k // 4, 4)
            x = lax.rem(tile // 2 + lax.rem(k, 4), 4)
            greet(semaphore, sec, z * 8 + x * 2 + parity)
            return c

        lax.fori_loop(1, n_tile // 2, one, 0)

    for k in range(1, n_sec):
        s = lax.rem(sec + k, n_sec)
        greet(barrier, s, tile)
        greet(barrier, s, flipped(tile))
    greet(barrier, sec, flipped(tile))
    greet(barrier, sec, jnp.where(parity == 0, upper, lower))
    plane(barrier)

    zero = jnp.zeros((PAD, width), F32)
    for l in range(levels):
        ext[l, 0:top, :] = zero
        ext[l, low : low + PAD, :] = zero
    for c in range(2):
        cext[c, 0:top, :] = zero
        cext[c, low : low + PAD, :] = zero
        hsend[c, 8:16, :] = zero
    loads[0].wait()
    for l in range(levels):
        hsend[0, 2 * l : 2 * l + 2, :] = ext[l, top : top + 2, :]
        hsend[1, 2 * l : 2 * l + 2, :] = ext[l, low - 2 : low, :]
    loads[1].wait()
    for c in range(2):
        hsend[0, 8 + c : 9 + c, :] = cext[c, top : top + 1, :]
        hsend[1, 8 + c : 9 + c, :] = cext[c, low - 1 : low, :]

    pl.semaphore_wait(barrier, 2 * n_sec + n_tile // 2 - 1)

    def column_copy(src, dst, number, to):
        return pltpu.make_async_remote_copy(
            src_ref=src,
            dst_ref=dst,
            send_sem=cs_sem.at[number],
            recv_sem=cr_sem.at[number],
            device_id=(to, flipped(tile)),
            device_id_type=pl.DeviceIdType.MESH,
        )

    def mask_copy():
        return column_copy(mask, far_mask, 0, relay_sec)

    def base_copy():
        return column_copy(base, base, 1, relay_sec)

    def flux_copy():
        return column_copy(flux0, flux0, 2, ocean_sec)

    def halo(way, to):
        return pltpu.make_async_remote_copy(
            src_ref=hsend.at[way],
            dst_ref=hrecv.at[1 - way],
            send_sem=hs_sem.at[way],
            recv_sem=hr_sem.at[1 - way],
            device_id=(sec, to),
            device_id_type=pl.DeviceIdType.MESH,
        )

    halos = [halo(0, upper), halo(1, lower)]
    for copy in halos:
        copy.start()

    @pl.when(is_ocean)
    def _():
        loads[6].wait()
        mask_copy().start()

    plane(z_sem)

    loads[2].wait()
    loads[3].wait()
    loads[4].wait()
    loads[5].wait()

    @pl.when(jnp.logical_not(is_ocean))
    def _():
        loads[6].wait()


    lane = iota((8, 128), 1)
    left = lane < 64

    def place(number, a, owner):
        for kk in range(half):
            cols = pl.ds(pl.multiple_of((a * half + kk) * 128, 128), 128)
            x0[kk : kk + 1, :] = ot[0:1, cols].astype(F32)
            x1[kk : kk + 1, :] = ot[1:2, cols].astype(F32)
            d0[kk : kk + 1, :] = db[0:1, cols].astype(F32) + 1.0
            d1[kk : kk + 1, :] = db[1:2, cols].astype(F32) + 1.0
        src, dst = iota((128, 128), 0), iota((128, 128), 1)
        same = (src // 64) == (dst // 64)
        both = same.astype(F32).astype(BF16)
        before = (same & (src < dst)).astype(F32).astype(BF16)
        mine_of = owner.astype(F32)
        mine0 = x0[...] == mine_of
        mine1 = x1[...] == mine_of
        m0 = mine0.astype(F32).astype(BF16)
        m1 = mine1.astype(F32).astype(BF16)
        x0[...] = jnp.where(mine0, matmul(m0, before), -1.0)
        x1[...] = jnp.where(mine1, matmul(m1, before) + matmul(m0, both), -1.0)
        slot = iota((cap, 128), 0).astype(F32)
        parts = []
        for kk in range(half):
            parts.append(
                jnp.where(x0[kk : kk + 1, :] == slot, d0[kk : kk + 1, :], 0.0)
                + jnp.where(x1[kk : kk + 1, :] == slot, d1[kk : kk + 1, :], 0.0)
            )
        named = jnp.concatenate(parts, axis=0).astype(BF16)
        count = half * cap
        lane_c = iota((count, 128), 1)
        left_c = lane_c < 64
        want = (lax.rem(lane_c, 64) + 1).astype(F32)
        hot = (matmul(named, both) == want).astype(F32)
        turned = hot.T
        smat[number, :, 0:count] = turned[0:64].astype(BF16)
        smat[number, :, count : 2 * count] = turned[64:128].astype(BF16)
        other = pltpu.roll(hot, 64, 1)
        rmat[number, 0:count, :] = jnp.where(left_c, hot, other).astype(BF16)
        rmat[number, count : 2 * count, :] = jnp.where(left_c, other, hot).astype(BF16)

    @pl.when(is_ocean)
    def _():
        place(near_sec, near_sec, tile)

    @pl.when(is_relay)
    def _():
        for a in range(n_atm):
            place(a, a, flipped(tile))

    @pl.when(sec < relay_sec)
    def _():
        place(0, 0, flipped(tile))

    @pl.when(jnp.logical_not(is_ocean))
    def _():
        number = sec * n_tile + tile
        cols = pl.ds(pl.multiple_of((number // 2) * 128, 128), 128)

        def pairs(ref):
            r0 = jnp.broadcast_to(ref[0:1, cols].astype(F32), (8, 128))
            r1 = jnp.broadcast_to(ref[1:2, cols].astype(F32), (8, 128))
            even = jnp.where(left, r0, pltpu.roll(r1, 64, 1))
            odd = jnp.where(left, pltpu.roll(r0, 64, 1), r1)
            return jnp.where(parity == 0, even, odd)

        own, entry = pairs(ot), pairs(ti)
        across = jnp.broadcast_to(own[0:1], (128, 128))
        earlier = (across.T == across) & (iota((128, 128), 0) < iota((128, 128), 1))
        rank = jnp.sum(earlier.astype(F32), axis=0, keepdims=True)
        target = own * float(cap) + jnp.broadcast_to(rank, (8, 128))

        def doubled(v):
            turned = pltpu.roll(v, 64, 1)
            return jnp.where(left, v, turned), jnp.where(left, turned, v)

        t0, t1 = doubled(target)
        e0, e1 = doubled(entry)
        slots = iota((n_tile * cap, 128), 0).astype(F32)
        for b in range(ntab // 2):
            here = (lane // 64 + 2 * b).astype(F32)
            v0 = jnp.where(e0 == here, t0, -1.0)
            v1 = jnp.where(e1 == here, t1, -1.0)
            hot = ((slots == v0[0:1]) | (slots == v1[0:1])).astype(F32)
            mmat[:, 128 * b : 128 * (b + 1)] = hot.astype(BF16)
            mtmat[128 * b : 128 * (b + 1), :] = hot.T.astype(BF16)
        for t in range(ntab):
            hi, lo = split(tab[t])
            thi[t] = hi
            tlo[t] = lo

    for copy in halos:
        copy.wait()
    above = jnp.where(tile > 0, hrecv[0], 0.0)
    below = jnp.where(tile < n_tile - 1, hrecv[1], 0.0)
    for l in range(levels):
        ext[l, top - 2 : top, :] = above[2 * l : 2 * l + 2]
        ext[l, low : low + 2, :] = below[2 * l : 2 * l + 2]
    for c in range(2):
        cext[c, top - 1 : top, :] = above[8 + c : 9 + c]
        cext[c, low : low + 1, :] = below[8 + c : 9 + c]

    def substep(u, kappa, speed):
        n = u.shape[0]
        up = pltpu.roll(u, 1, 0)
        down = pltpu.roll(u, n - 1, 0)
        sides = pltpu.roll(u, 1, 1) + pltpu.roll(u, width - 1, 1)
        return u + kappa * (up + down + sides - 4.0 * u) - 0.5 * speed * (down - up)

    def stencil(l):
        kappa, speed = cext[0], cext[1]
        u = substep(ext[l], kappa, speed)
        return substep(u, kappa, speed)[top:low]

    fo[0, 0] = stencil(0)

    def pack(part, row):
        hi, lo = split(row)
        stacked = jnp.concatenate([hi, lo], axis=0)
        for t in range(ntab):
            r = matmul(stacked, thi[t])
            r = r[:rows] + r[rows:] + matmul(hi, tlo[t])
            here = slice(t * rows, (t + 1) * rows)
            pthi[here, :], ptlo[here, :] = split(r)
        out = matmul(mmat[...], pthi[...]) + matmul(mmat[...], ptlo[...])
        send[part] = out.reshape(send.shape[1:])

    def ship(part, to, whole):
        def one(k, c):
            t = lax.rem(tile + k, n_tile)
            o = t if to == ocean_sec else flipped(t)
            pltpu.make_async_remote_copy(
                src_ref=send.at[part, o],
                dst_ref=recv.at[part, sec, parity, tile // 2],
                send_sem=fs_sem.at[part],
                recv_sem=fr_sem.at[part, sec],
                device_id=(to, t),
                device_id_type=pl.DeviceIdType.MESH,
            ).start()
            return c

        if not whole:
            pltpu.make_async_copy(
                send.at[part, flipped(tile)],
                recv.at[part, sec, parity, tile // 2],
                fr_sem.at[part, sec],
            ).start()
        lax.fori_loop(0 if whole else 1, n_tile, one, 0)

    def shipped(part, whole):
        sent = send.at[part, (0 if whole else 1) : n_tile]
        pltpu.make_async_copy(sent, sent, fs_sem.at[part]).wait()

    def spread(number, part, a):
        pltpu.make_async_copy(recv.at[part, a], recv.at[part, a], fr_sem.at[part, a]).wait()
        hi, lo = split(recv[part, a].reshape(n_tile * cap, width))
        return matmul(smat[number], hi) + matmul(smat[number], lo)

    def give_back():
        ocean_tile = flipped(tile)

        def one(k, c):
            i = lax.rem(k, 16)
            j = i // 2
            z = 2 * (k // 16) + lax.rem(i + tile // 8, 2)
            t = 8 * z + 2 * lax.rem(j + tile // 2, 4) + j // 4

            def to(a):
                return pltpu.make_async_remote_copy(
                    src_ref=ret.at[a * n_tile + lax.rem(t, 2) * half + t // 2],
                    dst_ref=arr.at[ocean_tile],
                    send_sem=bs_sem,
                    recv_sem=br_sem,
                    device_id=(a, t),
                    device_id_type=pl.DeviceIdType.MESH,
                )

            @pl.when(t != tile)
            def _():
                to(relay_sec).start()

            for a in range(n_atm):
                if a != relay_sec:
                    to(a).start()
            return c

        lax.fori_loop(0, n_tile, one, 0)
        pltpu.make_async_copy(
            ret.at[relay_sec * n_tile + parity * half + tile // 2], arr.at[ocean_tile], br_sem
        ).start()

    def partial_copy():
        return pltpu.make_async_remote_copy(
            src_ref=mine_sum,
            dst_ref=far_sum.at[sec],
            send_sem=ps_sem,
            recv_sem=pr_sem.at[sec],
            device_id=(ocean_sec, flipped(tile)),
            device_id_type=pl.DeviceIdType.MESH,
        )

    @pl.when(jnp.logical_not(is_ocean))
    def _():
        pack(0, fo[0, 0])
        pl.semaphore_wait(z_sem, n_tile // 2 - 1)

        @pl.when(is_relay)
        def _():
            ship(0, relay_sec, False)

        @pl.when(jnp.logical_not(is_relay))
        def _():
            ship(0, relay_sec, True)

        for l in range(1, levels):
            fo[0, l] = stencil(l)
        pack(1, fo[0, 0] - fo[0, 1])

        @pl.when(is_near)
        def _():
            ship(1, ocean_sec, True)

        for a in range(near_sec):

            @pl.when(sec == a)
            def _():
                ship(1, a, False)


        for t in range(ntab):
            hi, lo = split(tab[t].T)
            tthi[t] = hi
            ttlo[t] = lo

        @pl.when(is_relay)
        def _():
            mask_copy().wait_recv()
            base_copy().wait_recv()
            water = far_mask[...].astype(F32)
            flux = spread(near_sec, 0, near_sec)
            for a in (1, 0):
                flux = flux + spread(a, 0, a)
            flux0[...] = flux
            flux_copy().start()
            hi, lo = split(water * (base[...] + forcing_rate * water * flux))
            both = jnp.concatenate([hi, lo], axis=0)
            for a in range(n_atm):
                ret[a * n_tile : (a + 1) * n_tile] = matmul(rmat[a], both).reshape(n_tile, cap, width)
            give_back()

        @pl.when(is_far)
        def _():
            mine_sum[...] = spread(sec, 1, sec)
            partial_copy().start()

        pltpu.make_async_copy(arr, arr, br_sem).wait()
        uhi, ulo = split(arr[...].reshape(n_tile * cap, width))
        v = matmul(mtmat[...], uhi) + matmul(mtmat[...], ulo)
        total = jnp.zeros((rows, width), F32)
        for t in range(ntab):
            vhi, vlo = split(v[t * rows : (t + 1) * rows])
            r = matmul(jnp.concatenate([vhi, vlo], axis=0), tthi[t])
            total = total + r[:rows] + r[rows:] + matmul(vhi, ttlo[t])
        su[0] = total

        @pl.when(is_relay)
        def _():
            shipped(0, False)
            others = ret.at[1 : n_atm * n_tile]
            pltpu.make_async_copy(others, others, bs_sem).wait()
            flux_copy().wait_send()

        @pl.when(jnp.logical_not(is_relay))
        def _():
            shipped(0, True)

        @pl.when(is_near)
        def _():
            shipped(1, True)

        @pl.when(is_far)
        def _():
            shipped(1, False)
            partial_copy().wait_send()


    @pl.when(is_ocean)
    def _():
        base[...] = fo[0, 0]
        base_copy().start()
        pl.semaphore_wait(z_sem, n_tile // 2 - 1)
        for l in range(1, levels):
            fo[0, l] = stencil(l)
        water = mask[...].astype(F32)
        flux = spread(near_sec, 1, near_sec)
        for a in range(near_sec):
            pltpu.make_async_copy(far_sum.at[a], far_sum.at[a], pr_sem.at[a]).wait()
            flux = flux + far_sum[a]
        fo[0, 1] = fo[0, 1] + forcing_rate * water * flux
        flux_copy().wait_recv()
        first = fo[0, 0] + forcing_rate * water * flux0[...]
        fo[0, 0] = first
        su[0] = water * first
        mask_copy().wait_send()
        base_copy().wait_send()


def store(fields, surface, fields_out, surface_out, sems):
    copies = [
        pltpu.make_async_copy(fields, fields_out, sems.at[0]),
        pltpu.make_async_copy(surface, surface_out, sems.at[1]),
    ]
    for copy in copies:
        copy.start()
    for copy in copies:
        copy.wait()


def local(fields, coefficients, owner_tile, dest_block, table_index, tables, land_mask):
    n_sec = lax.axis_size("sec")
    n_tile = lax.axis_size("tile")
    _, levels, rows, width = fields.shape
    blocks, fan_out = owner_tile.shape
    ntab = tables.shape[0]
    cap = 2 * fan_out * rows // n_tile
    n_atm = n_sec - 1
    half = n_tile // 2
    padded = rows + 2 * PAD
    slots = n_tile * cap
    scratch = [
        pltpu.VMEM((levels, padded, width), F32),
        pltpu.VMEM((2, padded, width), F32),
        pltpu.VMEM((fan_out, blocks), jnp.int32),
        pltpu.VMEM((fan_out, blocks), jnp.int32),
        pltpu.VMEM((fan_out, blocks), jnp.int32),
        pltpu.VMEM((ntab, width, width), F32),
        pltpu.VMEM((rows, width), jnp.int32),
        pltpu.VMEM((2, 16, width), F32),
        pltpu.VMEM((2, 16, width), F32),
        pltpu.VMEM((ntab, width, width), BF16),
        pltpu.VMEM((ntab, width, width), BF16),
        pltpu.VMEM((ntab, width, width), BF16),
        pltpu.VMEM((ntab, width, width), BF16),
        pltpu.VMEM((slots, ntab * rows), BF16),
        pltpu.VMEM((ntab * rows, slots), BF16),
        pltpu.VMEM((ntab * rows, width), BF16),
        pltpu.VMEM((ntab * rows, width), BF16),
        pltpu.VMEM((2, n_tile, cap, width), F32),
        pltpu.VMEM((2, n_atm, 2, half, cap, width), F32),
        pltpu.VMEM((half, 2 * rows), F32),
        pltpu.VMEM((half, 2 * rows), F32),
        pltpu.VMEM((half, 2 * rows), F32),
        pltpu.VMEM((half, 2 * rows), F32),
        pltpu.VMEM((n_atm, rows, slots), BF16),
        pltpu.VMEM((n_atm, slots, 2 * rows), BF16),
        pltpu.VMEM((n_atm * n_tile, cap, width), F32),
        pltpu.VMEM((n_tile, cap, width), F32),
        pltpu.VMEM((rows, width), F32),
        pltpu.VMEM((n_atm - 1, rows, width), F32),
        pltpu.VMEM((rows, width), F32),
        pltpu.VMEM((rows, width), F32),
        pltpu.VMEM((rows, width), jnp.int32),
        pltpu.SemaphoreType.DMA((7,)),
        pltpu.SemaphoreType.DMA((2,)),
        pltpu.SemaphoreType.DMA((2,)),
        pltpu.SemaphoreType.DMA((2,)),
        pltpu.SemaphoreType.DMA((2, n_atm)),
        pltpu.SemaphoreType.DMA,
        pltpu.SemaphoreType.DMA,
        pltpu.SemaphoreType.DMA,
        pltpu.SemaphoreType.DMA((n_atm - 1,)),
        pltpu.SemaphoreType.REGULAR,
        pltpu.SemaphoreType.DMA((3,)),
        pltpu.SemaphoreType.DMA((3,)),
    ]
    operands = (fields, coefficients, owner_tile.T, dest_block.T, table_index.T, tables, land_mask)
    shapes = (
        jax.ShapeDtypeStruct(fields.shape, F32),
        jax.ShapeDtypeStruct((1, rows, width), F32),
    )
    results = pl.pallas_call(
        functools.partial(kernel, n_sec, n_tile, cap),
        out_shape=shapes,
        in_specs=[pl.BlockSpec(memory_space=pltpu.HBM)] * 7,
        out_specs=(
            pl.BlockSpec(memory_space=pltpu.VMEM),
            pl.BlockSpec(memory_space=pltpu.VMEM),
        ),
        scratch_shapes=scratch,
        compiler_params=pltpu.CompilerParams(
            collective_id=0, has_side_effects=True, vmem_limit_bytes=32 * 1024 * 1024
        ),
    )(*(pltpu.with_memory_space_constraint(x, pltpu.HBM) for x in operands))
    return pl.pallas_call(
        store,
        out_shape=shapes,
        in_specs=[pl.BlockSpec(memory_space=pltpu.VMEM)] * 2,
        out_specs=(pl.BlockSpec(memory_space=pl.ANY),) * 2,
        scratch_shapes=[pltpu.SemaphoreType.DMA((2,))],
    )(*(pltpu.with_memory_space_constraint(x, pltpu.VMEM) for x in results))


def solution(mesh):
    placed = (
        P("sec", None, "tile", None),
        P("sec", None, "tile", None),
        P(),
        P(),
        P(),
        P(),
        P("tile", None),
    )
    return jax.shard_map(
        local,
        mesh=mesh,
        in_specs=placed,
        out_specs=(P("sec", None, "tile", None), P("sec", "tile", None)),
        check_vma=False,
    )
```

```python
import functools

import jax
import jax.numpy as jnp
from jax import lax
from jax.experimental import pallas as pl
from jax.experimental.pallas import tpu as pltpu
from jax.sharding import PartitionSpec as P

forcing_rate = 0.5

F32 = jnp.float32
BF16 = jnp.bfloat16
PAD = 8


def matmul(a, b):
    return lax.dot_general(a, b, (((1,), (0,)), ((), ())), preferred_element_type=F32)


def split(x):
    hi = x.astype(BF16)
    return hi, (x - hi.astype(F32)).astype(BF16)


def iota(shape, dim):
    return lax.broadcasted_iota(jnp.int32, shape, dim)


def kernel(
    n_sec, n_tile, cap,
    fields, coef, ot_in, db_in, ti_in, tables, mask_in,
    fo, su,
    ext, cext, ot, db, ti, tab, mask, hsend, hrecv,
    thi, tlo, tthi, ttlo, mmat, mtmat, pthi, ptlo, send, recv,
    x0, x1, d0, d1, smat, rmat, ret, arr, base, flux0, far_mask,
    in_sem, hs_sem, hr_sem, fs_sem, fr_sem, bs_sem, br_sem, o_sem, p_sem, k_sem, b_sem, cs_sem, cr_sem,
):
    n_atm = n_sec - 1
    ocean_sec = n_sec - 1
    near_sec = n_sec - 2
    relay_sec = near_sec - 1
    half = n_tile // 2
    levels, rows, width = fo.shape[1:]
    ntab = tables.shape[0]
    top, low = PAD, PAD + rows
    sec = lax.axis_index("sec")
    tile = lax.axis_index("tile")
    upper = lax.rem(tile + n_tile - 1, n_tile)
    lower = lax.rem(tile + 1, n_tile)
    is_ocean = sec == ocean_sec
    is_near = sec == near_sec
    is_relay = sec == relay_sec
    parity = lax.rem(tile, 2)

    def flipped(t):
        return t + 1 - 2 * lax.rem(t, 2)


    def load(number, src, dst):
        return pltpu.make_async_copy(src, dst, in_sem.at[number])

    loads = [
        load(0, fields.at[0], ext.at[:, top:low, :]),
        load(1, coef.at[0], cext.at[:, top:low, :]),
        load(2, ot_in, ot),
        load(3, db_in, db),
        load(4, ti_in, ti),
        load(5, tables, tab),
        load(6, mask_in, mask),
    ]
    for copy in loads:
        copy.start()

    barrier = pltpu.get_barrier_semaphore()
    has_upper, has_lower = tile > 0, tile < n_tile - 1
    neighbours = has_upper.astype(jnp.int32) + has_lower.astype(jnp.int32)

    def greet(semaphore, s, t):
        pl.semaphore_signal(semaphore, inc=1, device_id=(s, t), device_id_type=pl.DeviceIdType.MESH)

    @pl.when(jnp.logical_not(has_upper))
    def _():
        hrecv[0] = jnp.zeros_like(hrecv[0])

    @pl.when(jnp.logical_not(has_lower))
    def _():
        hrecv[1] = jnp.zeros_like(hrecv[1])

    @pl.when(has_upper)
    def _():
        greet(barrier, sec, upper)

    @pl.when(has_lower)
    def _():
        greet(barrier, sec, lower)

    @pl.when(is_relay | is_ocean)
    def _():
        def one(k, c):
            z = lax.rem(tile // 8 + k // 4, 4)
            x = lax.rem(tile // 2 + lax.rem(k, 4), 4)
            greet(barrier, sec, z * 8 + x * 2 + parity)
            return c

        lax.fori_loop(1, half, one, 0)

    @pl.when(is_relay)
    def _():
        greet(barrier, ocean_sec, flipped(tile))

    @pl.when(sec == 0)
    def _():
        greet(barrier, relay_sec, tile)

    @pl.when(is_near)
    def _():
        greet(barrier, ocean_sec, tile)
        greet(barrier, relay_sec, flipped(tile))

    zero = jnp.zeros((PAD, width), F32)
    for l in range(levels):
        ext[l, 0:top, :] = zero
        ext[l, low : low + PAD, :] = zero
    for c in range(2):
        cext[c, 0:top, :] = zero
        cext[c, low : low + PAD, :] = zero
        hsend[c, 8:16, :] = zero

    loads[0].wait()
    for l in range(levels):
        hsend[0, 2 * l : 2 * l + 2, :] = ext[l, top : top + 2, :]
        hsend[1, 2 * l : 2 * l + 2, :] = ext[l, low - 2 : low, :]
    loads[1].wait()
    for c in range(2):
        hsend[0, 8 + c : 9 + c, :] = cext[c, top : top + 1, :]
        hsend[1, 8 + c : 9 + c, :] = cext[c, low - 1 : low, :]

    @pl.when(is_relay | is_ocean)
    def _():
        pl.semaphore_wait(barrier, neighbours + half + 1)

    @pl.when(jnp.logical_not(is_relay | is_ocean))
    def _():
        pl.semaphore_wait(barrier, neighbours)

    def column_copy(src, dst, number, to):
        return pltpu.make_async_remote_copy(
            src_ref=src,
            dst_ref=dst,
            send_sem=cs_sem.at[number],
            recv_sem=cr_sem.at[number],
            device_id=(to, flipped(tile)),
            device_id_type=pl.DeviceIdType.MESH,
        )

    def mask_copy():
        return column_copy(mask, far_mask, 0, relay_sec)

    def base_copy():
        return column_copy(base, base, 1, relay_sec)

    def flux_copy():
        return column_copy(flux0, flux0, 2, ocean_sec)

    def halo(way, to):
        return pltpu.make_async_remote_copy(
            src_ref=hsend.at[way],
            dst_ref=hrecv.at[1 - way],
            send_sem=hs_sem.at[way],
            recv_sem=hr_sem.at[1 - way],
            device_id=(sec, to),
            device_id_type=pl.DeviceIdType.MESH,
        )

    halos = [halo(0, upper), halo(1, lower)]

    @pl.when(has_upper)
    def _():
        halos[0].start()

    @pl.when(has_lower)
    def _():
        halos[1].start()

    @pl.when(is_ocean)
    def _():
        loads[6].wait()
        mask_copy().start()

    @pl.when(is_relay | is_ocean)
    def _():
        greet(p_sem, sec, flipped(tile))

    loads[2].wait()
    loads[3].wait()
    loads[4].wait()
    loads[5].wait()

    @pl.when(jnp.logical_not(is_ocean))
    def _():
        loads[6].wait()


    lane = iota((8, 128), 1)
    left = lane < 64

    def place(number, a, owner):
        for kk in range(half):
            cols = pl.ds(pl.multiple_of((a * half + kk) * 128, 128), 128)
            x0[kk : kk + 1, :] = ot[0:1, cols].astype(F32)
            x1[kk : kk + 1, :] = ot[1:2, cols].astype(F32)
            d0[kk : kk + 1, :] = db[0:1, cols].astype(F32) + 1.0
            d1[kk : kk + 1, :] = db[1:2, cols].astype(F32) + 1.0
        src, dst = iota((128, 128), 0), iota((128, 128), 1)
        same = (src // 64) == (dst // 64)
        both = same.astype(F32).astype(BF16)
        before = (same & (src < dst)).astype(F32).astype(BF16)
        mine_of = owner.astype(F32)
        mine0 = x0[...] == mine_of
        mine1 = x1[...] == mine_of
        m0 = mine0.astype(F32).astype(BF16)
        m1 = mine1.astype(F32).astype(BF16)
        x0[...] = jnp.where(mine0, matmul(m0, before), -1.0)
        x1[...] = jnp.where(mine1, matmul(m1, before) + matmul(m0, both), -1.0)
        slot = iota((cap, 128), 0).astype(F32)
        parts = []
        for kk in range(half):
            parts.append(
                jnp.where(x0[kk : kk + 1, :] == slot, d0[kk : kk + 1, :], 0.0)
                + jnp.where(x1[kk : kk + 1, :] == slot, d1[kk : kk + 1, :], 0.0)
            )
        named = jnp.concatenate(parts, axis=0).astype(BF16)
        count = half * cap
        lane_c = iota((count, 128), 1)
        left_c = lane_c < 64
        want = (lax.rem(lane_c, 64) + 1).astype(F32)
        hot = (matmul(named, both) == want).astype(F32)
        turned = hot.T
        smat[number, :, 0:count] = turned[0:64].astype(BF16)
        smat[number, :, count : 2 * count] = turned[64:128].astype(BF16)
        other = pltpu.roll(hot, 64, 1)
        rmat[number, 0:count, :] = jnp.where(left_c, hot, other).astype(BF16)
        rmat[number, count : 2 * count, :] = jnp.where(left_c, other, hot).astype(BF16)

    @pl.when(is_ocean)
    def _():
        for a in range(n_atm):
            place(a, a, tile)

    @pl.when(is_relay)
    def _():
        for a in range(n_atm):
            place(a, a, flipped(tile))

    @pl.when(jnp.logical_not(is_ocean))
    def _():
        number = sec * n_tile + tile
        cols = pl.ds(pl.multiple_of((number // 2) * 128, 128), 128)

        def pairs(ref):
            r0 = jnp.broadcast_to(ref[0:1, cols].astype(F32), (8, 128))
            r1 = jnp.broadcast_to(ref[1:2, cols].astype(F32), (8, 128))
            even = jnp.where(left, r0, pltpu.roll(r1, 64, 1))
            odd = jnp.where(left, pltpu.roll(r0, 64, 1), r1)
            return jnp.where(parity == 0, even, odd)

        own, entry = pairs(ot), pairs(ti)
        across = jnp.broadcast_to(own[0:1], (128, 128))
        earlier = (across.T == across) & (iota((128, 128), 0) < iota((128, 128), 1))
        rank = jnp.sum(earlier.astype(F32), axis=0, keepdims=True)
        target = own * float(cap) + jnp.broadcast_to(rank, (8, 128))

        def doubled(v):
            turned = pltpu.roll(v, 64, 1)
            return jnp.where(left, v, turned), jnp.where(left, turned, v)

        t0, t1 = doubled(target)
        e0, e1 = doubled(entry)
        slots = iota((n_tile * cap, 128), 0).astype(F32)
        for b in range(ntab // 2):
            here = (lane // 64 + 2 * b).astype(F32)
            v0 = jnp.where(e0 == here, t0, -1.0)
            v1 = jnp.where(e1 == here, t1, -1.0)
            hot = ((slots == v0[0:1]) | (slots == v1[0:1])).astype(F32)
            mmat[:, 128 * b : 128 * (b + 1)] = hot.astype(BF16)
            mtmat[128 * b : 128 * (b + 1), :] = hot.T.astype(BF16)
        for t in range(ntab):
            hi, lo = split(tab[t])
            thi[t] = hi
            tlo[t] = lo

    @pl.when(is_relay)
    def _():
        pl.semaphore_wait(p_sem, 1)
        greet(k_sem, 0, tile)
        greet(k_sem, near_sec, flipped(tile))

    @pl.when(is_ocean)
    def _():
        pl.semaphore_wait(p_sem, 1)
        greet(o_sem, near_sec, tile)
        greet(b_sem, relay_sec, flipped(tile))

    @pl.when(has_upper)
    def _():
        halos[0].wait_send()
        halos[1].wait_recv()

    @pl.when(has_lower)
    def _():
        halos[1].wait_send()
        halos[0].wait_recv()

    above, below = hrecv[0], hrecv[1]
    for l in range(levels):
        ext[l, top - 2 : top, :] = above[2 * l : 2 * l + 2]
        ext[l, low : low + 2, :] = below[2 * l : 2 * l + 2]
    for c in range(2):
        cext[c, top - 1 : top, :] = above[8 + c : 9 + c]
        cext[c, low : low + 1, :] = below[8 + c : 9 + c]

    def substep(u, kappa, speed):
        n = u.shape[0]
        up = pltpu.roll(u, 1, 0)
        down = pltpu.roll(u, n - 1, 0)
        sides = pltpu.roll(u, 1, 1) + pltpu.roll(u, width - 1, 1)
        return u + kappa * (up + down + sides - 4.0 * u) - 0.5 * speed * (down - up)

    def stencil(l):
        kappa, speed = cext[0], cext[1]
        u = substep(ext[l], kappa, speed)
        return substep(u, kappa, speed)[top:low]

    fo[0, 0] = stencil(0)

    def pack(part, row):
        hi, lo = split(row)
        stacked = jnp.concatenate([hi, lo], axis=0)
        for t in range(ntab):
            r = matmul(stacked, thi[t])
            r = r[:rows] + r[rows:] + matmul(hi, tlo[t])
            here = slice(t * rows, (t + 1) * rows)
            pthi[here, :], ptlo[here, :] = split(r)
        out = matmul(mmat[...], pthi[...]) + matmul(mmat[...], ptlo[...])
        send[part] = out.reshape(send.shape[1:])

    def ship(part, to):
        def one(k, c):
            t = lax.rem(tile + k, n_tile)
            pltpu.make_async_remote_copy(
                src_ref=send.at[part, t if to == ocean_sec else flipped(t)],
                dst_ref=recv.at[part, sec, parity, tile // 2],
                send_sem=fs_sem.at[part],
                recv_sem=fr_sem.at[part, sec],
                device_id=(to, t),
                device_id_type=pl.DeviceIdType.MESH,
            ).start()
            return c

        if to == ocean_sec:
            lax.fori_loop(0, n_tile, one, 0)
            return

        @pl.when(is_relay)
        def _():
            pltpu.make_async_copy(
                send.at[part, flipped(tile)],
                recv.at[part, sec, parity, tile // 2],
                fr_sem.at[part, sec],
            ).start()
            lax.fori_loop(1, n_tile, one, 0)

        @pl.when(jnp.logical_not(is_relay))
        def _():
            lax.fori_loop(0, n_tile, one, 0)

    def shipped(part, kept):
        sent = send.at[part, kept:n_tile]
        pltpu.make_async_copy(sent, sent, fs_sem.at[part]).wait()

    def gather(part, sections):
        flux = jnp.zeros((rows, width), F32)
        for a in sections:
            pltpu.make_async_copy(recv.at[part, a], recv.at[part, a], fr_sem.at[part, a]).wait()
            hi, lo = split(recv[part, a].reshape(n_tile * cap, width))
            flux = flux + matmul(smat[a], hi) + matmul(smat[a], lo)
        return flux

    def give_back():
        ocean_tile = flipped(tile)

        def one(k, c):
            i = lax.rem(k, 16)
            z = 2 * (k // 16) + lax.rem(i // 4 + tile // 8, 2)
            t = 8 * z + 2 * lax.rem(i + tile // 2, 4) + i // 8

            z2 = 2 * (k // 16) + lax.rem(i // 8 + tile // 8, 2)
            t2 = 8 * z2 + 2 * lax.rem(i // 2 + tile // 2, 4) + lax.rem(i, 2)

            def to(a, t):
                return pltpu.make_async_remote_copy(
                    src_ref=ret.at[a * n_tile + lax.rem(t, 2) * half + t // 2],
                    dst_ref=arr.at[ocean_tile],
                    send_sem=bs_sem,
                    recv_sem=br_sem,
                    device_id=(a, t),
                    device_id_type=pl.DeviceIdType.MESH,
                )

            @pl.when(t != tile)
            def _():
                to(relay_sec, t).start()

            to(0, t).start()
            to(near_sec, t2).start()
            return c

        lax.fori_loop(0, n_tile, one, 0)
        pltpu.make_async_copy(
            ret.at[relay_sec * n_tile + parity * half + tile // 2], arr.at[ocean_tile], br_sem
        ).start()

    @pl.when(jnp.logical_not(is_ocean))
    def _():
        pack(0, fo[0, 0])

        @pl.when(jnp.logical_not(is_relay))
        def _():
            pl.semaphore_wait(k_sem, 1)

        ship(0, relay_sec)
        for l in range(1, levels):
            fo[0, l] = stencil(l)
        pack(1, fo[0, 0] - fo[0, 1])


        @pl.when(jnp.logical_not(is_relay))
        def _():
            shipped(0, 0)

        @pl.when(is_relay)
        def _():
            shipped(0, 1)

        @pl.when(is_near)
        def _():
            pl.semaphore_wait(o_sem, 1)
            ship(1, ocean_sec)

        @pl.when(sec < near_sec)
        def _():
            pl.semaphore_wait(b_sem, 1)

            @pl.when(is_relay)
            def _():
                greet(b_sem, 0, tile)

            ship(1, ocean_sec)

        for t in range(ntab):
            hi, lo = split(tab[t].T)
            tthi[t] = hi
            ttlo[t] = lo

        @pl.when(is_relay)
        def _():
            mask_copy().wait_recv()
            base_copy().wait_recv()
            water = far_mask[...].astype(F32)
            flux = gather(0, (1, 0, 2))
            flux0[...] = flux
            flux_copy().start()
            hi, lo = split(water * (base[...] + forcing_rate * water * flux))
            both = jnp.concatenate([hi, lo], axis=0)
            for a in range(n_atm):
                ret[a * n_tile : (a + 1) * n_tile] = matmul(rmat[a], both).reshape(n_tile, cap, width)
            give_back()

        pltpu.make_async_copy(arr, arr, br_sem).wait()
        uhi, ulo = split(arr[...].reshape(n_tile * cap, width))
        v = matmul(mtmat[...], uhi) + matmul(mtmat[...], ulo)
        total = jnp.zeros((rows, width), F32)
        for t in range(ntab):
            vhi, vlo = split(v[t * rows : (t + 1) * rows])
            r = matmul(jnp.concatenate([vhi, vlo], axis=0), tthi[t])
            total = total + r[:rows] + r[rows:] + matmul(vhi, ttlo[t])
        su[0] = total

        shipped(1, 0)

        @pl.when(is_relay)
        def _():
            others = ret.at[1 : n_atm * n_tile]
            pltpu.make_async_copy(others, others, bs_sem).wait()
            flux_copy().wait_send()

    @pl.when(is_ocean)
    def _():
        base[...] = fo[0, 0]
        base_copy().start()
        for l in range(1, levels):
            fo[0, l] = stencil(l)
        water = mask[...].astype(F32)
        flux_copy().wait_recv()
        first = fo[0, 0] + forcing_rate * water * flux0[...]
        fo[0, 0] = first
        su[0] = water * first
        fo[0, 1] = fo[0, 1] + forcing_rate * water * gather(1, (2, 1, 0))
        mask_copy().wait_send()
        base_copy().wait_send()


def store(fields, surface, fields_out, surface_out, sems):
    copies = [
        pltpu.make_async_copy(fields, fields_out, sems.at[0]),
        pltpu.make_async_copy(surface, surface_out, sems.at[1]),
    ]
    for copy in copies:
        copy.start()
    for copy in copies:
        copy.wait()


def local(fields, coefficients, owner_tile, dest_block, table_index, tables, land_mask):
    n_sec = lax.axis_size("sec")
    n_tile = lax.axis_size("tile")
    _, levels, rows, width = fields.shape
    blocks, fan_out = owner_tile.shape
    ntab = tables.shape[0]
    cap = 2 * fan_out * rows // n_tile
    n_atm = n_sec - 1
    half = n_tile // 2
    padded = rows + 2 * PAD
    slots = n_tile * cap
    scratch = [
        pltpu.VMEM((levels, padded, width), F32),
        pltpu.VMEM((2, padded, width), F32),
        pltpu.VMEM((fan_out, blocks), jnp.int32),
        pltpu.VMEM((fan_out, blocks), jnp.int32),
        pltpu.VMEM((fan_out, blocks), jnp.int32),
        pltpu.VMEM((ntab, width, width), F32),
        pltpu.VMEM((rows, width), jnp.int32),
        pltpu.VMEM((2, 16, width), F32),
        pltpu.VMEM((2, 16, width), F32),
        pltpu.VMEM((ntab, width, width), BF16),
        pltpu.VMEM((ntab, width, width), BF16),
        pltpu.VMEM((ntab, width, width), BF16),
        pltpu.VMEM((ntab, width, width), BF16),
        pltpu.VMEM((slots, ntab * rows), BF16),
        pltpu.VMEM((ntab * rows, slots), BF16),
        pltpu.VMEM((ntab * rows, width), BF16),
        pltpu.VMEM((ntab * rows, width), BF16),
        pltpu.VMEM((2, n_tile, cap, width), F32),
        pltpu.VMEM((2, n_atm, 2, half, cap, width), F32),
        pltpu.VMEM((half, 2 * rows), F32),
        pltpu.VMEM((half, 2 * rows), F32),
        pltpu.VMEM((half, 2 * rows), F32),
        pltpu.VMEM((half, 2 * rows), F32),
        pltpu.VMEM((n_atm, rows, slots), BF16),
        pltpu.VMEM((n_atm, slots, 2 * rows), BF16),
        pltpu.VMEM((n_atm * n_tile, cap, width), F32),
        pltpu.VMEM((n_tile, cap, width), F32),
        pltpu.VMEM((rows, width), F32),
        pltpu.VMEM((rows, width), F32),
        pltpu.VMEM((rows, width), jnp.int32),
        pltpu.SemaphoreType.DMA((7,)),
        pltpu.SemaphoreType.DMA((2,)),
        pltpu.SemaphoreType.DMA((2,)),
        pltpu.SemaphoreType.DMA((2,)),
        pltpu.SemaphoreType.DMA((2, n_atm)),
        pltpu.SemaphoreType.DMA,
        pltpu.SemaphoreType.DMA,
        pltpu.SemaphoreType.REGULAR,
        pltpu.SemaphoreType.REGULAR,
        pltpu.SemaphoreType.REGULAR,
        pltpu.SemaphoreType.REGULAR,
        pltpu.SemaphoreType.DMA((3,)),
        pltpu.SemaphoreType.DMA((3,)),
    ]
    operands = (fields, coefficients, owner_tile.T, dest_block.T, table_index.T, tables, land_mask)
    shapes = (
        jax.ShapeDtypeStruct(fields.shape, F32),
        jax.ShapeDtypeStruct((1, rows, width), F32),
    )
    results = pl.pallas_call(
        functools.partial(kernel, n_sec, n_tile, cap),
        out_shape=shapes,
        in_specs=[pl.BlockSpec(memory_space=pltpu.HBM)] * 7,
        out_specs=(
            pl.BlockSpec(memory_space=pltpu.VMEM),
            pl.BlockSpec(memory_space=pltpu.VMEM),
        ),
        scratch_shapes=scratch,
        compiler_params=pltpu.CompilerParams(
            collective_id=0, has_side_effects=True, vmem_limit_bytes=32 * 1024 * 1024
        ),
    )(*(pltpu.with_memory_space_constraint(x, pltpu.HBM) for x in operands))
    return pl.pallas_call(
        store,
        out_shape=shapes,
        in_specs=[pl.BlockSpec(memory_space=pltpu.VMEM)] * 2,
        out_specs=(pl.BlockSpec(memory_space=pl.ANY),) * 2,
        scratch_shapes=[pltpu.SemaphoreType.DMA((2,))],
    )(*(pltpu.with_memory_space_constraint(x, pltpu.VMEM) for x in results))


def solution(mesh):
    placed = (
        P("sec", None, "tile", None),
        P("sec", None, "tile", None),
        P(),
        P(),
        P(),
        P(),
        P("tile", None),
    )
    return jax.shard_map(
        local,
        mesh=mesh,
        in_specs=placed,
        out_specs=(P("sec", None, "tile", None), P("sec", "tile", None)),
        check_vma=False,
    )
```

```python
import functools

import jax
import jax.numpy as jnp
from jax import lax
from jax.experimental import pallas as pl
from jax.experimental.pallas import tpu as pltpu
from jax.sharding import PartitionSpec as P

forcing_rate = 0.5

F32 = jnp.float32
BF16 = jnp.bfloat16
PAD = 8
PLANES = 4


def matmul(a, b):
    return lax.dot_general(a, b, (((1,), (0,)), ((), ())), preferred_element_type=F32)


def split(x):
    hi = x.astype(BF16)
    return hi, (x - hi.astype(F32)).astype(BF16)


def iota(shape, dim):
    return lax.broadcasted_iota(jnp.int32, shape, dim)


def kernel(
    n_sec, n_tile, cap,
    fields, coef, ot_in, db_in, ti_in, tables, mask_in,
    fo, su,
    ext, cext, ot, db, ti, tab, mask, hsend, hrecv,
    thi, tlo, tthi, ttlo, mmat, mtmat, pthi, ptlo, send, recv,
    x0, x1, d0, d1, hots, smat, rmat, ret, arr, base, flux0, far_mask,
    in_sem, hs_sem, hr_sem, fs_sem, fr_sem, bs_sem, br_sem, o_sem, p_sem, k_sem, g_sem, h_sem, cs_sem, cr_sem,
):
    n_atm = n_sec - 1
    ocean_sec = n_sec - 1
    near_sec = n_sec - 2
    relay_sec = near_sec - 1
    half = n_tile // 2
    in_plane = n_tile // PLANES // 2
    filled = n_atm * in_plane
    levels, rows, width = fo.shape[1:]
    ntab = tables.shape[0]
    top, low = PAD, PAD + rows
    sec = lax.axis_index("sec")
    tile = lax.axis_index("tile")
    upper = lax.rem(tile + n_tile - 1, n_tile)
    lower = lax.rem(tile + 1, n_tile)
    is_ocean = sec == ocean_sec
    is_near = sec == near_sec
    is_relay = sec == relay_sec
    parity = lax.rem(tile, 2)

    def flipped(t):
        return t + 1 - 2 * lax.rem(t, 2)


    def load(number, src, dst):
        return pltpu.make_async_copy(src, dst, in_sem.at[number])

    loads = [
        load(0, fields.at[0], ext.at[:, top:low, :]),
        load(1, coef.at[0], cext.at[:, top:low, :]),
        load(2, ot_in, ot),
        load(3, db_in, db),
        load(4, ti_in, ti),
        load(5, tables, tab),
        load(6, mask_in, mask),
    ]
    for copy in loads:
        copy.start()

    barrier = pltpu.get_barrier_semaphore()
    has_upper, has_lower = tile > 0, tile < n_tile - 1
    neighbours = has_upper.astype(jnp.int32) + has_lower.astype(jnp.int32)

    def greet(semaphore, s, t):
        pl.semaphore_signal(semaphore, inc=1, device_id=(s, t), device_id_type=pl.DeviceIdType.MESH)

    @pl.when(jnp.logical_not(has_upper))
    def _():
        hrecv[0] = jnp.zeros_like(hrecv[0])

    @pl.when(jnp.logical_not(has_lower))
    def _():
        hrecv[1] = jnp.zeros_like(hrecv[1])

    def clear(part):
        for z in range(PLANES):
            for h in range(2):
                recv[part, z, h, filled:] = jnp.zeros_like(recv[part, z, h, filled:])

    @pl.when(is_relay)
    def _():
        clear(0)

    @pl.when(is_ocean)
    def _():
        clear(1)

    @pl.when(has_upper)
    def _():
        greet(barrier, sec, upper)

    @pl.when(has_lower)
    def _():
        greet(barrier, sec, lower)

    def greet_plane(semaphore):
        def one(k, c):
            z = lax.rem(tile // 8 + k // 4, 4)
            x = lax.rem(tile // 2 + lax.rem(k, 4), 4)
            greet(semaphore, sec, z * 8 + x * 2 + parity)
            return c

        lax.fori_loop(1, half, one, 0)

    @pl.when(is_relay)
    def _():
        greet_plane(barrier)
        greet(barrier, ocean_sec, flipped(tile))

    @pl.when(sec == 0)
    def _():
        greet(barrier, relay_sec, tile)

    @pl.when(is_near | is_ocean)
    def _():
        greet(barrier, relay_sec, flipped(tile))

    zero = jnp.zeros((PAD, width), F32)
    for l in range(levels):
        ext[l, 0:top, :] = zero
        ext[l, low : low + PAD, :] = zero
    for c in range(2):
        cext[c, 0:top, :] = zero
        cext[c, low : low + PAD, :] = zero
        hsend[c, 8:16, :] = zero

    loads[0].wait()
    for l in range(levels):
        hsend[0, 2 * l : 2 * l + 2, :] = ext[l, top : top + 2, :]
        hsend[1, 2 * l : 2 * l + 2, :] = ext[l, low - 2 : low, :]
    loads[1].wait()
    for c in range(2):
        hsend[0, 8 + c : 9 + c, :] = cext[c, top : top + 1, :]
        hsend[1, 8 + c : 9 + c, :] = cext[c, low - 1 : low, :]

    @pl.when(is_relay)
    def _():
        pl.semaphore_wait(barrier, neighbours + half + 2)

    @pl.when(is_ocean)
    def _():
        pl.semaphore_wait(barrier, neighbours + 1)

    @pl.when(jnp.logical_not(is_relay | is_ocean))
    def _():
        pl.semaphore_wait(barrier, neighbours)

    def column_copy(src, dst, number, to):
        return pltpu.make_async_remote_copy(
            src_ref=src,
            dst_ref=dst,
            send_sem=cs_sem.at[number],
            recv_sem=cr_sem.at[number],
            device_id=(to, flipped(tile)),
            device_id_type=pl.DeviceIdType.MESH,
        )

    def mask_copy():
        return column_copy(mask, far_mask, 0, relay_sec)

    def base_copy():
        return column_copy(base, base, 1, relay_sec)

    def flux_copy():
        return column_copy(flux0, flux0, 2, ocean_sec)

    def halo(way, to):
        return pltpu.make_async_remote_copy(
            src_ref=hsend.at[way],
            dst_ref=hrecv.at[1 - way],
            send_sem=hs_sem.at[way],
            recv_sem=hr_sem.at[1 - way],
            device_id=(sec, to),
            device_id_type=pl.DeviceIdType.MESH,
        )

    halos = [halo(0, upper), halo(1, lower)]

    @pl.when(has_upper)
    def _():
        halos[0].start()

    @pl.when(has_lower)
    def _():
        halos[1].start()

    @pl.when(is_ocean)
    def _():
        loads[6].wait()
        mask_copy().start()

    @pl.when(is_relay)
    def _():
        greet(p_sem, sec, flipped(tile))
        greet_plane(g_sem)

    loads[2].wait()
    loads[3].wait()
    loads[4].wait()
    loads[5].wait()

    @pl.when(jnp.logical_not(is_ocean))
    def _():
        loads[6].wait()


    lane = iota((8, 128), 1)
    left = lane < 64

    def place(number, a, owner):
        for kk in range(half):
            cols = pl.ds(pl.multiple_of((a * half + kk) * 128, 128), 128)
            x0[kk : kk + 1, :] = ot[0:1, cols].astype(F32)
            x1[kk : kk + 1, :] = ot[1:2, cols].astype(F32)
            d0[kk : kk + 1, :] = db[0:1, cols].astype(F32) + 1.0
            d1[kk : kk + 1, :] = db[1:2, cols].astype(F32) + 1.0
        src, dst = iota((128, 128), 0), iota((128, 128), 1)
        same = (src // 64) == (dst // 64)
        both = same.astype(F32).astype(BF16)
        before = (same & (src < dst)).astype(F32).astype(BF16)
        mine_of = owner.astype(F32)
        mine0 = x0[...] == mine_of
        mine1 = x1[...] == mine_of
        m0 = mine0.astype(F32).astype(BF16)
        m1 = mine1.astype(F32).astype(BF16)
        x0[...] = jnp.where(mine0, matmul(m0, before), -1.0)
        x1[...] = jnp.where(mine1, matmul(m1, before) + matmul(m0, both), -1.0)
        slot = iota((cap, 128), 0).astype(F32)
        parts = []
        for kk in range(half):
            parts.append(
                jnp.where(x0[kk : kk + 1, :] == slot, d0[kk : kk + 1, :], 0.0)
                + jnp.where(x1[kk : kk + 1, :] == slot, d1[kk : kk + 1, :], 0.0)
            )
        named = jnp.concatenate(parts, axis=0).astype(BF16)
        count = half * cap
        lane_c = iota((count, 128), 1)
        left_c = lane_c < 64
        want = (lax.rem(lane_c, 64) + 1).astype(F32)
        hot = (matmul(named, both) == want).astype(F32)
        width_z = in_plane * cap
        for z in range(PLANES):
            hots[z, a * width_z : (a + 1) * width_z, :] = hot[z * width_z : (z + 1) * width_z]
        other = pltpu.roll(hot, 64, 1)
        rmat[number, 0:count, :] = jnp.where(left_c, hot, other).astype(BF16)
        rmat[number, count : 2 * count, :] = jnp.where(left_c, other, hot).astype(BF16)

    def place_all(owner):
        hots[:, filled * cap :, :] = jnp.zeros_like(hots[:, filled * cap :, :])
        for a in range(n_atm):
            place(a, a, owner)
        for z in range(PLANES):
            turned = hots[z].T
            smat[z, :, 0:128] = turned[0:64].astype(BF16)
            smat[z, :, 128:256] = turned[64:128].astype(BF16)

    @pl.when(jnp.logical_not(is_ocean))
    def _():
        number = sec * n_tile + tile
        cols = pl.ds(pl.multiple_of((number // 2) * 128, 128), 128)

        def pairs(ref):
            r0 = jnp.broadcast_to(ref[0:1, cols].astype(F32), (8, 128))
            r1 = jnp.broadcast_to(ref[1:2, cols].astype(F32), (8, 128))
            even = jnp.where(left, r0, pltpu.roll(r1, 64, 1))
            odd = jnp.where(left, pltpu.roll(r0, 64, 1), r1)
            return jnp.where(parity == 0, even, odd)

        own, entry = pairs(ot), pairs(ti)
        across = jnp.broadcast_to(own[0:1], (128, 128))
        earlier = (across.T == across) & (iota((128, 128), 0) < iota((128, 128), 1))
        rank = jnp.sum(earlier.astype(F32), axis=0, keepdims=True)
        target = own * float(cap) + jnp.broadcast_to(rank, (8, 128))

        def doubled(v):
            turned = pltpu.roll(v, 64, 1)
            return jnp.where(left, v, turned), jnp.where(left, turned, v)

        t0, t1 = doubled(target)
        e0, e1 = doubled(entry)
        slots = iota((n_tile * cap, 128), 0).astype(F32)
        for b in range(ntab // 2):
            here = (lane // 64 + 2 * b).astype(F32)
            v0 = jnp.where(e0 == here, t0, -1.0)
            v1 = jnp.where(e1 == here, t1, -1.0)
            hot = ((slots == v0[0:1]) | (slots == v1[0:1])).astype(F32)
            mmat[:, 128 * b : 128 * (b + 1)] = hot.astype(BF16)
            mtmat[128 * b : 128 * (b + 1), :] = hot.T.astype(BF16)
        for t in range(ntab):
            hi, lo = split(tab[t])
            thi[t] = hi
            tlo[t] = lo

    @pl.when(is_relay)
    def _():
        pl.semaphore_wait(p_sem, 1)
        greet(k_sem, 0, tile)
        greet(k_sem, near_sec, flipped(tile))

    @pl.when(is_relay)
    def _():
        pl.semaphore_wait(g_sem, half - 1)
        greet(h_sem, sec, flipped(tile))

    @pl.when(has_upper)
    def _():
        halos[0].wait_send()
        halos[1].wait_recv()

    @pl.when(has_lower)
    def _():
        halos[1].wait_send()
        halos[0].wait_recv()

    above, below = hrecv[0], hrecv[1]
    for l in range(levels):
        ext[l, top - 2 : top, :] = above[2 * l : 2 * l + 2]
        ext[l, low : low + 2, :] = below[2 * l : 2 * l + 2]
    for c in range(2):
        cext[c, top - 1 : top, :] = above[8 + c : 9 + c]
        cext[c, low : low + 1, :] = below[8 + c : 9 + c]

    def substep(u, kappa, speed):
        n = u.shape[0]
        up = pltpu.roll(u, 1, 0)
        down = pltpu.roll(u, n - 1, 0)
        sides = pltpu.roll(u, 1, 1) + pltpu.roll(u, width - 1, 1)
        return u + kappa * (up + down + sides - 4.0 * u) - 0.5 * speed * (down - up)

    def stencil(l):
        kappa, speed = cext[0], cext[1]
        u = substep(ext[l], kappa, speed)
        return substep(u, kappa, speed)[top:low]

    fo[0, 0] = stencil(0)

    def pack(part, row):
        hi, lo = split(row)
        stacked = jnp.concatenate([hi, lo], axis=0)
        for t in range(ntab):
            r = matmul(stacked, thi[t])
            r = r[:rows] + r[rows:] + matmul(hi, tlo[t])
            here = slice(t * rows, (t + 1) * rows)
            pthi[here, :], ptlo[here, :] = split(r)
        out = matmul(mmat[...], pthi[...]) + matmul(mmat[...], ptlo[...])
        send[part] = out.reshape(send.shape[1:])

    def ship(part, to):
        def one(k, c):
            t = lax.rem(tile + k, n_tile)
            pltpu.make_async_remote_copy(
                src_ref=send.at[part, t if to == ocean_sec else flipped(t)],
                dst_ref=recv.at[part, tile // 8, parity, sec * in_plane + lax.rem(tile // 2, in_plane)],
                send_sem=fs_sem.at[part],
                recv_sem=fr_sem.at[part, tile // 8],
                device_id=(to, t),
                device_id_type=pl.DeviceIdType.MESH,
            ).start()
            return c

        if to == ocean_sec:
            lax.fori_loop(0, n_tile, one, 0)
            return

        @pl.when(is_relay)
        def _():
            pltpu.make_async_copy(
                send.at[part, flipped(tile)],
                recv.at[part, tile // 8, parity, sec * in_plane + lax.rem(tile // 2, in_plane)],
                fr_sem.at[part, tile // 8],
            ).start()
            lax.fori_loop(1, n_tile, one, 0)

        @pl.when(jnp.logical_not(is_relay))
        def _():
            lax.fori_loop(0, n_tile, one, 0)

    def shipped(part, kept):
        sent = send.at[part, kept:n_tile]
        pltpu.make_async_copy(sent, sent, fs_sem.at[part]).wait()

    def gather(part):
        flux = jnp.zeros((rows, width), F32)
        for z in range(PLANES):
            came = recv.at[part, z, :, 0:filled]
            pltpu.make_async_copy(came, came, fr_sem.at[part, z]).wait()
            hi, lo = split(recv[part, z].reshape(4 * rows, width))
            flux = flux + matmul(smat[z], hi) + matmul(smat[z], lo)
        return flux

    def give_back(first_k, last_k):
        ocean_tile = flipped(tile)

        def one(k, c):
            i = lax.rem(k, 16)
            z = 2 * (k // 16) + lax.rem(i // 4 + tile // 8, 2)
            t = 8 * z + 2 * lax.rem(i + tile // 2, 4) + i // 8

            z2 = 2 * (k // 16) + lax.rem(i // 8 + tile // 8, 2)
            t2 = 8 * z2 + 2 * lax.rem(i // 2 + tile // 2, 4) + lax.rem(i, 2)

            def to(a, t):
                return pltpu.make_async_remote_copy(
                    src_ref=ret.at[a * n_tile + lax.rem(t, 2) * half + t // 2],
                    dst_ref=arr.at[ocean_tile],
                    send_sem=bs_sem,
                    recv_sem=br_sem,
                    device_id=(a, t),
                    device_id_type=pl.DeviceIdType.MESH,
                )

            @pl.when(t != tile)
            def _():
                to(relay_sec, t).start()

            to(0, t).start()
            to(near_sec, t2).start()
            return c

        lax.fori_loop(first_k, last_k, one, 0)

    def keep_own():
        ocean_tile = flipped(tile)
        pltpu.make_async_copy(
            ret.at[relay_sec * n_tile + parity * half + tile // 2], arr.at[ocean_tile], br_sem
        ).start()

    @pl.when(jnp.logical_not(is_ocean))
    def _():
        pack(0, fo[0, 0])

        @pl.when(jnp.logical_not(is_relay))
        def _():
            pl.semaphore_wait(k_sem, 1)

        ship(0, relay_sec)

        @pl.when(is_relay)
        def _():
            pl.semaphore_wait(h_sem, 1)
            greet(o_sem, 0, tile)
            greet(o_sem, near_sec, flipped(tile))

        for l in range(1, levels):
            fo[0, l] = stencil(l)
        pack(1, fo[0, 0] - fo[0, 1])


        @pl.when(jnp.logical_not(is_relay))
        def _():
            shipped(0, 0)

        @pl.when(is_relay)
        def _():
            shipped(0, 1)

        @pl.when(jnp.logical_not(is_relay))
        def _():
            pl.semaphore_wait(o_sem, 1)

        ship(1, ocean_sec)

        @pl.when(is_relay)
        def _():
            place_all(flipped(tile))

        for t in range(ntab):
            hi, lo = split(tab[t].T)
            tthi[t] = hi
            ttlo[t] = lo

        @pl.when(is_relay)
        def _():
            mask_copy().wait_recv()
            base_copy().wait_recv()
            water = far_mask[...].astype(F32)
            flux = gather(0)
            flux0[...] = flux
            flux_copy().start()
            hi, lo = split(water * (base[...] + forcing_rate * water * flux))
            both = jnp.concatenate([hi, lo], axis=0)
            count = half * cap // 2
            for low_high in range(2):
                for a in range(n_atm):
                    for h in range(2):
                        n = 2 * h + low_high
                        ret[a * n_tile + n * 8 : a * n_tile + n * 8 + 8] = matmul(
                            rmat[a, n * count : (n + 1) * count], both
                        ).reshape(8, cap, width)
                give_back(low_high * half, (low_high + 1) * half)
            keep_own()

        pltpu.make_async_copy(arr, arr, br_sem).wait()
        uhi, ulo = split(arr[...].reshape(n_tile * cap, width))
        v = matmul(mtmat[...], uhi) + matmul(mtmat[...], ulo)
        total = jnp.zeros((rows, width), F32)
        for t in range(ntab):
            vhi, vlo = split(v[t * rows : (t + 1) * rows])
            r = matmul(jnp.concatenate([vhi, vlo], axis=0), tthi[t])
            total = total + r[:rows] + r[rows:] + matmul(vhi, ttlo[t])
        su[0] = total

        shipped(1, 0)

        @pl.when(is_relay)
        def _():
            others = ret.at[1 : n_atm * n_tile]
            pltpu.make_async_copy(others, others, bs_sem).wait()
            flux_copy().wait_send()

    @pl.when(is_ocean)
    def _():
        base[...] = fo[0, 0]
        base_copy().start()
        place_all(tile)
        for l in range(1, levels):
            fo[0, l] = stencil(l)
        water = mask[...].astype(F32)
        flux_copy().wait_recv()
        first = fo[0, 0] + forcing_rate * water * flux0[...]
        fo[0, 0] = first
        su[0] = water * first
        fo[0, 1] = fo[0, 1] + forcing_rate * water * gather(1)
        mask_copy().wait_send()
        base_copy().wait_send()


def store(fields, surface, fields_out, surface_out, sems):
    copies = [
        pltpu.make_async_copy(fields, fields_out, sems.at[0]),
        pltpu.make_async_copy(surface, surface_out, sems.at[1]),
    ]
    for copy in copies:
        copy.start()
    for copy in copies:
        copy.wait()


def local(fields, coefficients, owner_tile, dest_block, table_index, tables, land_mask):
    n_sec = lax.axis_size("sec")
    n_tile = lax.axis_size("tile")
    _, levels, rows, width = fields.shape
    blocks, fan_out = owner_tile.shape
    ntab = tables.shape[0]
    cap = 2 * fan_out * rows // n_tile
    n_atm = n_sec - 1
    half = n_tile // 2
    padded = rows + 2 * PAD
    slots = n_tile * cap
    scratch = [
        pltpu.VMEM((levels, padded, width), F32),
        pltpu.VMEM((2, padded, width), F32),
        pltpu.VMEM((fan_out, blocks), jnp.int32),
        pltpu.VMEM((fan_out, blocks), jnp.int32),
        pltpu.VMEM((fan_out, blocks), jnp.int32),
        pltpu.VMEM((ntab, width, width), F32),
        pltpu.VMEM((rows, width), jnp.int32),
        pltpu.VMEM((2, 16, width), F32),
        pltpu.VMEM((2, 16, width), F32),
        pltpu.VMEM((ntab, width, width), BF16),
        pltpu.VMEM((ntab, width, width), BF16),
        pltpu.VMEM((ntab, width, width), BF16),
        pltpu.VMEM((ntab, width, width), BF16),
        pltpu.VMEM((slots, ntab * rows), BF16),
        pltpu.VMEM((ntab * rows, slots), BF16),
        pltpu.VMEM((ntab * rows, width), BF16),
        pltpu.VMEM((ntab * rows, width), BF16),
        pltpu.VMEM((2, n_tile, cap, width), F32),
        pltpu.VMEM((2, PLANES, 2, 16, cap, width), F32),
        pltpu.VMEM((half, 2 * rows), F32),
        pltpu.VMEM((half, 2 * rows), F32),
        pltpu.VMEM((half, 2 * rows), F32),
        pltpu.VMEM((half, 2 * rows), F32),
        pltpu.VMEM((PLANES, 2 * rows, 2 * rows), F32),
        pltpu.VMEM((PLANES, rows, 4 * rows), BF16),
        pltpu.VMEM((n_atm, slots, 2 * rows), BF16),
        pltpu.VMEM((n_atm * n_tile, cap, width), F32),
        pltpu.VMEM((n_tile, cap, width), F32),
        pltpu.VMEM((rows, width), F32),
        pltpu.VMEM((rows, width), F32),
        pltpu.VMEM((rows, width), jnp.int32),
        pltpu.SemaphoreType.DMA((7,)),
        pltpu.SemaphoreType.DMA((2,)),
        pltpu.SemaphoreType.DMA((2,)),
        pltpu.SemaphoreType.DMA((2,)),
        pltpu.SemaphoreType.DMA((2, PLANES)),
        pltpu.SemaphoreType.DMA,
        pltpu.SemaphoreType.DMA,
        pltpu.SemaphoreType.REGULAR,
        pltpu.SemaphoreType.REGULAR,
        pltpu.SemaphoreType.REGULAR,
        pltpu.SemaphoreType.REGULAR,
        pltpu.SemaphoreType.REGULAR,
        pltpu.SemaphoreType.DMA((3,)),
        pltpu.SemaphoreType.DMA((3,)),
    ]
    operands = (fields, coefficients, owner_tile.T, dest_block.T, table_index.T, tables, land_mask)
    shapes = (
        jax.ShapeDtypeStruct(fields.shape, F32),
        jax.ShapeDtypeStruct((1, rows, width), F32),
    )
    results = pl.pallas_call(
        functools.partial(kernel, n_sec, n_tile, cap),
        out_shape=shapes,
        in_specs=[pl.BlockSpec(memory_space=pltpu.HBM)] * 7,
        out_specs=(
            pl.BlockSpec(memory_space=pltpu.VMEM),
            pl.BlockSpec(memory_space=pltpu.VMEM),
        ),
        scratch_shapes=scratch,
        compiler_params=pltpu.CompilerParams(
            collective_id=0, has_side_effects=True, vmem_limit_bytes=32 * 1024 * 1024
        ),
    )(*(pltpu.with_memory_space_constraint(x, pltpu.HBM) for x in operands))
    return pl.pallas_call(
        store,
        out_shape=shapes,
        in_specs=[pl.BlockSpec(memory_space=pltpu.VMEM)] * 2,
        out_specs=(pl.BlockSpec(memory_space=pl.ANY),) * 2,
        scratch_shapes=[pltpu.SemaphoreType.DMA((2,))],
    )(*(pltpu.with_memory_space_constraint(x, pltpu.VMEM) for x in results))


def solution(mesh):
    placed = (
        P("sec", None, "tile", None),
        P("sec", None, "tile", None),
        P(),
        P(),
        P(),
        P(),
        P("tile", None),
    )
    return jax.shard_map(
        local,
        mesh=mesh,
        in_specs=placed,
        out_specs=(P("sec", None, "tile", None), P("sec", "tile", None)),
        check_vma=False,
    )
```

```python
import functools

import jax
import jax.numpy as jnp
from jax import lax
from jax.experimental import pallas as pl
from jax.experimental.pallas import tpu as pltpu
from jax.sharding import PartitionSpec as P

forcing_rate = 0.5

F32 = jnp.float32
BF16 = jnp.bfloat16
PAD = 8
PLANES = 4


def matmul(a, b):
    return lax.dot_general(a, b, (((1,), (0,)), ((), ())), preferred_element_type=F32)


def split(x):
    hi = x.astype(BF16)
    return hi, (x - hi.astype(F32)).astype(BF16)


def iota(shape, dim):
    return lax.broadcasted_iota(jnp.int32, shape, dim)


def kernel(
    n_sec, n_tile, cap,
    fields, coef, ot_in, db_in, ti_in, tables, mask_in,
    fo, su,
    ext, cext, ot, db, ti, tab, mask, hsend, hrecv,
    thi, tlo, tthi, ttlo, mmat, mtmat, pthi, ptlo, send, recv,
    x0, x1, d0, d1, hots, smat, rmat, ret, arr, base, flux0, far_mask,
    in_sem, hs_sem, hr_sem, fs_sem, fr_sem, bs_sem, br_sem, o_sem, p_sem, k_sem, g_sem, h_sem, cs_sem, cr_sem,
):
    n_atm = n_sec - 1
    ocean_sec = n_sec - 1
    near_sec = n_sec - 2
    relay_sec = near_sec - 1
    half = n_tile // 2
    in_plane = n_tile // PLANES // 2
    filled = n_atm * in_plane
    levels, rows, width = fo.shape[1:]
    ntab = tables.shape[0]
    top, low = PAD, PAD + rows
    sec = lax.axis_index("sec")
    tile = lax.axis_index("tile")
    upper = lax.rem(tile + n_tile - 1, n_tile)
    lower = lax.rem(tile + 1, n_tile)
    is_ocean = sec == ocean_sec
    is_near = sec == near_sec
    is_relay = sec == relay_sec
    parity = lax.rem(tile, 2)

    def flipped(t):
        return t + 1 - 2 * lax.rem(t, 2)


    def load(number, src, dst):
        return pltpu.make_async_copy(src, dst, in_sem.at[number])

    loads = [
        load(0, fields.at[0], ext.at[:, top:low, :]),
        load(1, coef.at[0], cext.at[:, top:low, :]),
        load(2, ot_in, ot),
        load(3, db_in, db),
        load(4, ti_in, ti),
        load(5, tables, tab),
        load(6, mask_in, mask),
    ]
    for copy in loads:
        copy.start()

    barrier = pltpu.get_barrier_semaphore()
    has_upper, has_lower = tile > 0, tile < n_tile - 1
    neighbours = has_upper.astype(jnp.int32) + has_lower.astype(jnp.int32)

    def greet(semaphore, s, t):
        pl.semaphore_signal(semaphore, inc=1, device_id=(s, t), device_id_type=pl.DeviceIdType.MESH)

    @pl.when(jnp.logical_not(has_upper))
    def _():
        hrecv[0] = jnp.zeros_like(hrecv[0])

    @pl.when(jnp.logical_not(has_lower))
    def _():
        hrecv[1] = jnp.zeros_like(hrecv[1])

    def clear(part):
        for z in range(PLANES):
            for h in range(2):
                recv[part, z, h, filled:] = jnp.zeros_like(recv[part, z, h, filled:])

    @pl.when(is_relay)
    def _():
        clear(0)

    @pl.when(is_ocean)
    def _():
        clear(1)

    @pl.when(has_upper)
    def _():
        greet(barrier, sec, upper)

    @pl.when(has_lower)
    def _():
        greet(barrier, sec, lower)

    def greet_plane(semaphore):
        def one(k, c):
            z = lax.rem(tile // 8 + k // 4, 4)
            x = lax.rem(tile // 2 + lax.rem(k, 4), 4)
            greet(semaphore, sec, z * 8 + x * 2 + parity)
            return c

        lax.fori_loop(1, half, one, 0)

    @pl.when(is_relay)
    def _():
        greet_plane(barrier)
        greet(barrier, ocean_sec, flipped(tile))

    @pl.when(sec == 0)
    def _():
        greet(barrier, relay_sec, tile)

    @pl.when(is_near | is_ocean)
    def _():
        greet(barrier, relay_sec, flipped(tile))

    zero = jnp.zeros((PAD, width), F32)
    for l in range(levels):
        ext[l, 0:top, :] = zero
        ext[l, low : low + PAD, :] = zero
    for c in range(2):
        cext[c, 0:top, :] = zero
        cext[c, low : low + PAD, :] = zero
        hsend[c, 8:16, :] = zero

    loads[0].wait()
    for l in range(levels):
        hsend[0, 2 * l : 2 * l + 2, :] = ext[l, top : top + 2, :]
        hsend[1, 2 * l : 2 * l + 2, :] = ext[l, low - 2 : low, :]
    loads[1].wait()
    for c in range(2):
        hsend[0, 8 + c : 9 + c, :] = cext[c, top : top + 1, :]
        hsend[1, 8 + c : 9 + c, :] = cext[c, low - 1 : low, :]

    @pl.when(is_relay)
    def _():
        pl.semaphore_wait(barrier, neighbours + half + 2)

    @pl.when(is_ocean)
    def _():
        pl.semaphore_wait(barrier, neighbours + 1)

    @pl.when(jnp.logical_not(is_relay | is_ocean))
    def _():
        pl.semaphore_wait(barrier, neighbours)

    def column_copy(src, dst, number, to):
        return pltpu.make_async_remote_copy(
            src_ref=src,
            dst_ref=dst,
            send_sem=cs_sem.at[number],
            recv_sem=cr_sem.at[number],
            device_id=(to, flipped(tile)),
            device_id_type=pl.DeviceIdType.MESH,
        )

    def mask_copy():
        return column_copy(mask, far_mask, 0, relay_sec)

    def base_copy():
        return column_copy(base, base, 1, relay_sec)

    def flux_copy():
        return column_copy(flux0, flux0, 2, ocean_sec)

    def halo(way, to):
        return pltpu.make_async_remote_copy(
            src_ref=hsend.at[way],
            dst_ref=hrecv.at[1 - way],
            send_sem=hs_sem.at[way],
            recv_sem=hr_sem.at[1 - way],
            device_id=(sec, to),
            device_id_type=pl.DeviceIdType.MESH,
        )

    halos = [halo(0, upper), halo(1, lower)]

    @pl.when(has_upper)
    def _():
        halos[0].start()

    @pl.when(has_lower)
    def _():
        halos[1].start()

    @pl.when(is_ocean)
    def _():
        loads[6].wait()
        mask_copy().start()

    @pl.when(is_relay)
    def _():
        greet(p_sem, sec, flipped(tile))
        greet_plane(g_sem)

    loads[2].wait()
    loads[3].wait()
    loads[4].wait()
    loads[5].wait()

    @pl.when(jnp.logical_not(is_ocean))
    def _():
        loads[6].wait()


    lane = iota((8, 128), 1)
    left = lane < 64

    def place(number, a, owner):
        for kk in range(half):
            cols = pl.ds(pl.multiple_of((a * half + kk) * 128, 128), 128)
            x0[kk : kk + 1, :] = ot[0:1, cols].astype(F32)
            x1[kk : kk + 1, :] = ot[1:2, cols].astype(F32)
            d0[kk : kk + 1, :] = db[0:1, cols].astype(F32) + 1.0
            d1[kk : kk + 1, :] = db[1:2, cols].astype(F32) + 1.0
        src, dst = iota((128, 128), 0), iota((128, 128), 1)
        same = (src // 64) == (dst // 64)
        both = same.astype(F32).astype(BF16)
        before = (same & (src < dst)).astype(F32).astype(BF16)
        mine_of = owner.astype(F32)
        mine0 = x0[...] == mine_of
        mine1 = x1[...] == mine_of
        m0 = mine0.astype(F32).astype(BF16)
        m1 = mine1.astype(F32).astype(BF16)
        x0[...] = jnp.where(mine0, matmul(m0, before), -1.0)
        x1[...] = jnp.where(mine1, matmul(m1, before) + matmul(m0, both), -1.0)
        slot = iota((cap, 128), 0).astype(F32)
        parts = []
        for kk in range(half):
            parts.append(
                jnp.where(x0[kk : kk + 1, :] == slot, d0[kk : kk + 1, :], 0.0)
                + jnp.where(x1[kk : kk + 1, :] == slot, d1[kk : kk + 1, :], 0.0)
            )
        named = jnp.concatenate(parts, axis=0).astype(BF16)
        count = half * cap
        lane_c = iota((count, 128), 1)
        left_c = lane_c < 64
        want = (lax.rem(lane_c, 64) + 1).astype(F32)
        hot = (matmul(named, both) == want).astype(F32)
        width_z = in_plane * cap
        for z in range(PLANES):
            hots[z, a * width_z : (a + 1) * width_z, :] = hot[z * width_z : (z + 1) * width_z]
        other = pltpu.roll(hot, 64, 1)
        rmat[number, 0:count, :] = jnp.where(left_c, hot, other).astype(BF16)
        rmat[number, count : 2 * count, :] = jnp.where(left_c, other, hot).astype(BF16)

    def place_all(owner):
        hots[:, filled * cap :, :] = jnp.zeros_like(hots[:, filled * cap :, :])
        for a in range(n_atm):
            place(a, a, owner)
        for z in range(PLANES):
            turned = hots[z].T
            smat[z, :, 0:128] = turned[0:64].astype(BF16)
            smat[z, :, 128:256] = turned[64:128].astype(BF16)

    @pl.when(jnp.logical_not(is_ocean))
    def _():
        number = sec * n_tile + tile
        cols = pl.ds(pl.multiple_of((number // 2) * 128, 128), 128)

        def pairs(ref):
            r0 = jnp.broadcast_to(ref[0:1, cols].astype(F32), (8, 128))
            r1 = jnp.broadcast_to(ref[1:2, cols].astype(F32), (8, 128))
            even = jnp.where(left, r0, pltpu.roll(r1, 64, 1))
            odd = jnp.where(left, pltpu.roll(r0, 64, 1), r1)
            return jnp.where(parity == 0, even, odd)

        own, entry = pairs(ot), pairs(ti)
        across = jnp.broadcast_to(own[0:1], (128, 128))
        earlier = (across.T == across) & (iota((128, 128), 0) < iota((128, 128), 1))
        rank = jnp.sum(earlier.astype(F32), axis=0, keepdims=True)
        target = own * float(cap) + jnp.broadcast_to(rank, (8, 128))

        def doubled(v):
            turned = pltpu.roll(v, 64, 1)
            return jnp.where(left, v, turned), jnp.where(left, turned, v)

        t0, t1 = doubled(target)
        e0, e1 = doubled(entry)
        slots = iota((n_tile * cap, 128), 0).astype(F32)
        for b in range(ntab // 2):
            here = (lane // 64 + 2 * b).astype(F32)
            v0 = jnp.where(e0 == here, t0, -1.0)
            v1 = jnp.where(e1 == here, t1, -1.0)
            hot = ((slots == v0[0:1]) | (slots == v1[0:1])).astype(F32)
            mmat[:, 128 * b : 128 * (b + 1)] = hot.astype(BF16)
            mtmat[128 * b : 128 * (b + 1), :] = hot.T.astype(BF16)
        for t in range(ntab):
            hi, lo = split(tab[t])
            thi[t] = hi
            tlo[t] = lo

    @pl.when(is_relay)
    def _():
        pl.semaphore_wait(p_sem, 1)
        greet(k_sem, 0, tile)
        greet(k_sem, near_sec, flipped(tile))

    @pl.when(is_relay)
    def _():
        pl.semaphore_wait(g_sem, half - 1)
        greet(h_sem, sec, flipped(tile))

    @pl.when(has_upper)
    def _():
        halos[0].wait_send()
        halos[1].wait_recv()

    @pl.when(has_lower)
    def _():
        halos[1].wait_send()
        halos[0].wait_recv()

    above, below = hrecv[0], hrecv[1]
    for l in range(levels):
        ext[l, top - 2 : top, :] = above[2 * l : 2 * l + 2]
        ext[l, low : low + 2, :] = below[2 * l : 2 * l + 2]
    for c in range(2):
        cext[c, top - 1 : top, :] = above[8 + c : 9 + c]
        cext[c, low : low + 1, :] = below[8 + c : 9 + c]

    def substep(u, kappa, speed):
        n = u.shape[0]
        up = pltpu.roll(u, 1, 0)
        down = pltpu.roll(u, n - 1, 0)
        sides = pltpu.roll(u, 1, 1) + pltpu.roll(u, width - 1, 1)
        return u + kappa * (up + down + sides - 4.0 * u) - 0.5 * speed * (down - up)

    def stencil(l):
        kappa, speed = cext[0], cext[1]
        u = substep(ext[l], kappa, speed)
        return substep(u, kappa, speed)[top:low]

    fo[0, 0] = stencil(0)

    def pack(part, row):
        hi, lo = split(row)
        stacked = jnp.concatenate([hi, lo], axis=0)
        for t in range(ntab):
            r = matmul(stacked, thi[t])
            r = r[:rows] + r[rows:] + matmul(hi, tlo[t])
            here = slice(t * rows, (t + 1) * rows)
            pthi[here, :], ptlo[here, :] = split(r)
        out = matmul(mmat[...], pthi[...]) + matmul(mmat[...], ptlo[...])
        send[part] = out.reshape(send.shape[1:])

    def ship(part, to):
        def one(k, c):
            t = lax.rem(tile + k, n_tile)
            pltpu.make_async_remote_copy(
                src_ref=send.at[part, t if to == ocean_sec else flipped(t)],
                dst_ref=recv.at[part, tile // 8, parity, sec * in_plane + lax.rem(tile // 2, in_plane)],
                send_sem=fs_sem.at[part],
                recv_sem=fr_sem.at[part, tile // 8],
                device_id=(to, t),
                device_id_type=pl.DeviceIdType.MESH,
            ).start()
            return c

        if to == ocean_sec:
            lax.fori_loop(0, n_tile, one, 0)
            return

        @pl.when(is_relay)
        def _():
            pltpu.make_async_copy(
                send.at[part, flipped(tile)],
                recv.at[part, tile // 8, parity, sec * in_plane + lax.rem(tile // 2, in_plane)],
                fr_sem.at[part, tile // 8],
            ).start()
            lax.fori_loop(1, n_tile, one, 0)

        @pl.when(jnp.logical_not(is_relay))
        def _():
            lax.fori_loop(0, n_tile, one, 0)

    def shipped(part, kept):
        sent = send.at[part, kept:n_tile]
        pltpu.make_async_copy(sent, sent, fs_sem.at[part]).wait()

    def gather(part):
        flux = jnp.zeros((rows, width), F32)
        for z in range(PLANES):
            came = recv.at[part, z, :, 0:filled]
            pltpu.make_async_copy(came, came, fr_sem.at[part, z]).wait()
            hi, lo = split(recv[part, z].reshape(4 * rows, width))
            flux = flux + matmul(smat[z], hi) + matmul(smat[z], lo)
        return flux

    def give_back(first_k, last_k):
        ocean_tile = flipped(tile)

        def one(k, c):
            i = lax.rem(k, 16)
            z = 2 * (k // 16) + lax.rem(i // 4 + tile // 8, 2)
            t = 8 * z + 2 * lax.rem(i, 4) + i // 8

            z2 = 2 * (k // 16) + lax.rem(i // 8 + tile // 8, 2)
            t2 = 8 * z2 + 2 * lax.rem(i // 2 + tile // 2, 4) + lax.rem(i, 2)

            def to(a, t):
                return pltpu.make_async_remote_copy(
                    src_ref=ret.at[a * n_tile + lax.rem(t, 2) * half + t // 2],
                    dst_ref=arr.at[ocean_tile],
                    send_sem=bs_sem,
                    recv_sem=br_sem,
                    device_id=(a, t),
                    device_id_type=pl.DeviceIdType.MESH,
                )

            @pl.when(t != tile)
            def _():
                to(relay_sec, t).start()

            to(0, t).start()
            to(near_sec, t2).start()
            return c

        lax.fori_loop(first_k, last_k, one, 0)

    def keep_own():
        ocean_tile = flipped(tile)
        pltpu.make_async_copy(
            ret.at[relay_sec * n_tile + parity * half + tile // 2], arr.at[ocean_tile], br_sem
        ).start()

    @pl.when(jnp.logical_not(is_ocean))
    def _():
        pack(0, fo[0, 0])

        @pl.when(jnp.logical_not(is_relay))
        def _():
            pl.semaphore_wait(k_sem, 1)

        ship(0, relay_sec)

        @pl.when(is_relay)
        def _():
            pl.semaphore_wait(h_sem, 1)
            greet(o_sem, 0, tile)
            greet(o_sem, near_sec, flipped(tile))

        for l in range(1, levels):
            fo[0, l] = stencil(l)
        pack(1, fo[0, 0] - fo[0, 1])


        @pl.when(jnp.logical_not(is_relay))
        def _():
            shipped(0, 0)

        @pl.when(is_relay)
        def _():
            shipped(0, 1)

        @pl.when(jnp.logical_not(is_relay))
        def _():
            pl.semaphore_wait(o_sem, 1)

        ship(1, ocean_sec)

        @pl.when(is_relay)
        def _():
            place_all(flipped(tile))

        for t in range(ntab):
            hi, lo = split(tab[t].T)
            tthi[t] = hi
            ttlo[t] = lo

        @pl.when(is_relay)
        def _():
            mask_copy().wait_recv()
            base_copy().wait_recv()
            water = far_mask[...].astype(F32)
            flux = gather(0)
            flux0[...] = flux
            flux_copy().start()
            hi, lo = split(water * (base[...] + forcing_rate * water * flux))
            both = jnp.concatenate([hi, lo], axis=0)
            count = half * cap // 2
            for low_high in range(2):
                for a in range(n_atm):
                    for h in range(2):
                        n = 2 * h + low_high
                        ret[a * n_tile + n * 8 : a * n_tile + n * 8 + 8] = matmul(
                            rmat[a, n * count : (n + 1) * count], both
                        ).reshape(8, cap, width)
                give_back(low_high * half, (low_high + 1) * half)
            keep_own()

        pltpu.make_async_copy(arr, arr, br_sem).wait()
        uhi, ulo = split(arr[...].reshape(n_tile * cap, width))
        v = matmul(mtmat[...], uhi) + matmul(mtmat[...], ulo)
        total = jnp.zeros((rows, width), F32)
        for t in range(ntab):
            vhi, vlo = split(v[t * rows : (t + 1) * rows])
            r = matmul(jnp.concatenate([vhi, vlo], axis=0), tthi[t])
            total = total + r[:rows] + r[rows:] + matmul(vhi, ttlo[t])
        su[0] = total

        shipped(1, 0)

        @pl.when(is_relay)
        def _():
            others = ret.at[1 : n_atm * n_tile]
            pltpu.make_async_copy(others, others, bs_sem).wait()
            flux_copy().wait_send()

    @pl.when(is_ocean)
    def _():
        base[...] = fo[0, 0]
        base_copy().start()
        place_all(tile)
        for l in range(1, levels):
            fo[0, l] = stencil(l)
        water = mask[...].astype(F32)
        flux_copy().wait_recv()
        first = fo[0, 0] + forcing_rate * water * flux0[...]
        fo[0, 0] = first
        su[0] = water * first
        fo[0, 1] = fo[0, 1] + forcing_rate * water * gather(1)
        mask_copy().wait_send()
        base_copy().wait_send()


def store(fields, surface, fields_out, surface_out, sems):
    copies = [
        pltpu.make_async_copy(fields, fields_out, sems.at[0]),
        pltpu.make_async_copy(surface, surface_out, sems.at[1]),
    ]
    for copy in copies:
        copy.start()
    for copy in copies:
        copy.wait()


def local(fields, coefficients, owner_tile, dest_block, table_index, tables, land_mask):
    n_sec = lax.axis_size("sec")
    n_tile = lax.axis_size("tile")
    _, levels, rows, width = fields.shape
    blocks, fan_out = owner_tile.shape
    ntab = tables.shape[0]
    cap = 2 * fan_out * rows // n_tile
    n_atm = n_sec - 1
    half = n_tile // 2
    padded = rows + 2 * PAD
    slots = n_tile * cap
    scratch = [
        pltpu.VMEM((levels, padded, width), F32),
        pltpu.VMEM((2, padded, width), F32),
        pltpu.VMEM((fan_out, blocks), jnp.int32),
        pltpu.VMEM((fan_out, blocks), jnp.int32),
        pltpu.VMEM((fan_out, blocks), jnp.int32),
        pltpu.VMEM((ntab, width, width), F32),
        pltpu.VMEM((rows, width), jnp.int32),
        pltpu.VMEM((2, 16, width), F32),
        pltpu.VMEM((2, 16, width), F32),
        pltpu.VMEM((ntab, width, width), BF16),
        pltpu.VMEM((ntab, width, width), BF16),
        pltpu.VMEM((ntab, width, width), BF16),
        pltpu.VMEM((ntab, width, width), BF16),
        pltpu.VMEM((slots, ntab * rows), BF16),
        pltpu.VMEM((ntab * rows, slots), BF16),
        pltpu.VMEM((ntab * rows, width), BF16),
        pltpu.VMEM((ntab * rows, width), BF16),
        pltpu.VMEM((2, n_tile, cap, width), F32),
        pltpu.VMEM((2, PLANES, 2, 16, cap, width), F32),
        pltpu.VMEM((half, 2 * rows), F32),
        pltpu.VMEM((half, 2 * rows), F32),
        pltpu.VMEM((half, 2 * rows), F32),
        pltpu.VMEM((half, 2 * rows), F32),
        pltpu.VMEM((PLANES, 2 * rows, 2 * rows), F32),
        pltpu.VMEM((PLANES, rows, 4 * rows), BF16),
        pltpu.VMEM((n_atm, slots, 2 * rows), BF16),
        pltpu.VMEM((n_atm * n_tile, cap, width), F32),
        pltpu.VMEM((n_tile, cap, width), F32),
        pltpu.VMEM((rows, width), F32),
        pltpu.VMEM((rows, width), F32),
        pltpu.VMEM((rows, width), jnp.int32),
        pltpu.SemaphoreType.DMA((7,)),
        pltpu.SemaphoreType.DMA((2,)),
        pltpu.SemaphoreType.DMA((2,)),
        pltpu.SemaphoreType.DMA((2,)),
        pltpu.SemaphoreType.DMA((2, PLANES)),
        pltpu.SemaphoreType.DMA,
        pltpu.SemaphoreType.DMA,
        pltpu.SemaphoreType.REGULAR,
        pltpu.SemaphoreType.REGULAR,
        pltpu.SemaphoreType.REGULAR,
        pltpu.SemaphoreType.REGULAR,
        pltpu.SemaphoreType.REGULAR,
        pltpu.SemaphoreType.DMA((3,)),
        pltpu.SemaphoreType.DMA((3,)),
    ]
    operands = (fields, coefficients, owner_tile.T, dest_block.T, table_index.T, tables, land_mask)
    shapes = (
        jax.ShapeDtypeStruct(fields.shape, F32),
        jax.ShapeDtypeStruct((1, rows, width), F32),
    )
    results = pl.pallas_call(
        functools.partial(kernel, n_sec, n_tile, cap),
        out_shape=shapes,
        in_specs=[pl.BlockSpec(memory_space=pltpu.HBM)] * 7,
        out_specs=(
            pl.BlockSpec(memory_space=pltpu.VMEM),
            pl.BlockSpec(memory_space=pltpu.VMEM),
        ),
        scratch_shapes=scratch,
        compiler_params=pltpu.CompilerParams(
            collective_id=0, has_side_effects=True, vmem_limit_bytes=32 * 1024 * 1024
        ),
    )(*(pltpu.with_memory_space_constraint(x, pltpu.HBM) for x in operands))
    return pl.pallas_call(
        store,
        out_shape=shapes,
        in_specs=[pl.BlockSpec(memory_space=pltpu.VMEM)] * 2,
        out_specs=(pl.BlockSpec(memory_space=pl.ANY),) * 2,
        scratch_shapes=[pltpu.SemaphoreType.DMA((2,))],
    )(*(pltpu.with_memory_space_constraint(x, pltpu.VMEM) for x in results))


def solution(mesh):
    placed = (
        P("sec", None, "tile", None),
        P("sec", None, "tile", None),
        P(),
        P(),
        P(),
        P(),
        P("tile", None),
    )
    return jax.shard_map(
        local,
        mesh=mesh,
        in_specs=placed,
        out_specs=(P("sec", None, "tile", None), P("sec", "tile", None)),
        check_vma=False,
    )
```

```python
import functools

import jax
import jax.numpy as jnp
from jax import lax
from jax.experimental import pallas as pl
from jax.experimental.pallas import tpu as pltpu
from jax.sharding import PartitionSpec as P

forcing_rate = 0.5

F32 = jnp.float32
BF16 = jnp.bfloat16
PAD = 8
PLANES = 4


def matmul(a, b):
    return lax.dot_general(a, b, (((1,), (0,)), ((), ())), preferred_element_type=F32)


def split(x):
    hi = x.astype(BF16)
    return hi, (x - hi.astype(F32)).astype(BF16)


def iota(shape, dim):
    return lax.broadcasted_iota(jnp.int32, shape, dim)


def kernel(
    n_sec, n_tile, cap,
    fields, coef, ot_in, db_in, ti_in, tables, mask_in,
    fo, su,
    ext, cext, ot, db, ti, tab, mask, hsend, hrecv,
    thi, tlo, tthi, ttlo, mmat, mtmat, pthi, ptlo, send, recv,
    x0, x1, d0, d1, hots, smat, rmat, ret, arr, base, flux0, far_mask,
    in_sem, hs_sem, hr_sem, fs_sem, fr_sem, bs_sem, br_sem, o_sem, p_sem, k_sem, g_sem, h_sem, cs_sem, cr_sem,
):
    n_atm = n_sec - 1
    ocean_sec = n_sec - 1
    near_sec = n_sec - 2
    relay_sec = near_sec - 1
    half = n_tile // 2
    in_plane = n_tile // PLANES // 2
    filled = n_atm * in_plane
    levels, rows, width = fo.shape[1:]
    ntab = tables.shape[0]
    top, low = PAD, PAD + rows
    sec = lax.axis_index("sec")
    tile = lax.axis_index("tile")
    upper = lax.rem(tile + n_tile - 1, n_tile)
    lower = lax.rem(tile + 1, n_tile)
    is_ocean = sec == ocean_sec
    is_near = sec == near_sec
    is_relay = sec == relay_sec
    parity = lax.rem(tile, 2)

    def flipped(t):
        return t + 1 - 2 * lax.rem(t, 2)


    def load(number, src, dst):
        return pltpu.make_async_copy(src, dst, in_sem.at[number])

    loads = [
        load(0, fields.at[0], ext.at[:, top:low, :]),
        load(1, coef.at[0], cext.at[:, top:low, :]),
        load(2, ot_in, ot),
        load(3, db_in, db),
        load(4, ti_in, ti),
        load(5, tables, tab),
        load(6, mask_in, mask),
    ]
    for copy in loads:
        copy.start()

    barrier = pltpu.get_barrier_semaphore()
    has_upper, has_lower = tile > 0, tile < n_tile - 1
    neighbours = has_upper.astype(jnp.int32) + has_lower.astype(jnp.int32)

    def greet(semaphore, s, t):
        pl.semaphore_signal(semaphore, inc=1, device_id=(s, t), device_id_type=pl.DeviceIdType.MESH)

    @pl.when(jnp.logical_not(has_upper))
    def _():
        hrecv[0] = jnp.zeros_like(hrecv[0])

    @pl.when(jnp.logical_not(has_lower))
    def _():
        hrecv[1] = jnp.zeros_like(hrecv[1])

    def clear(part):
        for z in range(PLANES):
            for h in range(2):
                recv[part, z, h, filled:] = jnp.zeros_like(recv[part, z, h, filled:])

    @pl.when(is_relay)
    def _():
        clear(0)

    @pl.when(is_ocean)
    def _():
        clear(1)

    @pl.when(has_upper)
    def _():
        greet(barrier, sec, upper)

    @pl.when(has_lower)
    def _():
        greet(barrier, sec, lower)

    def greet_plane(semaphore):
        def one(k, c):
            z = lax.rem(tile // 8 + k // 4, 4)
            x = lax.rem(tile // 2 + lax.rem(k, 4), 4)
            greet(semaphore, sec, z * 8 + x * 2 + parity)
            return c

        lax.fori_loop(1, half, one, 0)

    @pl.when(is_relay)
    def _():
        greet_plane(barrier)
        greet(barrier, ocean_sec, flipped(tile))

    @pl.when(sec == 0)
    def _():
        greet(barrier, relay_sec, tile)

    @pl.when(is_near | is_ocean)
    def _():
        greet(barrier, relay_sec, flipped(tile))

    zero = jnp.zeros((PAD, width), F32)
    for l in range(levels):
        ext[l, 0:top, :] = zero
        ext[l, low : low + PAD, :] = zero
    for c in range(2):
        cext[c, 0:top, :] = zero
        cext[c, low : low + PAD, :] = zero
        hsend[c, 0] = zero
        hsend[c, 1] = zero

    loads[0].wait()
    for l in range(levels):
        group, at = (0, 0) if l == 0 else (1, 2 * l - 2)
        hsend[0, group, at : at + 2, :] = ext[l, top : top + 2, :]
        hsend[1, group, at : at + 2, :] = ext[l, low - 2 : low, :]
    loads[1].wait()
    for c in range(2):
        hsend[0, 0, 2 + c : 3 + c, :] = cext[c, top : top + 1, :]
        hsend[1, 0, 2 + c : 3 + c, :] = cext[c, low - 1 : low, :]

    @pl.when(is_relay)
    def _():
        pl.semaphore_wait(barrier, neighbours + half + 2)

    @pl.when(is_ocean)
    def _():
        pl.semaphore_wait(barrier, neighbours + 1)

    @pl.when(jnp.logical_not(is_relay | is_ocean))
    def _():
        pl.semaphore_wait(barrier, neighbours)

    def column_copy(src, dst, number, to):
        return pltpu.make_async_remote_copy(
            src_ref=src,
            dst_ref=dst,
            send_sem=cs_sem.at[number],
            recv_sem=cr_sem.at[number],
            device_id=(to, flipped(tile)),
            device_id_type=pl.DeviceIdType.MESH,
        )

    def mask_copy():
        return column_copy(mask, far_mask, 0, relay_sec)

    def base_copy():
        return column_copy(base, base, 1, relay_sec)

    def flux_copy():
        return column_copy(flux0, flux0, 2, ocean_sec)

    def halo(way, to, group):
        return pltpu.make_async_remote_copy(
            src_ref=hsend.at[way, group],
            dst_ref=hrecv.at[1 - way, group],
            send_sem=hs_sem.at[way, group],
            recv_sem=hr_sem.at[1 - way, group],
            device_id=(sec, to),
            device_id_type=pl.DeviceIdType.MESH,
        )

    for group in range(2):

        @pl.when(has_upper)
        def _():
            halo(0, upper, group).start()

        @pl.when(has_lower)
        def _():
            halo(1, lower, group).start()

    def halo_wait(group):
        @pl.when(has_upper)
        def _():
            halo(0, upper, group).wait_send()
            halo(1, lower, group).wait_recv()

        @pl.when(has_lower)
        def _():
            halo(1, lower, group).wait_send()
            halo(0, upper, group).wait_recv()

    @pl.when(is_ocean)
    def _():
        loads[6].wait()
        mask_copy().start()

    @pl.when(is_relay)
    def _():
        greet(p_sem, sec, flipped(tile))
        greet_plane(g_sem)

    loads[2].wait()
    loads[3].wait()
    loads[4].wait()
    loads[5].wait()

    @pl.when(jnp.logical_not(is_ocean))
    def _():
        loads[6].wait()


    lane = iota((8, 128), 1)
    left = lane < 64

    def place(number, a, owner):
        for kk in range(half):
            cols = pl.ds(pl.multiple_of((a * half + kk) * 128, 128), 128)
            x0[kk : kk + 1, :] = ot[0:1, cols].astype(F32)
            x1[kk : kk + 1, :] = ot[1:2, cols].astype(F32)
            d0[kk : kk + 1, :] = db[0:1, cols].astype(F32) + 1.0
            d1[kk : kk + 1, :] = db[1:2, cols].astype(F32) + 1.0
        src, dst = iota((128, 128), 0), iota((128, 128), 1)
        same = (src // 64) == (dst // 64)
        both = same.astype(F32).astype(BF16)
        before = (same & (src < dst)).astype(F32).astype(BF16)
        mine_of = owner.astype(F32)
        mine0 = x0[...] == mine_of
        mine1 = x1[...] == mine_of
        m0 = mine0.astype(F32).astype(BF16)
        m1 = mine1.astype(F32).astype(BF16)
        x0[...] = jnp.where(mine0, matmul(m0, before), -1.0)
        x1[...] = jnp.where(mine1, matmul(m1, before) + matmul(m0, both), -1.0)
        slot = iota((cap, 128), 0).astype(F32)
        parts = []
        for kk in range(half):
            parts.append(
                jnp.where(x0[kk : kk + 1, :] == slot, d0[kk : kk + 1, :], 0.0)
                + jnp.where(x1[kk : kk + 1, :] == slot, d1[kk : kk + 1, :], 0.0)
            )
        named = jnp.concatenate(parts, axis=0).astype(BF16)
        count = half * cap
        lane_c = iota((count, 128), 1)
        left_c = lane_c < 64
        want = (lax.rem(lane_c, 64) + 1).astype(F32)
        hot = (matmul(named, both) == want).astype(F32)
        width_z = in_plane * cap
        for z in range(PLANES):
            hots[z, a * width_z : (a + 1) * width_z, :] = hot[z * width_z : (z + 1) * width_z]
        other = pltpu.roll(hot, 64, 1)
        rmat[number, 0:count, :] = jnp.where(left_c, hot, other).astype(BF16)
        rmat[number, count : 2 * count, :] = jnp.where(left_c, other, hot).astype(BF16)

    def place_all(owner):
        hots[:, filled * cap :, :] = jnp.zeros_like(hots[:, filled * cap :, :])
        for a in range(n_atm):
            place(a, a, owner)
        for z in range(PLANES):
            turned = hots[z].T
            smat[z, :, 0:128] = turned[0:64].astype(BF16)
            smat[z, :, 128:256] = turned[64:128].astype(BF16)

    @pl.when(jnp.logical_not(is_ocean))
    def _():
        number = sec * n_tile + tile
        cols = pl.ds(pl.multiple_of((number // 2) * 128, 128), 128)

        def pairs(ref):
            r0 = jnp.broadcast_to(ref[0:1, cols].astype(F32), (8, 128))
            r1 = jnp.broadcast_to(ref[1:2, cols].astype(F32), (8, 128))
            even = jnp.where(left, r0, pltpu.roll(r1, 64, 1))
            odd = jnp.where(left, pltpu.roll(r0, 64, 1), r1)
            return jnp.where(parity == 0, even, odd)

        own, entry = pairs(ot), pairs(ti)
        across = jnp.broadcast_to(own[0:1], (128, 128))
        earlier = (across.T == across) & (iota((128, 128), 0) < iota((128, 128), 1))
        rank = jnp.sum(earlier.astype(F32), axis=0, keepdims=True)
        target = own * float(cap) + jnp.broadcast_to(rank, (8, 128))

        def doubled(v):
            turned = pltpu.roll(v, 64, 1)
            return jnp.where(left, v, turned), jnp.where(left, turned, v)

        t0, t1 = doubled(target)
        e0, e1 = doubled(entry)
        slots = iota((n_tile * cap, 128), 0).astype(F32)
        for b in range(ntab // 2):
            here = (lane // 64 + 2 * b).astype(F32)
            v0 = jnp.where(e0 == here, t0, -1.0)
            v1 = jnp.where(e1 == here, t1, -1.0)
            hot = ((slots == v0[0:1]) | (slots == v1[0:1])).astype(F32)
            mmat[:, 128 * b : 128 * (b + 1)] = hot.astype(BF16)
            mtmat[128 * b : 128 * (b + 1), :] = hot.T.astype(BF16)
        for t in range(ntab):
            hi, lo = split(tab[t])
            thi[t] = hi
            tlo[t] = lo

    @pl.when(is_relay)
    def _():
        pl.semaphore_wait(p_sem, 1)
        greet(k_sem, 0, tile)
        greet(k_sem, near_sec, flipped(tile))

    @pl.when(is_relay)
    def _():
        pl.semaphore_wait(g_sem, half - 1)
        greet(h_sem, sec, flipped(tile))

    halo_wait(0)
    above, below = hrecv[0, 0], hrecv[1, 0]
    ext[0, top - 2 : top, :] = above[0:2]
    ext[0, low : low + 2, :] = below[0:2]
    for c in range(2):
        cext[c, top - 1 : top, :] = above[2 + c : 3 + c]
        cext[c, low : low + 1, :] = below[2 + c : 3 + c]

    def other_levels():
        halo_wait(1)
        above, below = hrecv[0, 1], hrecv[1, 1]
        for l in range(1, levels):
            ext[l, top - 2 : top, :] = above[2 * l - 2 : 2 * l]
            ext[l, low : low + 2, :] = below[2 * l - 2 : 2 * l]
            fo[0, l] = stencil(l)

    def substep(u, kappa, speed):
        n = u.shape[0]
        up = pltpu.roll(u, 1, 0)
        down = pltpu.roll(u, n - 1, 0)
        sides = pltpu.roll(u, 1, 1) + pltpu.roll(u, width - 1, 1)
        return u + kappa * (up + down + sides - 4.0 * u) - 0.5 * speed * (down - up)

    def stencil(l):
        kappa, speed = cext[0], cext[1]
        u = substep(ext[l], kappa, speed)
        return substep(u, kappa, speed)[top:low]

    fo[0, 0] = stencil(0)

    def pack(part, row):
        hi, lo = split(row)
        stacked = jnp.concatenate([hi, lo], axis=0)
        for t in range(ntab):
            r = matmul(stacked, thi[t])
            r = r[:rows] + r[rows:] + matmul(hi, tlo[t])
            here = slice(t * rows, (t + 1) * rows)
            pthi[here, :], ptlo[here, :] = split(r)
        out = matmul(mmat[...], pthi[...]) + matmul(mmat[...], ptlo[...])
        send[part] = out.reshape(send.shape[1:])

    def ship(part, to):
        def one(k, c):
            t = lax.rem(tile + k, n_tile)
            pltpu.make_async_remote_copy(
                src_ref=send.at[part, t if to == ocean_sec else flipped(t)],
                dst_ref=recv.at[part, tile // 8, parity, sec * in_plane + lax.rem(tile // 2, in_plane)],
                send_sem=fs_sem.at[part],
                recv_sem=fr_sem.at[part, tile // 8],
                device_id=(to, t),
                device_id_type=pl.DeviceIdType.MESH,
            ).start()
            return c

        if to == ocean_sec:
            lax.fori_loop(0, n_tile, one, 0)
            return

        @pl.when(is_relay)
        def _():
            pltpu.make_async_copy(
                send.at[part, flipped(tile)],
                recv.at[part, tile // 8, parity, sec * in_plane + lax.rem(tile // 2, in_plane)],
                fr_sem.at[part, tile // 8],
            ).start()
            lax.fori_loop(1, n_tile, one, 0)

        @pl.when(jnp.logical_not(is_relay))
        def _():
            lax.fori_loop(0, n_tile, one, 0)

    def shipped(part, kept):
        sent = send.at[part, kept:n_tile]
        pltpu.make_async_copy(sent, sent, fs_sem.at[part]).wait()

    def gather(part):
        flux = jnp.zeros((rows, width), F32)
        for z in range(PLANES):
            came = recv.at[part, z, :, 0:filled]
            pltpu.make_async_copy(came, came, fr_sem.at[part, z]).wait()
            hi, lo = split(recv[part, z].reshape(4 * rows, width))
            flux = flux + matmul(smat[z], hi) + matmul(smat[z], lo)
        return flux

    def give_back(first_k, last_k):
        ocean_tile = flipped(tile)

        def one(k, c):
            i = lax.rem(k, 16)
            z = 2 * (k // 16) + lax.rem(i // 4 + tile // 8, 2)
            t = 8 * z + 2 * lax.rem(i, 4) + i // 8

            z2 = 2 * (k // 16) + lax.rem(i // 8 + tile // 8, 2)
            t2 = 8 * z2 + 2 * lax.rem(i // 2 + tile // 2, 4) + lax.rem(i, 2)

            def to(a, t):
                return pltpu.make_async_remote_copy(
                    src_ref=ret.at[a * n_tile + lax.rem(t, 2) * half + t // 2],
                    dst_ref=arr.at[ocean_tile],
                    send_sem=bs_sem,
                    recv_sem=br_sem,
                    device_id=(a, t),
                    device_id_type=pl.DeviceIdType.MESH,
                )

            @pl.when(t != tile)
            def _():
                to(relay_sec, t).start()

            to(0, t).start()
            to(near_sec, t2).start()
            return c

        lax.fori_loop(first_k, last_k, one, 0)

    def keep_own():
        ocean_tile = flipped(tile)
        pltpu.make_async_copy(
            ret.at[relay_sec * n_tile + parity * half + tile // 2], arr.at[ocean_tile], br_sem
        ).start()

    @pl.when(jnp.logical_not(is_ocean))
    def _():
        pack(0, fo[0, 0])

        @pl.when(jnp.logical_not(is_relay))
        def _():
            pl.semaphore_wait(k_sem, 1)

        ship(0, relay_sec)

        @pl.when(is_relay)
        def _():
            pl.semaphore_wait(h_sem, 1)
            greet(o_sem, 0, tile)
            greet(o_sem, near_sec, flipped(tile))

        other_levels()
        pack(1, fo[0, 0] - fo[0, 1])


        @pl.when(jnp.logical_not(is_relay))
        def _():
            shipped(0, 0)

        @pl.when(is_relay)
        def _():
            shipped(0, 1)

        @pl.when(jnp.logical_not(is_relay))
        def _():
            pl.semaphore_wait(o_sem, 1)

        ship(1, ocean_sec)

        @pl.when(is_relay)
        def _():
            place_all(flipped(tile))

        for t in range(ntab):
            hi, lo = split(tab[t].T)
            tthi[t] = hi
            ttlo[t] = lo

        @pl.when(is_relay)
        def _():
            mask_copy().wait_recv()
            base_copy().wait_recv()
            water = far_mask[...].astype(F32)
            flux = gather(0)
            flux0[...] = flux
            flux_copy().start()
            hi, lo = split(water * (base[...] + forcing_rate * water * flux))
            both = jnp.concatenate([hi, lo], axis=0)
            count = half * cap // 2
            for low_high in range(2):
                for a in range(n_atm):
                    for h in range(2):
                        n = 2 * h + low_high
                        ret[a * n_tile + n * 8 : a * n_tile + n * 8 + 8] = matmul(
                            rmat[a, n * count : (n + 1) * count], both
                        ).reshape(8, cap, width)
                give_back(low_high * half, (low_high + 1) * half)
            keep_own()

        pltpu.make_async_copy(arr, arr, br_sem).wait()
        uhi, ulo = split(arr[...].reshape(n_tile * cap, width))
        v = matmul(mtmat[...], uhi) + matmul(mtmat[...], ulo)
        total = jnp.zeros((rows, width), F32)
        for t in range(ntab):
            vhi, vlo = split(v[t * rows : (t + 1) * rows])
            r = matmul(jnp.concatenate([vhi, vlo], axis=0), tthi[t])
            total = total + r[:rows] + r[rows:] + matmul(vhi, ttlo[t])
        su[0] = total

        shipped(1, 0)

        @pl.when(is_relay)
        def _():
            others = ret.at[1 : n_atm * n_tile]
            pltpu.make_async_copy(others, others, bs_sem).wait()
            flux_copy().wait_send()

    @pl.when(is_ocean)
    def _():
        base[...] = fo[0, 0]
        base_copy().start()
        place_all(tile)
        other_levels()
        water = mask[...].astype(F32)
        flux_copy().wait_recv()
        first = fo[0, 0] + forcing_rate * water * flux0[...]
        fo[0, 0] = first
        su[0] = water * first
        fo[0, 1] = fo[0, 1] + forcing_rate * water * gather(1)
        mask_copy().wait_send()
        base_copy().wait_send()


def store(fields, surface, fields_out, surface_out, sems):
    copies = [
        pltpu.make_async_copy(fields, fields_out, sems.at[0]),
        pltpu.make_async_copy(surface, surface_out, sems.at[1]),
    ]
    for copy in copies:
        copy.start()
    for copy in copies:
        copy.wait()


def local(fields, coefficients, owner_tile, dest_block, table_index, tables, land_mask):
    n_sec = lax.axis_size("sec")
    n_tile = lax.axis_size("tile")
    _, levels, rows, width = fields.shape
    blocks, fan_out = owner_tile.shape
    ntab = tables.shape[0]
    cap = 2 * fan_out * rows // n_tile
    n_atm = n_sec - 1
    half = n_tile // 2
    padded = rows + 2 * PAD
    slots = n_tile * cap
    scratch = [
        pltpu.VMEM((levels, padded, width), F32),
        pltpu.VMEM((2, padded, width), F32),
        pltpu.VMEM((fan_out, blocks), jnp.int32),
        pltpu.VMEM((fan_out, blocks), jnp.int32),
        pltpu.VMEM((fan_out, blocks), jnp.int32),
        pltpu.VMEM((ntab, width, width), F32),
        pltpu.VMEM((rows, width), jnp.int32),
        pltpu.VMEM((2, 2, 8, width), F32),
        pltpu.VMEM((2, 2, 8, width), F32),
        pltpu.VMEM((ntab, width, width), BF16),
        pltpu.VMEM((ntab, width, width), BF16),
        pltpu.VMEM((ntab, width, width), BF16),
        pltpu.VMEM((ntab, width, width), BF16),
        pltpu.VMEM((slots, ntab * rows), BF16),
        pltpu.VMEM((ntab * rows, slots), BF16),
        pltpu.VMEM((ntab * rows, width), BF16),
        pltpu.VMEM((ntab * rows, width), BF16),
        pltpu.VMEM((2, n_tile, cap, width), F32),
        pltpu.VMEM((2, PLANES, 2, 16, cap, width), F32),
        pltpu.VMEM((half, 2 * rows), F32),
        pltpu.VMEM((half, 2 * rows), F32),
        pltpu.VMEM((half, 2 * rows), F32),
        pltpu.VMEM((half, 2 * rows), F32),
        pltpu.VMEM((PLANES, 2 * rows, 2 * rows), F32),
        pltpu.VMEM((PLANES, rows, 4 * rows), BF16),
        pltpu.VMEM((n_atm, slots, 2 * rows), BF16),
        pltpu.VMEM((n_atm * n_tile, cap, width), F32),
        pltpu.VMEM((n_tile, cap, width), F32),
        pltpu.VMEM((rows, width), F32),
        pltpu.VMEM((rows, width), F32),
        pltpu.VMEM((rows, width), jnp.int32),
        pltpu.SemaphoreType.DMA((7,)),
        pltpu.SemaphoreType.DMA((2, 2)),
        pltpu.SemaphoreType.DMA((2, 2)),
        pltpu.SemaphoreType.DMA((2,)),
        pltpu.SemaphoreType.DMA((2, PLANES)),
        pltpu.SemaphoreType.DMA,
        pltpu.SemaphoreType.DMA,
        pltpu.SemaphoreType.REGULAR,
        pltpu.SemaphoreType.REGULAR,
        pltpu.SemaphoreType.REGULAR,
        pltpu.SemaphoreType.REGULAR,
        pltpu.SemaphoreType.REGULAR,
        pltpu.SemaphoreType.DMA((3,)),
        pltpu.SemaphoreType.DMA((3,)),
    ]
    operands = (fields, coefficients, owner_tile.T, dest_block.T, table_index.T, tables, land_mask)
    shapes = (
        jax.ShapeDtypeStruct(fields.shape, F32),
        jax.ShapeDtypeStruct((1, rows, width), F32),
    )
    results = pl.pallas_call(
        functools.partial(kernel, n_sec, n_tile, cap),
        out_shape=shapes,
        in_specs=[pl.BlockSpec(memory_space=pltpu.HBM)] * 7,
        out_specs=(
            pl.BlockSpec(memory_space=pltpu.VMEM),
            pl.BlockSpec(memory_space=pltpu.VMEM),
        ),
        scratch_shapes=scratch,
        compiler_params=pltpu.CompilerParams(
            collective_id=0, has_side_effects=True, vmem_limit_bytes=32 * 1024 * 1024
        ),
    )(*(pltpu.with_memory_space_constraint(x, pltpu.HBM) for x in operands))
    return pl.pallas_call(
        store,
        out_shape=shapes,
        in_specs=[pl.BlockSpec(memory_space=pltpu.VMEM)] * 2,
        out_specs=(pl.BlockSpec(memory_space=pl.ANY),) * 2,
        scratch_shapes=[pltpu.SemaphoreType.DMA((2,))],
    )(*(pltpu.with_memory_space_constraint(x, pltpu.VMEM) for x in results))


def solution(mesh):
    placed = (
        P("sec", None, "tile", None),
        P("sec", None, "tile", None),
        P(),
        P(),
        P(),
        P(),
        P("tile", None),
    )
    return jax.shard_map(
        local,
        mesh=mesh,
        in_specs=placed,
        out_specs=(P("sec", None, "tile", None), P("sec", "tile", None)),
        check_vma=False,
    )
```

```python
import functools

import jax
import jax.numpy as jnp
from jax import lax
from jax.experimental import pallas as pl
from jax.experimental.pallas import tpu as pltpu
from jax.sharding import PartitionSpec as P

forcing_rate = 0.5

F32 = jnp.float32
BF16 = jnp.bfloat16
PAD = 8
PLANES = 4


def matmul(a, b):
    return lax.dot_general(a, b, (((1,), (0,)), ((), ())), preferred_element_type=F32)


def split(x):
    hi = x.astype(BF16)
    return hi, (x - hi.astype(F32)).astype(BF16)


def iota(shape, dim):
    return lax.broadcasted_iota(jnp.int32, shape, dim)


def kernel(
    n_sec, n_tile, cap,
    fields, coef, ot_in, db_in, ti_in, tables, mask_in,
    fo, su,
    ext, cext, ot, db, ti, tab, mask, hsend, hrecv,
    thi, tlo, tthi, ttlo, mmat, mtmat, pthi, ptlo, send, recv,
    x0, x1, d0, d1, hots, smat, rmat, ret, arr, base, flux0, far_mask,
    in_sem, hs_sem, hr_sem, fs_sem, fr_sem, bs_sem, br_sem, o_sem, p_sem, k_sem, g_sem, h_sem, cs_sem, cr_sem,
):
    n_atm = n_sec - 1
    ocean_sec = n_sec - 1
    near_sec = n_sec - 2
    relay_sec = near_sec - 1
    half = n_tile // 2
    in_plane = n_tile // PLANES // 2
    filled = n_atm * in_plane
    levels, rows, width = fo.shape[1:]
    ntab = tables.shape[0]
    top, low = PAD, PAD + rows
    sec = lax.axis_index("sec")
    tile = lax.axis_index("tile")
    upper = lax.rem(tile + n_tile - 1, n_tile)
    lower = lax.rem(tile + 1, n_tile)
    is_ocean = sec == ocean_sec
    is_near = sec == near_sec
    is_relay = sec == relay_sec
    parity = lax.rem(tile, 2)

    def flipped(t):
        return t + 1 - 2 * lax.rem(t, 2)


    barrier = pltpu.get_barrier_semaphore()
    has_upper, has_lower = tile > 0, tile < n_tile - 1
    neighbours = has_upper.astype(jnp.int32) + has_lower.astype(jnp.int32)

    def greet(semaphore, s, t):
        pl.semaphore_signal(semaphore, inc=1, device_id=(s, t), device_id_type=pl.DeviceIdType.MESH)

    @pl.when(jnp.logical_not(has_upper))
    def _():
        hrecv[0] = jnp.zeros_like(hrecv[0])

    @pl.when(jnp.logical_not(has_lower))
    def _():
        hrecv[1] = jnp.zeros_like(hrecv[1])

    @pl.when(has_upper)
    def _():
        greet(barrier, sec, upper)

    @pl.when(has_lower)
    def _():
        greet(barrier, sec, lower)

    def greet_plane(semaphore):
        def one(k, c):
            z = lax.rem(tile // 8 + k // 4, 4)
            x = lax.rem(tile // 2 + lax.rem(k, 4), 4)
            greet(semaphore, sec, z * 8 + x * 2 + parity)
            return c

        lax.fori_loop(1, half, one, 0)

    @pl.when(is_relay)
    def _():
        greet_plane(barrier)
        greet(barrier, ocean_sec, flipped(tile))

    @pl.when(sec == 0)
    def _():
        greet(barrier, relay_sec, tile)

    @pl.when(is_near | is_ocean)
    def _():
        greet(barrier, relay_sec, flipped(tile))

    def load(number, src, dst):
        return pltpu.make_async_copy(src, dst, in_sem.at[number])

    loads = [
        load(0, fields.at[0], ext.at[:, top:low, :]),
        load(1, coef.at[0], cext.at[:, top:low, :]),
        load(2, ot_in, ot),
        load(3, db_in, db),
        load(4, ti_in, ti),
        load(5, tables, tab),
        load(6, mask_in, mask),
    ]
    for copy in loads:
        copy.start()

    def clear(part):
        for z in range(PLANES):
            for h in range(2):
                recv[part, z, h, filled:] = jnp.zeros_like(recv[part, z, h, filled:])

    @pl.when(is_relay)
    def _():
        clear(0)

    @pl.when(is_ocean)
    def _():
        clear(1)

    zero = jnp.zeros((PAD, width), F32)
    for l in range(levels):
        ext[l, 0:top, :] = zero
        ext[l, low : low + PAD, :] = zero
    for c in range(2):
        cext[c, 0:top, :] = zero
        cext[c, low : low + PAD, :] = zero
        hsend[c, 0] = zero
        hsend[c, 1] = zero

    loads[0].wait()
    for l in range(levels):
        group, at = (0, 0) if l == 0 else (1, 2 * l - 2)
        hsend[0, group, at : at + 2, :] = ext[l, top : top + 2, :]
        hsend[1, group, at : at + 2, :] = ext[l, low - 2 : low, :]
    loads[1].wait()
    for c in range(2):
        hsend[0, 0, 2 + c : 3 + c, :] = cext[c, top : top + 1, :]
        hsend[1, 0, 2 + c : 3 + c, :] = cext[c, low - 1 : low, :]

    @pl.when(is_relay)
    def _():
        pl.semaphore_wait(barrier, neighbours + half + 2)

    @pl.when(is_ocean)
    def _():
        pl.semaphore_wait(barrier, neighbours + 1)

    @pl.when(jnp.logical_not(is_relay | is_ocean))
    def _():
        pl.semaphore_wait(barrier, neighbours)

    def column_copy(src, dst, number, to):
        return pltpu.make_async_remote_copy(
            src_ref=src,
            dst_ref=dst,
            send_sem=cs_sem.at[number],
            recv_sem=cr_sem.at[number],
            device_id=(to, flipped(tile)),
            device_id_type=pl.DeviceIdType.MESH,
        )

    def mask_copy():
        return column_copy(mask, far_mask, 0, relay_sec)

    def base_copy():
        return column_copy(base, base, 1, relay_sec)

    def flux_copy():
        return column_copy(flux0, flux0, 2, ocean_sec)

    def halo(way, to, group):
        return pltpu.make_async_remote_copy(
            src_ref=hsend.at[way, group],
            dst_ref=hrecv.at[1 - way, group],
            send_sem=hs_sem.at[way, group],
            recv_sem=hr_sem.at[1 - way, group],
            device_id=(sec, to),
            device_id_type=pl.DeviceIdType.MESH,
        )

    for group in range(2):

        @pl.when(has_upper)
        def _():
            halo(0, upper, group).start()

        @pl.when(has_lower)
        def _():
            halo(1, lower, group).start()

    def halo_wait(group):
        @pl.when(has_upper)
        def _():
            halo(0, upper, group).wait_send()
            halo(1, lower, group).wait_recv()

        @pl.when(has_lower)
        def _():
            halo(1, lower, group).wait_send()
            halo(0, upper, group).wait_recv()

    @pl.when(is_ocean)
    def _():
        loads[6].wait()
        mask_copy().start()

    @pl.when(is_relay)
    def _():
        greet(p_sem, sec, flipped(tile))
        greet_plane(g_sem)

    loads[2].wait()
    loads[3].wait()
    loads[4].wait()
    loads[5].wait()

    @pl.when(jnp.logical_not(is_ocean))
    def _():
        loads[6].wait()


    lane = iota((8, 128), 1)
    left = lane < 64

    def place(number, a, owner):
        for kk in range(half):
            cols = pl.ds(pl.multiple_of((a * half + kk) * 128, 128), 128)
            x0[kk : kk + 1, :] = ot[0:1, cols].astype(F32)
            x1[kk : kk + 1, :] = ot[1:2, cols].astype(F32)
            d0[kk : kk + 1, :] = db[0:1, cols].astype(F32) + 1.0
            d1[kk : kk + 1, :] = db[1:2, cols].astype(F32) + 1.0
        src, dst = iota((128, 128), 0), iota((128, 128), 1)
        same = (src // 64) == (dst // 64)
        both = same.astype(F32).astype(BF16)
        before = (same & (src < dst)).astype(F32).astype(BF16)
        mine_of = owner.astype(F32)
        mine0 = x0[...] == mine_of
        mine1 = x1[...] == mine_of
        m0 = mine0.astype(F32).astype(BF16)
        m1 = mine1.astype(F32).astype(BF16)
        x0[...] = jnp.where(mine0, matmul(m0, before), -1.0)
        x1[...] = jnp.where(mine1, matmul(m1, before) + matmul(m0, both), -1.0)
        slot = iota((cap, 128), 0).astype(F32)
        parts = []
        for kk in range(half):
            parts.append(
                jnp.where(x0[kk : kk + 1, :] == slot, d0[kk : kk + 1, :], 0.0)
                + jnp.where(x1[kk : kk + 1, :] == slot, d1[kk : kk + 1, :], 0.0)
            )
        named = jnp.concatenate(parts, axis=0).astype(BF16)
        count = half * cap
        lane_c = iota((count, 128), 1)
        left_c = lane_c < 64
        want = (lax.rem(lane_c, 64) + 1).astype(F32)
        hot = (matmul(named, both) == want).astype(F32)
        width_z = in_plane * cap
        for z in range(PLANES):
            hots[z, a * width_z : (a + 1) * width_z, :] = hot[z * width_z : (z + 1) * width_z]
        other = pltpu.roll(hot, 64, 1)
        rmat[number, 0:count, :] = jnp.where(left_c, hot, other).astype(BF16)
        rmat[number, count : 2 * count, :] = jnp.where(left_c, other, hot).astype(BF16)

    def place_all(owner):
        hots[:, filled * cap :, :] = jnp.zeros_like(hots[:, filled * cap :, :])
        for a in range(n_atm):
            place(a, a, owner)
        for z in range(PLANES):
            turned = hots[z].T
            smat[z, :, 0:128] = turned[0:64].astype(BF16)
            smat[z, :, 128:256] = turned[64:128].astype(BF16)

    @pl.when(jnp.logical_not(is_ocean))
    def _():
        number = sec * n_tile + tile
        cols = pl.ds(pl.multiple_of((number // 2) * 128, 128), 128)

        def pairs(ref):
            r0 = jnp.broadcast_to(ref[0:1, cols].astype(F32), (8, 128))
            r1 = jnp.broadcast_to(ref[1:2, cols].astype(F32), (8, 128))
            even = jnp.where(left, r0, pltpu.roll(r1, 64, 1))
            odd = jnp.where(left, pltpu.roll(r0, 64, 1), r1)
            return jnp.where(parity == 0, even, odd)

        own, entry = pairs(ot), pairs(ti)
        across = jnp.broadcast_to(own[0:1], (128, 128))
        earlier = (across.T == across) & (iota((128, 128), 0) < iota((128, 128), 1))
        rank = jnp.sum(earlier.astype(F32), axis=0, keepdims=True)
        target = own * float(cap) + jnp.broadcast_to(rank, (8, 128))

        def doubled(v):
            turned = pltpu.roll(v, 64, 1)
            return jnp.where(left, v, turned), jnp.where(left, turned, v)

        t0, t1 = doubled(target)
        e0, e1 = doubled(entry)
        slots = iota((n_tile * cap, 128), 0).astype(F32)
        for b in range(ntab // 2):
            here = (lane // 64 + 2 * b).astype(F32)
            v0 = jnp.where(e0 == here, t0, -1.0)
            v1 = jnp.where(e1 == here, t1, -1.0)
            hot = ((slots == v0[0:1]) | (slots == v1[0:1])).astype(F32)
            mmat[:, 128 * b : 128 * (b + 1)] = hot.astype(BF16)
            mtmat[128 * b : 128 * (b + 1), :] = hot.T.astype(BF16)
        for t in range(ntab):
            hi, lo = split(tab[t])
            thi[t] = hi
            tlo[t] = lo

    @pl.when(is_relay)
    def _():
        pl.semaphore_wait(p_sem, 1)
        greet(k_sem, 0, tile)
        greet(k_sem, near_sec, flipped(tile))

    @pl.when(is_relay)
    def _():
        pl.semaphore_wait(g_sem, half - 1)
        greet(h_sem, sec, flipped(tile))

    halo_wait(0)
    above, below = hrecv[0, 0], hrecv[1, 0]
    ext[0, top - 2 : top, :] = above[0:2]
    ext[0, low : low + 2, :] = below[0:2]
    for c in range(2):
        cext[c, top - 1 : top, :] = above[2 + c : 3 + c]
        cext[c, low : low + 1, :] = below[2 + c : 3 + c]

    def other_levels():
        halo_wait(1)
        above, below = hrecv[0, 1], hrecv[1, 1]
        for l in range(1, levels):
            ext[l, top - 2 : top, :] = above[2 * l - 2 : 2 * l]
            ext[l, low : low + 2, :] = below[2 * l - 2 : 2 * l]
            fo[0, l] = stencil(l)

    def substep(u, kappa, speed):
        n = u.shape[0]
        up = pltpu.roll(u, 1, 0)
        down = pltpu.roll(u, n - 1, 0)
        sides = pltpu.roll(u, 1, 1) + pltpu.roll(u, width - 1, 1)
        return u + kappa * (up + down + sides - 4.0 * u) - 0.5 * speed * (down - up)

    def stencil(l):
        kappa, speed = cext[0], cext[1]
        u = substep(ext[l], kappa, speed)
        return substep(u, kappa, speed)[top:low]

    fo[0, 0] = stencil(0)

    def pack(part, row):
        hi, lo = split(row)
        stacked = jnp.concatenate([hi, lo], axis=0)
        for t in range(ntab):
            r = matmul(stacked, thi[t])
            r = r[:rows] + r[rows:] + matmul(hi, tlo[t])
            here = slice(t * rows, (t + 1) * rows)
            pthi[here, :], ptlo[here, :] = split(r)
        out = matmul(mmat[...], pthi[...]) + matmul(mmat[...], ptlo[...])
        send[part] = out.reshape(send.shape[1:])

    def ship(part, to):
        def one(k, c):
            t = lax.rem(tile + k, n_tile)
            pltpu.make_async_remote_copy(
                src_ref=send.at[part, t if to == ocean_sec else flipped(t)],
                dst_ref=recv.at[part, tile // 8, parity, sec * in_plane + lax.rem(tile // 2, in_plane)],
                send_sem=fs_sem.at[part],
                recv_sem=fr_sem.at[part, tile // 8],
                device_id=(to, t),
                device_id_type=pl.DeviceIdType.MESH,
            ).start()
            return c

        if to == ocean_sec:
            lax.fori_loop(0, n_tile, one, 0)
            return

        @pl.when(is_relay)
        def _():
            pltpu.make_async_copy(
                send.at[part, flipped(tile)],
                recv.at[part, tile // 8, parity, sec * in_plane + lax.rem(tile // 2, in_plane)],
                fr_sem.at[part, tile // 8],
            ).start()
            lax.fori_loop(1, n_tile, one, 0)

        @pl.when(jnp.logical_not(is_relay))
        def _():
            lax.fori_loop(0, n_tile, one, 0)

    def shipped(part, kept):
        sent = send.at[part, kept:n_tile]
        pltpu.make_async_copy(sent, sent, fs_sem.at[part]).wait()

    def gather(part):
        flux = jnp.zeros((rows, width), F32)
        for z in range(PLANES):
            came = recv.at[part, z, :, 0:filled]
            pltpu.make_async_copy(came, came, fr_sem.at[part, z]).wait()
            hi, lo = split(recv[part, z].reshape(4 * rows, width))
            flux = flux + matmul(smat[z], hi) + matmul(smat[z], lo)
        return flux

    def give_back(first_k, last_k):
        ocean_tile = flipped(tile)

        def one(k, c):
            i = lax.rem(k, 16)
            z = 2 * (k // 16) + lax.rem(i // 4 + tile // 8, 2)
            t = 8 * z + 2 * lax.rem(i, 4) + i // 8

            z2 = 2 * (k // 16) + lax.rem(i // 8 + tile // 8, 2)
            t2 = 8 * z2 + 2 * lax.rem(i // 2 + tile // 2, 4) + lax.rem(i, 2)

            def to(a, t):
                return pltpu.make_async_remote_copy(
                    src_ref=ret.at[a * n_tile + lax.rem(t, 2) * half + t // 2],
                    dst_ref=arr.at[ocean_tile],
                    send_sem=bs_sem,
                    recv_sem=br_sem,
                    device_id=(a, t),
                    device_id_type=pl.DeviceIdType.MESH,
                )

            @pl.when(t != tile)
            def _():
                to(relay_sec, t).start()

            to(0, t).start()
            to(near_sec, t2).start()
            return c

        lax.fori_loop(first_k, last_k, one, 0)

    def keep_own():
        ocean_tile = flipped(tile)
        pltpu.make_async_copy(
            ret.at[relay_sec * n_tile + parity * half + tile // 2], arr.at[ocean_tile], br_sem
        ).start()

    @pl.when(jnp.logical_not(is_ocean))
    def _():
        pack(0, fo[0, 0])

        @pl.when(jnp.logical_not(is_relay))
        def _():
            pl.semaphore_wait(k_sem, 1)

        ship(0, relay_sec)

        @pl.when(is_relay)
        def _():
            pl.semaphore_wait(h_sem, 1)
            greet(o_sem, 0, tile)
            greet(o_sem, near_sec, flipped(tile))

        other_levels()
        pack(1, fo[0, 0] - fo[0, 1])


        @pl.when(jnp.logical_not(is_relay))
        def _():
            shipped(0, 0)

        @pl.when(is_relay)
        def _():
            shipped(0, 1)

        @pl.when(jnp.logical_not(is_relay))
        def _():
            pl.semaphore_wait(o_sem, 1)

        ship(1, ocean_sec)

        @pl.when(is_relay)
        def _():
            place_all(flipped(tile))

        for t in range(ntab):
            hi, lo = split(tab[t].T)
            tthi[t] = hi
            ttlo[t] = lo

        @pl.when(is_relay)
        def _():
            mask_copy().wait_recv()
            base_copy().wait_recv()
            water = far_mask[...].astype(F32)
            flux = gather(0)
            flux0[...] = flux
            flux_copy().start()
            hi, lo = split(water * (base[...] + forcing_rate * water * flux))
            both = jnp.concatenate([hi, lo], axis=0)
            count = half * cap // 2
            for low_high in range(2):
                for a in range(n_atm):
                    for h in range(2):
                        n = 2 * h + low_high
                        ret[a * n_tile + n * 8 : a * n_tile + n * 8 + 8] = matmul(
                            rmat[a, n * count : (n + 1) * count], both
                        ).reshape(8, cap, width)
                give_back(low_high * half, (low_high + 1) * half)
            keep_own()

        pltpu.make_async_copy(arr, arr, br_sem).wait()
        uhi, ulo = split(arr[...].reshape(n_tile * cap, width))
        v = matmul(mtmat[...], uhi) + matmul(mtmat[...], ulo)
        total = jnp.zeros((rows, width), F32)
        for t in range(ntab):
            vhi, vlo = split(v[t * rows : (t + 1) * rows])
            r = matmul(jnp.concatenate([vhi, vlo], axis=0), tthi[t])
            total = total + r[:rows] + r[rows:] + matmul(vhi, ttlo[t])
        su[0] = total

        shipped(1, 0)

        @pl.when(is_relay)
        def _():
            others = ret.at[1 : n_atm * n_tile]
            pltpu.make_async_copy(others, others, bs_sem).wait()
            flux_copy().wait_send()

    @pl.when(is_ocean)
    def _():
        base[...] = fo[0, 0]
        base_copy().start()
        place_all(tile)
        other_levels()
        water = mask[...].astype(F32)
        flux_copy().wait_recv()
        first = fo[0, 0] + forcing_rate * water * flux0[...]
        fo[0, 0] = first
        su[0] = water * first
        fo[0, 1] = fo[0, 1] + forcing_rate * water * gather(1)
        mask_copy().wait_send()
        base_copy().wait_send()


def store(fields, surface, fields_out, surface_out, sems):
    copies = [
        pltpu.make_async_copy(fields, fields_out, sems.at[0]),
        pltpu.make_async_copy(surface, surface_out, sems.at[1]),
    ]
    for copy in copies:
        copy.start()
    for copy in copies:
        copy.wait()


def local(fields, coefficients, owner_tile, dest_block, table_index, tables, land_mask):
    n_sec = lax.axis_size("sec")
    n_tile = lax.axis_size("tile")
    _, levels, rows, width = fields.shape
    blocks, fan_out = owner_tile.shape
    ntab = tables.shape[0]
    cap = 2 * fan_out * rows // n_tile
    n_atm = n_sec - 1
    half = n_tile // 2
    padded = rows + 2 * PAD
    slots = n_tile * cap
    scratch = [
        pltpu.VMEM((levels, padded, width), F32),
        pltpu.VMEM((2, padded, width), F32),
        pltpu.VMEM((fan_out, blocks), jnp.int32),
        pltpu.VMEM((fan_out, blocks), jnp.int32),
        pltpu.VMEM((fan_out, blocks), jnp.int32),
        pltpu.VMEM((ntab, width, width), F32),
        pltpu.VMEM((rows, width), jnp.int32),
        pltpu.VMEM((2, 2, 8, width), F32),
        pltpu.VMEM((2, 2, 8, width), F32),
        pltpu.VMEM((ntab, width, width), BF16),
        pltpu.VMEM((ntab, width, width), BF16),
        pltpu.VMEM((ntab, width, width), BF16),
        pltpu.VMEM((ntab, width, width), BF16),
        pltpu.VMEM((slots, ntab * rows), BF16),
        pltpu.VMEM((ntab * rows, slots), BF16),
        pltpu.VMEM((ntab * rows, width), BF16),
        pltpu.VMEM((ntab * rows, width), BF16),
        pltpu.VMEM((2, n_tile, cap, width), F32),
        pltpu.VMEM((2, PLANES, 2, 16, cap, width), F32),
        pltpu.VMEM((half, 2 * rows), F32),
        pltpu.VMEM((half, 2 * rows), F32),
        pltpu.VMEM((half, 2 * rows), F32),
        pltpu.VMEM((half, 2 * rows), F32),
        pltpu.VMEM((PLANES, 2 * rows, 2 * rows), F32),
        pltpu.VMEM((PLANES, rows, 4 * rows), BF16),
        pltpu.VMEM((n_atm, slots, 2 * rows), BF16),
        pltpu.VMEM((n_atm * n_tile, cap, width), F32),
        pltpu.VMEM((n_tile, cap, width), F32),
        pltpu.VMEM((rows, width), F32),
        pltpu.VMEM((rows, width), F32),
        pltpu.VMEM((rows, width), jnp.int32),
        pltpu.SemaphoreType.DMA((7,)),
        pltpu.SemaphoreType.DMA((2, 2)),
        pltpu.SemaphoreType.DMA((2, 2)),
        pltpu.SemaphoreType.DMA((2,)),
        pltpu.SemaphoreType.DMA((2, PLANES)),
        pltpu.SemaphoreType.DMA,
        pltpu.SemaphoreType.DMA,
        pltpu.SemaphoreType.REGULAR,
        pltpu.SemaphoreType.REGULAR,
        pltpu.SemaphoreType.REGULAR,
        pltpu.SemaphoreType.REGULAR,
        pltpu.SemaphoreType.REGULAR,
        pltpu.SemaphoreType.DMA((3,)),
        pltpu.SemaphoreType.DMA((3,)),
    ]
    operands = (fields, coefficients, owner_tile.T, dest_block.T, table_index.T, tables, land_mask)
    shapes = (
        jax.ShapeDtypeStruct(fields.shape, F32),
        jax.ShapeDtypeStruct((1, rows, width), F32),
    )
    results = pl.pallas_call(
        functools.partial(kernel, n_sec, n_tile, cap),
        out_shape=shapes,
        in_specs=[pl.BlockSpec(memory_space=pltpu.HBM)] * 7,
        out_specs=(
            pl.BlockSpec(memory_space=pltpu.VMEM),
            pl.BlockSpec(memory_space=pltpu.VMEM),
        ),
        scratch_shapes=scratch,
        compiler_params=pltpu.CompilerParams(
            collective_id=0, has_side_effects=True, vmem_limit_bytes=32 * 1024 * 1024
        ),
    )(*(pltpu.with_memory_space_constraint(x, pltpu.HBM) for x in operands))
    return pl.pallas_call(
        store,
        out_shape=shapes,
        in_specs=[pl.BlockSpec(memory_space=pltpu.VMEM)] * 2,
        out_specs=(pl.BlockSpec(memory_space=pl.ANY),) * 2,
        scratch_shapes=[pltpu.SemaphoreType.DMA((2,))],
    )(*(pltpu.with_memory_space_constraint(x, pltpu.VMEM) for x in results))


def solution(mesh):
    placed = (
        P("sec", None, "tile", None),
        P("sec", None, "tile", None),
        P(),
        P(),
        P(),
        P(),
        P("tile", None),
    )
    return jax.shard_map(
        local,
        mesh=mesh,
        in_specs=placed,
        out_specs=(P("sec", None, "tile", None), P("sec", "tile", None)),
        check_vma=False,
    )
```

```python
import functools

import jax
import jax.numpy as jnp
from jax import lax
from jax.experimental import pallas as pl
from jax.experimental.pallas import tpu as pltpu
from jax.sharding import PartitionSpec as P

forcing_rate = 0.5

F32 = jnp.float32
BF16 = jnp.bfloat16
PAD = 8
PLANES = 4


def matmul(a, b):
    return lax.dot_general(a, b, (((1,), (0,)), ((), ())), preferred_element_type=F32)


def split(x):
    hi = x.astype(BF16)
    return hi, (x - hi.astype(F32)).astype(BF16)


def iota(shape, dim):
    return lax.broadcasted_iota(jnp.int32, shape, dim)


def kernel(
    n_sec, n_tile, cap,
    fields, coef, ot_in, db_in, ti_in, tables, mask_in,
    fo, su,
    ext, cext, ot, db, ti, tab, mask, hsend, hrecv,
    thi, tlo, tthi, ttlo, mmat, mtmat, pthi, ptlo, send, recv,
    x0, x1, d0, d1, hots, smat, rmat, ret, arr, base, flux0, far_mask,
    in_sem, hs_sem, hr_sem, fs_sem, fr_sem, bs_sem, br_sem, o_sem, p_sem, k_sem, g_sem, h_sem, cs_sem, cr_sem,
):
    n_atm = n_sec - 1
    ocean_sec = n_sec - 1
    near_sec = n_sec - 2
    relay_sec = near_sec - 1
    half = n_tile // 2
    in_plane = n_tile // PLANES // 2
    filled = n_atm * in_plane
    levels, rows, width = fo.shape[1:]
    ntab = tables.shape[0]
    top, low = PAD, PAD + rows
    sec = lax.axis_index("sec")
    tile = lax.axis_index("tile")
    upper = lax.rem(tile + n_tile - 1, n_tile)
    lower = lax.rem(tile + 1, n_tile)
    is_ocean = sec == ocean_sec
    is_near = sec == near_sec
    is_relay = sec == relay_sec
    parity = lax.rem(tile, 2)

    def flipped(t):
        return t + 1 - 2 * lax.rem(t, 2)


    def load(number, src, dst):
        return pltpu.make_async_copy(src, dst, in_sem.at[number])

    loads = [
        load(0, fields.at[0], ext.at[:, top:low, :]),
        load(1, coef.at[0], cext.at[:, top:low, :]),
        load(2, ot_in, ot),
        load(3, db_in, db),
        load(4, ti_in, ti),
        load(5, tables, tab),
        load(6, mask_in, mask),
    ]
    for copy in loads:
        copy.start()

    barrier = pltpu.get_barrier_semaphore()
    has_upper, has_lower = tile > 0, tile < n_tile - 1
    neighbours = has_upper.astype(jnp.int32) + has_lower.astype(jnp.int32)

    def greet(semaphore, s, t):
        pl.semaphore_signal(semaphore, inc=1, device_id=(s, t), device_id_type=pl.DeviceIdType.MESH)

    @pl.when(jnp.logical_not(has_upper))
    def _():
        hrecv[0] = jnp.zeros_like(hrecv[0])

    @pl.when(jnp.logical_not(has_lower))
    def _():
        hrecv[1] = jnp.zeros_like(hrecv[1])

    def clear(part):
        for z in range(PLANES):
            for h in range(2):
                recv[part, z, h, filled:] = jnp.zeros_like(recv[part, z, h, filled:])

    @pl.when(is_relay)
    def _():
        clear(0)

    @pl.when(is_ocean)
    def _():
        clear(1)

    @pl.when(has_upper)
    def _():
        greet(barrier, sec, upper)

    @pl.when(has_lower)
    def _():
        greet(barrier, sec, lower)

    def greet_plane(semaphore):
        def one(k, c):
            z = lax.rem(tile // 8 + k // 4, 4)
            x = lax.rem(tile // 2 + lax.rem(k, 4), 4)
            greet(semaphore, sec, z * 8 + x * 2 + parity)
            return c

        lax.fori_loop(1, half, one, 0)

    @pl.when(is_relay)
    def _():
        greet_plane(barrier)
        greet(barrier, ocean_sec, flipped(tile))

    @pl.when(sec == 0)
    def _():
        greet(barrier, relay_sec, tile)

    @pl.when(is_near | is_ocean)
    def _():
        greet(barrier, relay_sec, flipped(tile))

    zero = jnp.zeros((PAD, width), F32)
    for l in range(levels):
        ext[l, 0:top, :] = zero
        ext[l, low : low + PAD, :] = zero
    for c in range(2):
        cext[c, 0:top, :] = zero
        cext[c, low : low + PAD, :] = zero
        hsend[c, 8:16, :] = zero

    loads[0].wait()
    for l in range(levels):
        hsend[0, 2 * l : 2 * l + 2, :] = ext[l, top : top + 2, :]
        hsend[1, 2 * l : 2 * l + 2, :] = ext[l, low - 2 : low, :]
    loads[1].wait()
    for c in range(2):
        hsend[0, 8 + c : 9 + c, :] = cext[c, top : top + 1, :]
        hsend[1, 8 + c : 9 + c, :] = cext[c, low - 1 : low, :]

    @pl.when(is_relay)
    def _():
        pl.semaphore_wait(barrier, neighbours + half + 2)

    @pl.when(is_ocean)
    def _():
        pl.semaphore_wait(barrier, neighbours + 1)

    @pl.when(jnp.logical_not(is_relay | is_ocean))
    def _():
        pl.semaphore_wait(barrier, neighbours)

    def column_copy(src, dst, number, to):
        return pltpu.make_async_remote_copy(
            src_ref=src,
            dst_ref=dst,
            send_sem=cs_sem.at[number],
            recv_sem=cr_sem.at[number],
            device_id=(to, flipped(tile)),
            device_id_type=pl.DeviceIdType.MESH,
        )

    def mask_copy():
        return column_copy(mask, far_mask, 0, relay_sec)

    def base_copy():
        return column_copy(base, base, 1, relay_sec)

    def flux_copy():
        return column_copy(flux0, flux0, 2, ocean_sec)

    def halo(way, to):
        return pltpu.make_async_remote_copy(
            src_ref=hsend.at[way],
            dst_ref=hrecv.at[1 - way],
            send_sem=hs_sem.at[way],
            recv_sem=hr_sem.at[1 - way],
            device_id=(sec, to),
            device_id_type=pl.DeviceIdType.MESH,
        )

    halos = [halo(0, upper), halo(1, lower)]

    @pl.when(has_upper)
    def _():
        halos[0].start()

    @pl.when(has_lower)
    def _():
        halos[1].start()

    @pl.when(is_ocean)
    def _():
        loads[6].wait()
        mask_copy().start()

    @pl.when(is_relay)
    def _():
        greet(p_sem, sec, flipped(tile))
        greet_plane(g_sem)

    loads[2].wait()
    loads[3].wait()
    loads[4].wait()
    loads[5].wait()

    @pl.when(jnp.logical_not(is_ocean))
    def _():
        loads[6].wait()


    lane = iota((8, 128), 1)
    left = lane < 64

    def place(number, a, owner):
        for kk in range(half):
            cols = pl.ds(pl.multiple_of((a * half + kk) * 128, 128), 128)
            x0[kk : kk + 1, :] = ot[0:1, cols].astype(F32)
            x1[kk : kk + 1, :] = ot[1:2, cols].astype(F32)
            d0[kk : kk + 1, :] = db[0:1, cols].astype(F32) + 1.0
            d1[kk : kk + 1, :] = db[1:2, cols].astype(F32) + 1.0
        src, dst = iota((128, 128), 0), iota((128, 128), 1)
        same = (src // 64) == (dst // 64)
        both = same.astype(F32).astype(BF16)
        before = (same & (src < dst)).astype(F32).astype(BF16)
        mine_of = owner.astype(F32)
        mine0 = x0[...] == mine_of
        mine1 = x1[...] == mine_of
        m0 = mine0.astype(F32).astype(BF16)
        m1 = mine1.astype(F32).astype(BF16)
        x0[...] = jnp.where(mine0, matmul(m0, before), -1.0)
        x1[...] = jnp.where(mine1, matmul(m1, before) + matmul(m0, both), -1.0)
        slot = iota((cap, 128), 0).astype(F32)
        parts = []
        for kk in range(half):
            parts.append(
                jnp.where(x0[kk : kk + 1, :] == slot, d0[kk : kk + 1, :], 0.0)
                + jnp.where(x1[kk : kk + 1, :] == slot, d1[kk : kk + 1, :], 0.0)
            )
        named = jnp.concatenate(parts, axis=0).astype(BF16)
        count = half * cap
        lane_c = iota((count, 128), 1)
        left_c = lane_c < 64
        want = (lax.rem(lane_c, 64) + 1).astype(F32)
        hot = (matmul(named, both) == want).astype(F32)
        width_z = in_plane * cap
        for z in range(PLANES):
            hots[z, a * width_z : (a + 1) * width_z, :] = hot[z * width_z : (z + 1) * width_z]

        @pl.when(is_relay)
        def _():
            other = pltpu.roll(hot, 64, 1)
            rmat[number, 0:count, :] = jnp.where(left_c, hot, other).astype(BF16)
            rmat[number, count : 2 * count, :] = jnp.where(left_c, other, hot).astype(BF16)

    def place_all(owner):
        hots[:, filled * cap :, :] = jnp.zeros_like(hots[:, filled * cap :, :])
        for a in range(n_atm):
            place(a, a, owner)
        for z in range(PLANES):
            turned = hots[z].T
            smat[z, :, 0:128] = turned[0:64].astype(BF16)
            smat[z, :, 128:256] = turned[64:128].astype(BF16)

    @pl.when(jnp.logical_not(is_ocean))
    def _():
        number = sec * n_tile + tile
        cols = pl.ds(pl.multiple_of((number // 2) * 128, 128), 128)

        def pairs(ref):
            r0 = jnp.broadcast_to(ref[0:1, cols].astype(F32), (8, 128))
            r1 = jnp.broadcast_to(ref[1:2, cols].astype(F32), (8, 128))
            even = jnp.where(left, r0, pltpu.roll(r1, 64, 1))
            odd = jnp.where(left, pltpu.roll(r0, 64, 1), r1)
            return jnp.where(parity == 0, even, odd)

        own, entry = pairs(ot), pairs(ti)
        across = jnp.broadcast_to(own[0:1], (128, 128))
        earlier = (across.T == across) & (iota((128, 128), 0) < iota((128, 128), 1))
        rank = jnp.sum(earlier.astype(F32), axis=0, keepdims=True)
        target = own * float(cap) + jnp.broadcast_to(rank, (8, 128))

        def doubled(v):
            turned = pltpu.roll(v, 64, 1)
            return jnp.where(left, v, turned), jnp.where(left, turned, v)

        t0, t1 = doubled(target)
        e0, e1 = doubled(entry)
        slots = iota((n_tile * cap, 128), 0).astype(F32)
        for b in range(ntab // 2):
            here = (lane // 64 + 2 * b).astype(F32)
            v0 = jnp.where(e0 == here, t0, -1.0)
            v1 = jnp.where(e1 == here, t1, -1.0)
            hot = ((slots == v0[0:1]) | (slots == v1[0:1])).astype(F32)
            mmat[:, 128 * b : 128 * (b + 1)] = hot.astype(BF16)
            mtmat[128 * b : 128 * (b + 1), :] = hot.T.astype(BF16)
        for t in range(ntab):
            hi, lo = split(tab[t])
            thi[t] = hi
            tlo[t] = lo

    @pl.when(is_relay)
    def _():
        pl.semaphore_wait(p_sem, 1)
        greet(k_sem, 0, tile)
        greet(k_sem, near_sec, flipped(tile))

    @pl.when(is_relay)
    def _():
        pl.semaphore_wait(g_sem, half - 1)
        greet(h_sem, sec, flipped(tile))

    @pl.when(has_upper)
    def _():
        halos[0].wait_send()
        halos[1].wait_recv()

    @pl.when(has_lower)
    def _():
        halos[1].wait_send()
        halos[0].wait_recv()

    above, below = hrecv[0], hrecv[1]
    for l in range(levels):
        ext[l, top - 2 : top, :] = above[2 * l : 2 * l + 2]
        ext[l, low : low + 2, :] = below[2 * l : 2 * l + 2]
    for c in range(2):
        cext[c, top - 1 : top, :] = above[8 + c : 9 + c]
        cext[c, low : low + 1, :] = below[8 + c : 9 + c]

    def substep(u, kappa, speed):
        n = u.shape[0]
        up = pltpu.roll(u, 1, 0)
        down = pltpu.roll(u, n - 1, 0)
        sides = pltpu.roll(u, 1, 1) + pltpu.roll(u, width - 1, 1)
        return u + kappa * (up + down + sides - 4.0 * u) - 0.5 * speed * (down - up)

    def stencil(l):
        kappa, speed = cext[0], cext[1]
        u = substep(ext[l], kappa, speed)
        return substep(u, kappa, speed)[top:low]

    fo[0, 0] = stencil(0)

    def pack(part, row):
        hi, lo = split(row)
        stacked = jnp.concatenate([hi, lo], axis=0)
        for t in range(ntab):
            r = matmul(stacked, thi[t])
            r = r[:rows] + r[rows:] + matmul(hi, tlo[t])
            here = slice(t * rows, (t + 1) * rows)
            pthi[here, :], ptlo[here, :] = split(r)
        out = matmul(mmat[...], pthi[...]) + matmul(mmat[...], ptlo[...])
        send[part] = out.reshape(send.shape[1:])

    def ship(part, to):
        def one(k, c):
            t = lax.rem(tile + k, n_tile)
            pltpu.make_async_remote_copy(
                src_ref=send.at[part, t if to == ocean_sec else flipped(t)],
                dst_ref=recv.at[part, tile // 8, parity, sec * in_plane + lax.rem(tile // 2, in_plane)],
                send_sem=fs_sem.at[part],
                recv_sem=fr_sem.at[part, tile // 8],
                device_id=(to, t),
                device_id_type=pl.DeviceIdType.MESH,
            ).start()
            return c

        if to == ocean_sec:
            lax.fori_loop(0, n_tile, one, 0)
            return

        @pl.when(is_relay)
        def _():
            pltpu.make_async_copy(
                send.at[part, flipped(tile)],
                recv.at[part, tile // 8, parity, sec * in_plane + lax.rem(tile // 2, in_plane)],
                fr_sem.at[part, tile // 8],
            ).start()
            lax.fori_loop(1, n_tile, one, 0)

        @pl.when(jnp.logical_not(is_relay))
        def _():
            lax.fori_loop(0, n_tile, one, 0)

    def shipped(part, kept):
        sent = send.at[part, kept:n_tile]
        pltpu.make_async_copy(sent, sent, fs_sem.at[part]).wait()

    def gather(part):
        flux = jnp.zeros((rows, width), F32)
        for z in range(PLANES):
            came = recv.at[part, z, :, 0:filled]
            pltpu.make_async_copy(came, came, fr_sem.at[part, z]).wait()
            hi, lo = split(recv[part, z].reshape(4 * rows, width))
            flux = flux + matmul(smat[z], hi) + matmul(smat[z], lo)
        return flux

    def give_back(first_k, last_k):
        ocean_tile = flipped(tile)

        def one(k, c):
            i = lax.rem(k, 16)
            z = 2 * (k // 16) + lax.rem(i // 4 + tile // 8, 2)
            t = 8 * z + 2 * lax.rem(i, 4) + i // 8

            z2 = 2 * (k // 16) + lax.rem(i // 8 + tile // 8, 2)
            t2 = 8 * z2 + 2 * lax.rem(i // 2 + tile // 2, 4) + lax.rem(i, 2)

            def to(a, t):
                return pltpu.make_async_remote_copy(
                    src_ref=ret.at[a * n_tile + lax.rem(t, 2) * half + t // 2],
                    dst_ref=arr.at[ocean_tile],
                    send_sem=bs_sem,
                    recv_sem=br_sem,
                    device_id=(a, t),
                    device_id_type=pl.DeviceIdType.MESH,
                )

            @pl.when(t != tile)
            def _():
                to(relay_sec, t).start()

            to(0, t).start()
            to(near_sec, t2).start()
            return c

        lax.fori_loop(first_k, last_k, one, 0)

    def keep_own():
        ocean_tile = flipped(tile)
        pltpu.make_async_copy(
            ret.at[relay_sec * n_tile + parity * half + tile // 2], arr.at[ocean_tile], br_sem
        ).start()

    @pl.when(jnp.logical_not(is_ocean))
    def _():
        pack(0, fo[0, 0])

        @pl.when(jnp.logical_not(is_relay))
        def _():
            pl.semaphore_wait(k_sem, 1)

        ship(0, relay_sec)

        @pl.when(is_relay)
        def _():
            pl.semaphore_wait(h_sem, 1)
            greet(o_sem, 0, tile)
            greet(o_sem, near_sec, flipped(tile))

        for l in range(1, levels):
            fo[0, l] = stencil(l)
        pack(1, fo[0, 0] - fo[0, 1])


        @pl.when(jnp.logical_not(is_relay))
        def _():
            shipped(0, 0)

        @pl.when(is_relay)
        def _():
            shipped(0, 1)

        @pl.when(jnp.logical_not(is_relay))
        def _():
            pl.semaphore_wait(o_sem, 1)

        ship(1, ocean_sec)

        @pl.when(is_relay)
        def _():
            place_all(flipped(tile))

        for t in range(ntab):
            hi, lo = split(tab[t].T)
            tthi[t] = hi
            ttlo[t] = lo

        @pl.when(is_relay)
        def _():
            mask_copy().wait_recv()
            base_copy().wait_recv()
            water = far_mask[...].astype(F32)
            flux = gather(0)
            flux0[...] = flux
            flux_copy().start()
            hi, lo = split(water * (base[...] + forcing_rate * water * flux))
            both = jnp.concatenate([hi, lo], axis=0)
            count = half * cap // 2
            for low_high in range(2):
                for a in range(n_atm):
                    for h in range(2):
                        n = 2 * h + low_high
                        ret[a * n_tile + n * 8 : a * n_tile + n * 8 + 8] = matmul(
                            rmat[a, n * count : (n + 1) * count], both
                        ).reshape(8, cap, width)
                give_back(low_high * half, (low_high + 1) * half)
            keep_own()

        pltpu.make_async_copy(arr, arr, br_sem).wait()
        uhi, ulo = split(arr[...].reshape(n_tile * cap, width))
        v = matmul(mtmat[...], uhi) + matmul(mtmat[...], ulo)
        total = jnp.zeros((rows, width), F32)
        for t in range(ntab):
            vhi, vlo = split(v[t * rows : (t + 1) * rows])
            r = matmul(jnp.concatenate([vhi, vlo], axis=0), tthi[t])
            total = total + r[:rows] + r[rows:] + matmul(vhi, ttlo[t])
        su[0] = total

        shipped(1, 0)

        @pl.when(is_relay)
        def _():
            others = ret.at[1 : n_atm * n_tile]
            pltpu.make_async_copy(others, others, bs_sem).wait()
            flux_copy().wait_send()

    @pl.when(is_ocean)
    def _():
        base[...] = fo[0, 0]
        base_copy().start()
        place_all(tile)
        for l in range(1, levels):
            fo[0, l] = stencil(l)
        water = mask[...].astype(F32)
        flux_copy().wait_recv()
        first = fo[0, 0] + forcing_rate * water * flux0[...]
        fo[0, 0] = first
        su[0] = water * first
        fo[0, 1] = fo[0, 1] + forcing_rate * water * gather(1)
        mask_copy().wait_send()
        base_copy().wait_send()


def store(fields, surface, fields_out, surface_out, sems):
    copies = [
        pltpu.make_async_copy(fields, fields_out, sems.at[0]),
        pltpu.make_async_copy(surface, surface_out, sems.at[1]),
    ]
    for copy in copies:
        copy.start()
    for copy in copies:
        copy.wait()


def local(fields, coefficients, owner_tile, dest_block, table_index, tables, land_mask):
    n_sec = lax.axis_size("sec")
    n_tile = lax.axis_size("tile")
    _, levels, rows, width = fields.shape
    blocks, fan_out = owner_tile.shape
    ntab = tables.shape[0]
    cap = 2 * fan_out * rows // n_tile
    n_atm = n_sec - 1
    half = n_tile // 2
    padded = rows + 2 * PAD
    slots = n_tile * cap
    scratch = [
        pltpu.VMEM((levels, padded, width), F32),
        pltpu.VMEM((2, padded, width), F32),
        pltpu.VMEM((fan_out, blocks), jnp.int32),
        pltpu.VMEM((fan_out, blocks), jnp.int32),
        pltpu.VMEM((fan_out, blocks), jnp.int32),
        pltpu.VMEM((ntab, width, width), F32),
        pltpu.VMEM((rows, width), jnp.int32),
        pltpu.VMEM((2, 16, width), F32),
        pltpu.VMEM((2, 16, width), F32),
        pltpu.VMEM((ntab, width, width), BF16),
        pltpu.VMEM((ntab, width, width), BF16),
        pltpu.VMEM((ntab, width, width), BF16),
        pltpu.VMEM((ntab, width, width), BF16),
        pltpu.VMEM((slots, ntab * rows), BF16),
        pltpu.VMEM((ntab * rows, slots), BF16),
        pltpu.VMEM((ntab * rows, width), BF16),
        pltpu.VMEM((ntab * rows, width), BF16),
        pltpu.VMEM((2, n_tile, cap, width), F32),
        pltpu.VMEM((2, PLANES, 2, 16, cap, width), F32),
        pltpu.VMEM((half, 2 * rows), F32),
        pltpu.VMEM((half, 2 * rows), F32),
        pltpu.VMEM((half, 2 * rows), F32),
        pltpu.VMEM((half, 2 * rows), F32),
        pltpu.VMEM((PLANES, 2 * rows, 2 * rows), F32),
        pltpu.VMEM((PLANES, rows, 4 * rows), BF16),
        pltpu.VMEM((n_atm, slots, 2 * rows), BF16),
        pltpu.VMEM((n_atm * n_tile, cap, width), F32),
        pltpu.VMEM((n_tile, cap, width), F32),
        pltpu.VMEM((rows, width), F32),
        pltpu.VMEM((rows, width), F32),
        pltpu.VMEM((rows, width), jnp.int32),
        pltpu.SemaphoreType.DMA((7,)),
        pltpu.SemaphoreType.DMA((2,)),
        pltpu.SemaphoreType.DMA((2,)),
        pltpu.SemaphoreType.DMA((2,)),
        pltpu.SemaphoreType.DMA((2, PLANES)),
        pltpu.SemaphoreType.DMA,
        pltpu.SemaphoreType.DMA,
        pltpu.SemaphoreType.REGULAR,
        pltpu.SemaphoreType.REGULAR,
        pltpu.SemaphoreType.REGULAR,
        pltpu.SemaphoreType.REGULAR,
        pltpu.SemaphoreType.REGULAR,
        pltpu.SemaphoreType.DMA((3,)),
        pltpu.SemaphoreType.DMA((3,)),
    ]
    operands = (fields, coefficients, owner_tile.T, dest_block.T, table_index.T, tables, land_mask)
    shapes = (
        jax.ShapeDtypeStruct(fields.shape, F32),
        jax.ShapeDtypeStruct((1, rows, width), F32),
    )
    results = pl.pallas_call(
        functools.partial(kernel, n_sec, n_tile, cap),
        out_shape=shapes,
        in_specs=[pl.BlockSpec(memory_space=pltpu.HBM)] * 7,
        out_specs=(
            pl.BlockSpec(memory_space=pltpu.VMEM),
            pl.BlockSpec(memory_space=pltpu.VMEM),
        ),
        scratch_shapes=scratch,
        compiler_params=pltpu.CompilerParams(
            collective_id=0, has_side_effects=True, vmem_limit_bytes=32 * 1024 * 1024
        ),
    )(*(pltpu.with_memory_space_constraint(x, pltpu.HBM) for x in operands))
    return pl.pallas_call(
        store,
        out_shape=shapes,
        in_specs=[pl.BlockSpec(memory_space=pltpu.VMEM)] * 2,
        out_specs=(pl.BlockSpec(memory_space=pl.ANY),) * 2,
        scratch_shapes=[pltpu.SemaphoreType.DMA((2,))],
    )(*(pltpu.with_memory_space_constraint(x, pltpu.VMEM) for x in results))


def solution(mesh):
    placed = (
        P("sec", None, "tile", None),
        P("sec", None, "tile", None),
        P(),
        P(),
        P(),
        P(),
        P("tile", None),
    )
    return jax.shard_map(
        local,
        mesh=mesh,
        in_specs=placed,
        out_specs=(P("sec", None, "tile", None), P("sec", "tile", None)),
        check_vma=False,
    )
```
